128 devices in a mesh: brick: 16 (over y, x), sub: 8 (over z, core).
Axes of the slice: x: 4, y: 4, z: 4, core: 2. Of those that a mesh axis runs over, the one named last changes fastest.
Arguments:
- atom_features: bfloat16 [16, 8, 1024, 256], P('brick', 'sub'), may hold values from -6 to 6
- positions: float32 [3, 16, 8, 1024], P(None, 'brick', 'sub')
- charges: float32 [16, 8, 1024], P('brick', 'sub'), may hold values from -0.8 to 0.8
- slot_index: int32 [6144, 64], P(('brick', 'sub')), may hold values from 0 to 9215, as said below
- atom_count: int32 [6144], P(('brick', 'sub')), may hold values from 12 to 60
- cap_weight: float32 [6144, 64], P(('brick', 'sub')), may hold values from 0.25 to 1
- tile_pairs: int32 [2, 16, 8, 128], P(None, 'brick', 'sub'), may hold values from 0 to 71, as said below
- tile_count: int32 [16, 8], P('brick', 'sub'), may hold values from 16 to 128
- w_qkv: bfloat16 [2, 256, 768], replicated, may hold values from -0.375 to 0.375
- w_out: bfloat16 [2, 256, 256], replicated, may hold values from -0.375 to 0.375
- gains: float32 [3, 256], replicated, may hold values from 0.5 to 1.5
- rates: float32 [2, 8], replicated, may hold values from 0.05 to 1
- w_read: bfloat16 [256, 128], replicated, may hold values from -0.375 to 0.375
- w_energy: float32 [128], replicated, may hold values from -0.5 to 0.5
Outputs:
- forces: float32 [3, 16, 8, 1024], P(None, 'brick', 'sub')
- total_energy: float32 [], replicated
The draws below stay inside these ranges and needn't reach their ends.
Inputs may be any that keep to these rules, and one draw needn't show every extreme that they name: `slot_index`: A fragment's slots name distinct rows, all from the blocks of two devices that are adjacent to each other, each within one step along brick and along sub of the fragment's own device and inside the mesh. `tile_pairs`: row 0 names an own tile below 8, row 1 a neighbourhood tile.
All inputs are finite; a program needn't handle non-finite values.
Results may differ from the reference program's by a relative error of at most 0.009.
Values may be sent and summed in bfloat16 or wider, within the bound.
A program may use at most 64 MiB of HBM per device.

```python
import math
import jax
import jax.numpy as jnp
from jax import lax

F = 256
HEADS = 8
READ = 128
LAYERS = 2
SLOTS = 64
BLOCK_FRAGS = 8
TILE = 128
TILE_BLOCK = 16
FRAG_DEV = 48
ATOM_DEV = 1024
TILE_CAP = 128
RANKS = 128
FRAGS = 6144
TPD = 8
N_BRICK = 16
N_SUB = 8


def draw_positions(key, part):
    key = jax.random.fold_in(key, 5)
    uniform_draw = jax.random.uniform(key, (3, N_BRICK, N_SUB, ATOM_DEV), jnp.float32)
    brick_ids = jnp.arange(N_BRICK, dtype=jnp.int32)[None, :, None, None]
    sub_ids = jnp.arange(N_SUB, dtype=jnp.int32)[None, None, :, None]
    component = jnp.arange(3, dtype=jnp.int32)[:, None, None, None]
    base = jnp.where(component == 0, brick_ids, jnp.where(component == 1, sub_ids, 0)).astype(jnp.float32)
    return (base + uniform_draw) * 22.0


def draw_slot_index(key, part):
    key = jax.random.fold_in(key, 11)
    key_u, key_v, key_axis, key_sign, key_perm = jax.random.split(key, 5)
    frag_ids = jnp.arange(FRAGS, dtype=jnp.int32)
    device_ids = frag_ids // FRAG_DEV
    brick_at = device_ids // N_SUB
    sub_at = device_ids % N_SUB
    u_low = jnp.where(brick_at == 0, 0, -1)
    u_high = jnp.where(brick_at == N_BRICK - 1, 0, 1)
    v_low = jnp.where(sub_at == 0, 0, -1)
    v_high = jnp.where(sub_at == N_SUB - 1, 0, 1)
    u_step = u_low + jax.random.randint(key_u, (FRAGS,), 0, u_high - u_low + 1)
    v_step = v_low + jax.random.randint(key_v, (FRAGS,), 0, v_high - v_low + 1)
    u_step = u_step.at[0].set(1).at[FRAGS - 1].set(-1)
    v_step = v_step.at[0].set(1).at[FRAGS - 1].set(-1)
    axis_pick = jax.random.randint(key_axis, (FRAGS,), 0, 2)
    sign_pick = 2 * jax.random.randint(key_sign, (FRAGS,), 0, 2) - 1
    move_u = jnp.where(axis_pick == 0, sign_pick, 0)
    move_v = jnp.where(axis_pick == 1, sign_pick, 0)
    other_u = u_step + move_u
    other_v = v_step + move_v
    outside = (other_u < u_low) | (other_u > u_high) | (other_v < v_low) | (other_v > v_high)
    other_u = jnp.where(outside, u_step - move_u, other_u)
    other_v = jnp.where(outside, v_step - move_v, other_v)
    home_block = (u_step + 1) * 3 + v_step + 1
    other_block = (other_u + 1) * 3 + other_v + 1
    frag_keys = jax.random.split(key_perm, FRAGS)
    orders = jax.vmap(lambda one_key: jax.random.permutation(one_key, 2 * ATOM_DEV))(frag_keys)[:, :SLOTS]
    turn = jnp.zeros((FRAGS,), jnp.int32)
    turn = turn.at[0].set(ATOM_DEV - 1 - orders[0, 0])
    turn = turn.at[FRAGS - 1].set(-orders[FRAGS - 1, 0])
    chosen = (orders + turn[:, None]) % (2 * ATOM_DEV)
    block_of = jnp.where(chosen < ATOM_DEV, home_block[:, None], other_block[:, None])
    return (block_of * ATOM_DEV + chosen % ATOM_DEV).astype(jnp.int32)


def draw_atom_count(key, part):
    key = jax.random.fold_in(key, 13)
    key_count, key_high, key_low = jax.random.split(key, 3)
    counts_drawn = jax.random.randint(key_count, (FRAGS,), 12, 61)
    high_place = jax.random.randint(key_high, (), 0, FRAGS)
    low_place = (high_place + 1 + jax.random.randint(key_low, (), 0, FRAGS - 1)) % FRAGS
    counts_drawn = counts_drawn.at[high_place].set(60)
    counts_drawn = counts_drawn.at[low_place].set(12)
    return counts_drawn.astype(jnp.int32)


def draw_tile_pairs(key, part):
    key = jax.random.fold_in(key, 7)
    key_own, key_near = jax.random.split(key, 2)
    own_drawn = jax.random.randint(key_own, (N_BRICK, N_SUB, TILE_CAP), 0, TPD)
    near_drawn = jax.random.randint(key_near, (N_BRICK, N_SUB, TILE_CAP), 0, 9 * TPD)
    near_drawn = near_drawn.at[0, 0, 0].set(9 * TPD - 1)
    own_drawn = own_drawn.at[0, 0, 0].set(0)
    return jnp.stack([own_drawn, near_drawn], axis=0).astype(jnp.int32)


def draw_tile_count(key, part):
    key = jax.random.fold_in(key, 9)
    key_base, key_heavy, key_place, key_light = jax.random.split(key, 4)
    base = jax.random.randint(key_base, (N_BRICK * N_SUB,), TILE_CAP // 8, TILE_CAP // 2 + 1)
    heavy = jax.random.randint(key_heavy, (N_BRICK * N_SUB,), 0, 8) == 0
    counts_drawn = jnp.where(heavy, TILE_CAP, base)
    full_place = jax.random.randint(key_place, (), 0, N_BRICK * N_SUB)
    light_place = (full_place + 1 + jax.random.randint(key_light, (), 0, N_BRICK * N_SUB - 1)) % (N_BRICK * N_SUB)
    counts_drawn = counts_drawn.at[full_place].set(TILE_CAP)
    counts_drawn = counts_drawn.at[light_place].set(TILE_CAP // 8)
    return counts_drawn.reshape(N_BRICK, N_SUB).astype(jnp.int32)


def block_scale(rng, shape, cuts, least, largest):
    def one(axis_at, blocks):
        draws = jax.random.uniform(jax.random.fold_in(jax.random.fold_in(rng, 6), axis_at), (blocks,), jnp.float32, least / len(cuts), largest / len(cuts))
        return jnp.repeat(jnp.exp(draws), shape[axis_at] // blocks).reshape((-1,) + (1,) * (len(shape) - axis_at - 1))

    loudness = one(*cuts[0])
    for cut in cuts[1:]:
        loudness = loudness * one(*cut)
    return loudness


def noise(own_key, shape, scale, most, shards=(), held_as=jnp.bfloat16):
    values = scale * jax.random.normal(own_key, shape, jnp.float32)
    if shards:
        values = values * block_scale(own_key, shape, shards, -0.22, 0.18)
    return jnp.clip(values, -most, most).astype(held_as)


def setup_inputs(seed: int = 0) -> dict:
    keys = jax.random.split(jax.random.key(seed), 15)
    return {
        "atom_features": noise(keys[0], (N_BRICK, N_SUB, ATOM_DEV, F), 1.0, 6.0, ((0, 16), (1, 8))),
        "positions": draw_positions(jax.random.fold_in(keys[14], 71), 0),
        "charges": jnp.clip(jax.random.uniform(keys[2], (N_BRICK, N_SUB, ATOM_DEV), jnp.float32, -0.8, 0.8) * block_scale(keys[2], (N_BRICK, N_SUB, ATOM_DEV), ((0, 16), (1, 8)), -0.4, 0.0), -0.8, 0.8),
        "slot_index": draw_slot_index(jax.random.fold_in(keys[14], 71), 0),
        "atom_count": draw_atom_count(jax.random.fold_in(keys[14], 71), 0),
        "cap_weight": jnp.clip(0.25 + 0.75 * jax.random.uniform(keys[5], (FRAGS, SLOTS), jnp.float32) ** block_scale(keys[5], (FRAGS, SLOTS), ((0, 128),), -0.2, 0.2), 0.25, 1.0),
        "tile_pairs": draw_tile_pairs(jax.random.fold_in(keys[14], 71), 0),
        "tile_count": draw_tile_count(jax.random.fold_in(keys[14], 71), 0),
        "w_qkv": noise(keys[8], (LAYERS, F, 3 * F), F ** -0.5, 0.375),
        "w_out": noise(keys[9], (LAYERS, F, F), F ** -0.5, 0.375),
        "gains": jnp.clip(1.0 + 0.1 * jax.random.normal(keys[10], (LAYERS + 1, F), jnp.float32), 0.5, 1.5),
        "rates": jnp.clip(jnp.exp(jax.random.uniform(keys[11], (LAYERS, HEADS), jnp.float32, math.log(0.05), math.log(1.0))), 0.05, 1.0),
        "w_read": noise(keys[12], (F, READ), F ** -0.5, 0.375),
        "w_energy": noise(keys[13], (READ,), READ ** -0.5, 0.5, (), jnp.float32),
    }


NORM_EPS = 1e-05
PAIR_SOFTEN = 0.01
SCREEN_RATE = 0.1
COULOMB_UNIT = 14.4
CHARGE_SOFTEN = 1.0

def norm_rows(hidden, gain_row):
    centre = lax.optimization_barrier(jnp.mean(hidden, axis=-1, keepdims=True))
    spread = lax.optimization_barrier(jnp.mean((hidden - centre) ** 2, axis=-1, keepdims=True))
    return (hidden - centre) * lax.rsqrt(spread + NORM_EPS) * gain_row

def block_energy(coords, features, living, weight, w_qkv, w_out, gains, rates, w_read, w_energy):
    pair_count, block_rows, feature_width = features.shape
    head_count = rates.shape[1]
    head_dim = feature_width // head_count
    offset = coords[:, :, :, None] - coords[:, :, None, :]
    distance = jnp.sqrt(lax.optimization_barrier(jnp.sum(offset * offset, axis=1)) + PAIR_SOFTEN)
    halves = jnp.arange(block_rows, dtype=jnp.int32) // (block_rows // 2)
    same_frag = (halves[:, None] == halves[None, :]).astype(jnp.float32)
    pair_mask = living[:, :, None] * living[:, None, :] * same_frag
    hidden = features.astype(jnp.float32).reshape(pair_count * block_rows, feature_width)
    for layer_index in range(LAYERS):
        normed = norm_rows(hidden, gains[layer_index]).astype(jnp.bfloat16)
        project = jnp.dot(normed, w_qkv[layer_index], preferred_element_type=jnp.float32).astype(jnp.bfloat16)
        project = project.reshape(pair_count, block_rows, 3, head_count, head_dim)
        queries = project[:, :, 0].astype(jnp.float32)
        key_rows = project[:, :, 1].astype(jnp.float32)
        values = project[:, :, 2].astype(jnp.float32)
        scores = jnp.einsum('pihd,pjhd->phij', queries, key_rows) / math.sqrt(head_dim)
        damping = 1.0 / (1.0 + rates[layer_index][None, :, None, None] * distance[:, None])
        attend = (jax.nn.silu(scores) * damping * pair_mask[:, None]).astype(jnp.bfloat16)
        message = jnp.einsum('phij,pjhd->pihd', attend.astype(jnp.float32), values)
        message = message.astype(jnp.bfloat16).reshape(pair_count * block_rows, feature_width)
        hidden = hidden + jnp.dot(message, w_out[layer_index], preferred_element_type=jnp.float32)
    normed = norm_rows(hidden, gains[LAYERS]).astype(jnp.bfloat16)
    readout = jax.nn.silu(jnp.dot(normed, w_read, preferred_element_type=jnp.float32))
    energy = jnp.dot(readout, w_energy, precision=lax.Precision.HIGHEST)
    return jnp.sum(energy * (living * weight).reshape(-1))

def fragment_model(received, places, slot_index, atom_count, cap_weight, w_qkv, w_out, gains, rates, w_read, w_energy):
    frag_count, slot_count = slot_index.shape
    feature_width = received.shape[1]
    blocks = frag_count // BLOCK_FRAGS
    pair_count = BLOCK_FRAGS // 2
    slot_rows = slot_index.reshape(-1)
    living = (jnp.arange(slot_count, dtype=jnp.int32)[None, :] < atom_count[:, None]).astype(jnp.float32)
    features = received[slot_rows].reshape(blocks, pair_count, 2 * slot_count, feature_width)
    coords = places[:, slot_rows].reshape(3, blocks, pair_count, 2 * slot_count).transpose(1, 2, 0, 3)
    alive_blocks = living.reshape(blocks, pair_count, 2 * slot_count)
    weight_blocks = cap_weight.reshape(blocks, pair_count, 2 * slot_count)

    def one_block(inputs):
        coord_block, feature_block, alive_block, weight_block = inputs

        def energy_of(coord_value):
            return block_energy(coord_value, feature_block, alive_block, weight_block, w_qkv, w_out, gains, rates, w_read, w_energy)
        energy, pullback = jax.vjp(energy_of, coord_block)
        gradient = pullback(jnp.ones_like(energy))[0]
        return (energy, -gradient)
    energies, slot_force = lax.map(one_block, (coords, features, alive_blocks, weight_blocks))
    slot_force = slot_force.transpose(2, 0, 1, 3).reshape(3, -1) * living.reshape(-1)
    row_force = jnp.zeros((3, received.shape[0]), jnp.float32).at[:, slot_rows].add(slot_force)
    return (jnp.sum(energies), row_force)

def solvent_pairs(own_atoms, neighbours, own_list, near_list, tile_live, loop_count):
    tile_size = TILE
    own_tiles = own_atoms.reshape(4, -1, tile_size)
    near_tiles = neighbours.reshape(4, -1, tile_size)
    centre = 4 * own_atoms.shape[1]
    lane_ids = jnp.arange(tile_size, dtype=jnp.int32)
    gauss_slope = 2.0 * SCREEN_RATE / math.sqrt(math.pi)

    def visit_block(index, state_now):
        tile_force, energy = state_now
        start = index * TILE_BLOCK
        own_pick = lax.dynamic_slice_in_dim(own_list, start, TILE_BLOCK)
        near_pick = lax.dynamic_slice_in_dim(near_list, start, TILE_BLOCK)
        active = (start + jnp.arange(TILE_BLOCK, dtype=jnp.int32) < tile_live).astype(jnp.float32)
        own_block = own_tiles[:, own_pick]
        near_block = near_tiles[:, near_pick]
        offset = own_block[:3, :, :, None] - near_block[:3, :, None, :]
        square = lax.optimization_barrier(jnp.sum(offset * offset, axis=0)) + CHARGE_SOFTEN
        radius = jnp.sqrt(square)
        own_ids = centre + own_pick[:, None] * tile_size + lane_ids[None, :]
        near_ids = near_pick[:, None] * tile_size + lane_ids[None, :]
        distinct = (own_ids[:, :, None] != near_ids[:, None, :]).astype(jnp.float32)
        charge = own_block[3][:, :, None] * near_block[3][:, None, :] * distinct * active[:, None, None]
        screened = jax.scipy.special.erfc(SCREEN_RATE * radius) / radius
        energy = energy + 0.5 * COULOMB_UNIT * jnp.sum(charge * screened)
        strength = COULOMB_UNIT * charge * (screened + gauss_slope * jnp.exp(-SCREEN_RATE * SCREEN_RATE * square)) / square
        pull_force = lax.optimization_barrier(jnp.sum(strength[None] * offset, axis=3))
        tile_force = tile_force.at[:, own_pick].add(pull_force)
        return (tile_force, energy)
    start_state = (jnp.zeros((3, own_tiles.shape[1], tile_size), jnp.float32), jnp.zeros((), jnp.float32))
    tile_force, energy = lax.fori_loop(0, loop_count, visit_block, start_state)
    return (energy, tile_force.reshape(3, -1))

def reference(atom_features, positions, charges, slot_index, atom_count, cap_weight, tile_pairs, tile_count, w_qkv, w_out, gains, rates, w_read, w_energy):
    atom_table = jnp.concatenate([positions, charges[None]], axis=0)
    padded = jnp.pad(atom_table, ((0, 0), (1, 1), (1, 1), (0, 0)))
    padded_features = jnp.pad(atom_features, ((1, 1), (1, 1), (0, 0), (0, 0)))
    slots_each = slot_index.reshape(RANKS, FRAG_DEV, SLOTS)
    counts_each = atom_count.reshape(RANKS, FRAG_DEV)
    weights_each = cap_weight.reshape(RANKS, FRAG_DEV, SLOTS)
    own_lists = tile_pairs[0].reshape(RANKS, TILE_CAP)
    near_lists = tile_pairs[1].reshape(RANKS, TILE_CAP)
    live_tiles = tile_count.reshape(RANKS)
    sources = jnp.arange(RANKS, dtype=jnp.int32)

    def visit_rank(state_now, inputs):
        force_pad, energy = state_now
        rank_index, slot_rows, frag_atoms, slot_weights, own_list, near_list, tile_live = inputs
        brick_index = (rank_index // N_SUB).astype(jnp.int32)
        sub_index = (rank_index % N_SUB).astype(jnp.int32)
        zero_index = jnp.zeros((), jnp.int32)
        near_features = lax.dynamic_slice(padded_features, (brick_index, sub_index, zero_index, zero_index), (3, 3, ATOM_DEV, F)).reshape(9 * ATOM_DEV, F)
        neighbours = lax.dynamic_slice(padded, (zero_index, brick_index, sub_index, zero_index), (4, 3, 3, ATOM_DEV)).reshape(4, -1)
        ml_energy, row_force = fragment_model(near_features, neighbours[:3], slot_rows, frag_atoms, slot_weights, w_qkv, w_out, gains, rates, w_read, w_energy)
        current = lax.dynamic_slice(force_pad, (zero_index, brick_index, sub_index, zero_index), (3, 3, 3, ATOM_DEV))
        force_pad = lax.dynamic_update_slice(force_pad, current + row_force.reshape(3, 3, 3, ATOM_DEV), (zero_index, brick_index, sub_index, zero_index))
        own_atoms = lax.dynamic_slice(atom_table, (zero_index, brick_index, sub_index, zero_index), (4, 1, 1, ATOM_DEV)).reshape(4, -1)
        mm_energy, mm_force = solvent_pairs(own_atoms, neighbours, own_list, near_list, tile_live, TILE_CAP // TILE_BLOCK)
        centre_at = (zero_index, brick_index + 1, sub_index + 1, zero_index)
        current = lax.dynamic_slice(force_pad, centre_at, (3, 1, 1, ATOM_DEV))
        force_pad = lax.dynamic_update_slice(force_pad, current + mm_force.reshape(3, 1, 1, ATOM_DEV), centre_at)
        return ((force_pad, energy + ml_energy + mm_energy), None)
    start_state = (jnp.zeros((3, N_BRICK + 2, N_SUB + 2, ATOM_DEV), jnp.float32), jnp.zeros((), jnp.float32))
    (force_pad, energy), _ = lax.scan(visit_rank, start_state, (sources, slots_each, counts_each, weights_each, own_lists, near_lists, live_tiles))
    return (force_pad[:, 1:-1, 1:-1], energy)
```

```python
import math

import jax
import jax.numpy as jnp
from jax import lax
from jax.experimental import pallas as pl
from jax.experimental.pallas import tpu as pltpu
from jax.sharding import PartitionSpec as P

F = 256
HEADS = 8
LAYERS = 2
SLOTS = 64
TILE = 128
GROUP = 4
ROWS = GROUP * SLOTS
QUAD = 128

NORM_EPS = 1e-05
PAIR_SOFTEN = 0.01
SCREEN_RATE = 0.1
COULOMB_UNIT = 14.4
CHARGE_SOFTEN = 1.0
FAR = 1e30
GAUSS = 2.0 * SCREEN_RATE / math.sqrt(math.pi)
ERFC_P = 0.6
ERFC_C = (
    0.33858295223558404,
    0.33681896467541816,
    0.2948193558779553,
    0.06093701313639673,
    0.3109940554359323,
    -0.6781244471753995,
    0.4339317702022656,
    -0.0979638654555287,
)
MIB = 1024 * 1024


def dot(a, b):
    return lax.dot_general(a, b, (((1,), (0,)), ((), ())), preferred_element_type=jnp.float32)


def dot_nt(a, b):
    return lax.dot_general(a, b, (((1,), (1,)), ((), ())), preferred_element_type=jnp.float32)


def dot_tn(a, b):
    return lax.dot_general(a, b, (((0,), (0,)), ((), ())), preferred_element_type=jnp.float32)


def recip(x):
    return pl.reciprocal(x, approx=True)


def pair_body(pairs_ref, count_ref, own_ref, near_ref, force_ref, energy_ref):
    force_ref[...] = jnp.zeros_like(force_ref)
    energy_ref[...] = jnp.zeros_like(energy_ref)
    chunk = 32
    lane = lax.broadcasted_iota(jnp.int32, (chunk, TILE), 1)
    row = lax.broadcasted_iota(jnp.int32, (chunk, TILE), 0)
    rel = lane - row

    def one_pair(p, carry):
        own = pairs_ref[0, p]
        near = pairs_ref[1, p]
        o = own_ref[own]
        n = jnp.transpose(near_ref[near])
        xi, yi, zi, qi = (o[c : c + 1, :] for c in range(4))
        same = jnp.where(near - 4 * own_ref.shape[0] == own, 0, 4 * TILE)
        fx = jnp.zeros((8, TILE), jnp.float32)
        fy = jnp.zeros((8, TILE), jnp.float32)
        fz = jnp.zeros((8, TILE), jnp.float32)
        en = jnp.zeros((8, TILE), jnp.float32)
        for start in range(0, TILE, chunk):
            part = n[start : start + chunk]
            dx = xi - part[:, 0:1]
            dy = yi - part[:, 1:2]
            dz = zi - part[:, 2:3]
            qq = jnp.where(rel == same + start, 0.0, qi * part[:, 3:4])
            s = dx * dx + dy * dy + dz * dz + CHARGE_SOFTEN
            s = jnp.minimum(s, 1e6)
            rinv = lax.rsqrt(s)
            t = recip(1.0 + (ERFC_P * SCREEN_RATE) * (s * rinv))
            g = ERFC_C[-1]
            for coef in ERFC_C[-2::-1]:
                g = g * t + coef
            gauss = qq * jnp.exp((-SCREEN_RATE * SCREEN_RATE) * s)
            screened = gauss * (g * t) * rinv
            en += jnp.sum(screened.reshape(chunk // 8, 8, TILE), axis=0)
            w = (screened + GAUSS * gauss) * (rinv * rinv)
            fx += jnp.sum((w * dx).reshape(chunk // 8, 8, TILE), axis=0)
            fy += jnp.sum((w * dy).reshape(chunk // 8, 8, TILE), axis=0)
            fz += jnp.sum((w * dz).reshape(chunk // 8, 8, TILE), axis=0)
        energy_ref[...] += en
        force_ref[own, 0] += fx
        force_ref[own, 1] += fy
        force_ref[own, 2] += fz
        return carry

    lax.fori_loop(0, count_ref[0], one_pair, 0)


def solvent_pairs(own8, near8, pairs, count):
    tiles = own8.shape[0]
    smem = pl.BlockSpec(memory_space=pltpu.SMEM)
    vmem = pl.BlockSpec(memory_space=pltpu.VMEM)
    force, energy = pl.pallas_call(
        pair_body,
        out_shape=(
            jax.ShapeDtypeStruct((tiles, 3, 8, TILE), jnp.float32),
            jax.ShapeDtypeStruct((8, TILE), jnp.float32),
        ),
        in_specs=[smem, smem, vmem, vmem],
        out_specs=(vmem, vmem),
        name="pair_tiles",
    )(pairs, count, own8, near8)
    force = COULOMB_UNIT * jnp.sum(force, axis=2)
    return 0.5 * COULOMB_UNIT * jnp.sum(energy), force.transpose(1, 0, 2).reshape(3, -1)


def norm_parts(hidden):
    centre = jnp.mean(hidden, axis=-1, keepdims=True)
    shifted = hidden - centre
    spread = jnp.mean(shifted * shifted, axis=-1, keepdims=True)
    scale = lax.rsqrt(spread + NORM_EPS)
    return shifted * scale, scale


def norm_back(grad, gain, unit, scale):
    g = grad * gain
    mean_g = jnp.mean(g, axis=-1, keepdims=True)
    mean_gu = jnp.mean(g * unit, axis=-1, keepdims=True)
    return scale * (g - mean_g - unit * mean_gu)


def sigmoid(x):
    return 0.5 * jnp.tanh(0.5 * x) + 0.5


def fragment_body(
    slot_ref,
    count_ref,
    near_ref,
    feat_ref,
    cap_ref,
    wqkv_ref,
    wout_ref,
    gains_ref,
    rates_ref,
    wread_ref,
    wen_ref,
    force_ref,
    energy_ref,
    table,
    atoms,
    slot_feat,
    slot_atom,
    slot_force,
):
    tiles = near_ref.shape[0]
    blocks = slot_ref.shape[0] // GROUP

    def widen(i, carry):
        at = pl.multiple_of(i * TILE, TILE)
        table[pl.ds(at, TILE), :] = feat_ref[pl.ds(at, TILE), :].astype(jnp.float32)
        n = jnp.transpose(near_ref[i])
        atoms[pl.ds(at, TILE), :] = jnp.concatenate(
            [n, jnp.zeros((TILE, TILE - 8), jnp.float32)], axis=1
        )
        return carry

    lax.fori_loop(0, tiles, widen, 0)
    slot_feat[...] = jnp.zeros_like(slot_feat)
    slot_atom[...] = jnp.zeros_like(slot_atom)
    slot_force[...] = jnp.zeros_like(slot_force)
    energy_ref[...] = jnp.zeros_like(energy_ref)

    lane = lax.broadcasted_iota(jnp.int32, (1, QUAD), 1)
    head_mask = [(lane // 32 == h).astype(jnp.bfloat16) for h in range(4)]
    head_pick = [lane // 32 == h for h in range(4)]
    slot_row = lax.broadcasted_iota(jnp.int32, (SLOTS, 1), 0)
    slot_lane = lane % SLOTS
    frag_lane = lax.broadcasted_iota(jnp.int32, (SLOTS, cap_ref.shape[1]), 1)

    def spread_heads(x):
        return jnp.concatenate([x * head_mask[h] for h in range(4)], axis=0)

    def fold_heads(x):
        out = jnp.where(head_pick[0], x[0:SLOTS], 0.0)
        for h in range(1, 4):
            out = jnp.where(head_pick[h], x[h * SLOTS : (h + 1) * SLOTS], out)
        return out

    def rate_of(layer, quad):
        return rates_ref[layer : layer + 1, quad * 256 : (quad + 1) * 256]

    def one_block(b, carry):
        for f in range(GROUP):
            frag = b * GROUP + f

            def pull(j8, c, frag=frag, f=f):
                for k in range(8):
                    j = j8 * 8 + k
                    r = slot_ref[frag, j]
                    slot_feat[pl.ds(f * SLOTS + j, 1), :] = table[pl.ds(r, 1), :]
                    slot_atom[pl.ds(f * SLOTS + j, 1), :] = atoms[pl.ds(r, 1), :]
                return c

            lax.fori_loop(0, (count_ref[frag] + 7) // 8, pull, 0)

        atom_rows = jnp.transpose(slot_atom[...])
        dists, offsets, weights = [], [], []
        for f in range(GROUP):
            count = count_ref[b * GROUP + f]
            col = slot_atom[f * SLOTS : (f + 1) * SLOTS, :]
            row = atom_rows[0:8, f * SLOTS : (f + 1) * SLOTS]
            row = jnp.concatenate([row, row], axis=1)
            off = [col[:, c : c + 1] - row[c : c + 1, :] for c in range(3)]
            square = off[0] * off[0] + off[1] * off[1] + off[2] * off[2]
            live = jnp.logical_and(slot_row < count, slot_lane < count)
            dists.append(jnp.where(live, jnp.sqrt(square + PAIR_SOFTEN), FAR))
            offsets.append(off)
            cap = jnp.sum(
                jnp.where(frag_lane == b * GROUP + f, cap_ref[...], 0.0), axis=1, keepdims=True
            )
            weights.append(jnp.where(slot_row < count, cap, 0.0))
        weight = jnp.concatenate(weights, axis=0)

        def attention(layer, project):
            messages, kept = [], []
            for f in range(GROUP):
                dist = jnp.concatenate([dists[f], dists[f]], axis=1)
                parts = []
                for quad in range(2):
                    rows = slice(f * SLOTS, (f + 1) * SLOTS)
                    q, k, v = (
                        project[rows, part * F + quad * QUAD : part * F + (quad + 1) * QUAD]
                        for part in range(3)
                    )
                    kb = spread_heads(k)
                    vb = spread_heads(v)
                    s = dot_nt(q, kb) * (1.0 / math.sqrt(32.0))
                    sig = sigmoid(s)
                    rate = rate_of(layer, quad)
                    damp = recip(1.0 + rate * dist)
                    silu = s * sig
                    att = silu * damp
                    att16 = att.astype(jnp.bfloat16)
                    parts.append(dot(att16, vb).astype(jnp.bfloat16))
                    by_dist = att * (rate * damp)
                    by_score = None
                    if layer == 1:
                        by_score = (damp * (1.0 / math.sqrt(32.0))) * (sig + silu * (1.0 - sig))
                    kept.append((q, kb, vb, att16, by_dist, by_score))
                messages.append(jnp.concatenate(parts, axis=1))
            return jnp.concatenate(messages, axis=0), kept

        gain = [gains_ref[i : i + 1, :] for i in range(LAYERS + 1)]
        h0 = slot_feat[...]
        unit0, _ = norm_parts(h0)
        project0 = dot((unit0 * gain[0]).astype(jnp.bfloat16), wqkv_ref[0]).astype(jnp.bfloat16)
        message0, kept0 = attention(0, project0)
        h1 = h0 + dot(message0, wout_ref[0])
        unit1, scale1 = norm_parts(h1)
        project1 = dot((unit1 * gain[1]).astype(jnp.bfloat16), wqkv_ref[1]).astype(jnp.bfloat16)
        message1, kept1 = attention(1, project1)
        h2 = h1 + dot(message1, wout_ref[1])
        unit2, scale2 = norm_parts(h2)
        read = dot((unit2 * gain[2]).astype(jnp.bfloat16), wread_ref[...])
        sig = sigmoid(read)
        silu = read * sig
        wen = wen_ref[...]
        contrib = weight * (silu * wen)
        energy_ref[...] += jnp.sum(contrib.reshape(ROWS // 8, 8, QUAD), axis=0)

        dread = ((weight * wen) * (sig + silu * (1.0 - sig))).astype(jnp.bfloat16)
        dh2 = norm_back(dot_nt(dread, wread_ref[...]), gain[2], unit2, scale2)
        dmsg1 = dot_nt(dh2.astype(jnp.bfloat16), wout_ref[1]).astype(jnp.bfloat16)
        pulls = []
        dqkv = []
        for f in range(GROUP):
            rows = slice(f * SLOTS, (f + 1) * SLOTS)
            total = None
            cols = [[], [], []]
            for quad in range(2):
                q, kb, vb, att16, by_dist, by_score = kept1[2 * f + quad]
                dm = dmsg1[rows, quad * QUAD : (quad + 1) * QUAD]
                datt = dot_nt(dm, vb)
                ds = (datt * by_score).astype(jnp.bfloat16)
                cols[0].append(dot(ds, kb))
                cols[1].append(fold_heads(dot_tn(ds, q)))
                cols[2].append(fold_heads(dot_tn(att16, dm)))
                pull = datt * by_dist
                pull = pull[:, :QUAD] + pull[:, QUAD:]
                total = pull if total is None else total + pull
            pulls.append(total)
            dqkv.append(
                jnp.concatenate([x.astype(jnp.bfloat16) for part in cols for x in part], axis=1)
            )
        dproject = jnp.concatenate(dqkv, axis=0)
        dh1 = dh2 + norm_back(dot_nt(dproject, wqkv_ref[1]), gain[1], unit1, scale1)
        dmsg0 = dot_nt(dh1.astype(jnp.bfloat16), wout_ref[0]).astype(jnp.bfloat16)
        force_rows = []
        for f in range(GROUP):
            rows = slice(f * SLOTS, (f + 1) * SLOTS)
            total = pulls[f]
            for quad in range(2):
                q, kb, vb, att16, by_dist, by_score = kept0[2 * f + quad]
                datt = dot_nt(dmsg0[rows, quad * QUAD : (quad + 1) * QUAD], vb)
                pull = datt * by_dist
                total = total + (pull[:, :QUAD] + pull[:, QUAD:])
            pull = total / dists[f]
            pull = pull[:, :SLOTS] + pull[:, SLOTS:]
            pull = pull + jnp.transpose(pull)
            for c in range(3):
                force_rows.append(
                    -jnp.sum(pull * offsets[f][c][:, :SLOTS], axis=0, keepdims=True)
                )
        packed = jnp.concatenate(
            [
                jnp.concatenate([force_rows[3 * f + c] for f in range(GROUP)], axis=1)
                for c in range(3)
            ]
            + [jnp.zeros((5, ROWS), jnp.float32)],
            axis=0,
        )
        slot_force[:, 8:16] = jnp.transpose(packed)

        for f in range(GROUP):
            frag = b * GROUP + f
            count = count_ref[frag]

            def push(j8, c, frag=frag, f=f, count=count):
                rs = [slot_ref[frag, j8 * 8 + k] for k in range(8)]
                old = [atoms[pl.ds(r, 1), :] for r in rs]
                add = [slot_force[pl.ds(f * SLOTS + j8 * 8 + k, 1), :] for k in range(8)]
                for k in range(8):
                    atoms[pl.ds(rs[k], 1), :] = old[k] + add[k]
                return c

            lax.fori_loop(0, (count + 7) // 8, push, 0)
        return carry

    lax.fori_loop(0, blocks, one_block, 0)

    pick = (
        lax.broadcasted_iota(jnp.int32, (16, TILE), 0) + 8
        == lax.broadcasted_iota(jnp.int32, (16, TILE), 1)
    ).astype(jnp.bfloat16)
    for i in range(tiles // 8):
        force_ref[i] = dot_nt(pick, atoms[i * 1024 : (i + 1) * 1024, :].astype(jnp.bfloat16))[:8]


def fragment_model(near8, near_features, slot_index, atom_count, cap_weight, weights):
    w_qkv, w_out, gains, rates, w_read, w_energy = weights
    tiles = near8.shape[0]
    smem = pl.BlockSpec(memory_space=pltpu.SMEM)
    vmem = pl.BlockSpec(memory_space=pltpu.VMEM)
    lane_rates = jnp.repeat(rates, SLOTS, axis=1)
    force, energy = pl.pallas_call(
        fragment_body,
        out_shape=(
            jax.ShapeDtypeStruct((tiles // 8, 8, 1024), jnp.float32),
            jax.ShapeDtypeStruct((8, TILE), jnp.float32),
        ),
        in_specs=[smem, smem] + [vmem] * 9,
        out_specs=(vmem, vmem),
        scratch_shapes=[
            pltpu.VMEM((tiles * TILE, F), jnp.float32),
            pltpu.VMEM((tiles * TILE, TILE), jnp.float32),
            pltpu.VMEM((ROWS, F), jnp.float32),
            pltpu.VMEM((ROWS, TILE), jnp.float32),
            pltpu.VMEM((ROWS, TILE), jnp.float32),
        ],
        compiler_params=pltpu.CompilerParams(vmem_limit_bytes=56 * MIB),
        name="fragments",
    )(
        slot_index,
        atom_count,
        near8,
        near_features,
        cap_weight.T,
        w_qkv,
        w_out,
        gains,
        lane_rates,
        w_read,
        w_energy.reshape(1, -1),
    )
    return jnp.sum(energy), force


def with_halo(x, sides, width):
    for axis, dim in sides:
        devices, length = (lax.axis_size(axis), x.shape[dim])
        up = [(i, (i + 1) % devices) for i in range(devices - 1)]
        down = [(j, i) for i, j in up]
        last = lax.slice_in_dim(x, length - width, length, axis=dim)
        initial = lax.slice_in_dim(x, 0, width, axis=dim)
        before = lax.ppermute(last, axis, up)
        after = lax.ppermute(initial, axis, down)
        x = jnp.concatenate([before, x, after], axis=dim)
    return x


def body(
    atom_features,
    positions,
    charges,
    slot_index,
    atom_count,
    cap_weight,
    tile_pairs,
    tile_count,
    w_qkv,
    w_out,
    gains,
    rates,
    w_read,
    w_energy,
):
    own_size = atom_features.shape[2]
    own_tiles = own_size // TILE
    own8 = jnp.concatenate([positions.reshape(3, -1), charges.reshape(1, -1)], axis=0)
    own8 = jnp.pad(own8, ((0, 4), (0, 0))).reshape(8, own_tiles, TILE).transpose(1, 0, 2)
    near8 = with_halo(own8[None, None], (("brick", 0), ("sub", 1)), 1).reshape(-1, 8, TILE)
    near_features = with_halo(atom_features, (("brick", 0), ("sub", 1)), 1)
    mm_energy, mm_force = solvent_pairs(
        own8, near8, tile_pairs.reshape(2, -1), tile_count.reshape(1)
    )
    ml_energy, row_force = fragment_model(
        near8,
        near_features.reshape(-1, F),
        slot_index,
        atom_count,
        cap_weight,
        (w_qkv, w_out, gains, rates, w_read, w_energy),
    )
    row_force = row_force[:, :3].astype(jnp.bfloat16).transpose(1, 0, 2).reshape(3, 3, 3, own_size)
    returned = with_halo(row_force, (("brick", 1), ("sub", 2)), 1).astype(jnp.float32)
    ml_force = jnp.sum(returned[:, ::2, ::2], axis=(1, 2))
    energy_sum = lax.psum(ml_energy + mm_energy, ("brick", "sub"))
    return ((ml_force + mm_force).reshape(3, 1, 1, own_size), energy_sum)


def solution(mesh):
    in_specs = (
        P("brick", "sub", None, None),
        P(None, "brick", "sub", None),
        P("brick", "sub", None),
        P(("brick", "sub"), None),
        P(("brick", "sub")),
        P(("brick", "sub"), None),
        P(None, "brick", "sub", None),
        P("brick", "sub"),
        P(),
        P(),
        P(),
        P(),
        P(),
        P(),
    )
    out_specs = (P(None, "brick", "sub", None), P())
    return jax.shard_map(body, mesh=mesh, in_specs=in_specs, out_specs=out_specs, check_vma=False)
```

```python
import math

import jax
import jax.numpy as jnp
from jax import lax
from jax.experimental import pallas as pl
from jax.experimental.pallas import tpu as pltpu
from jax.sharding import PartitionSpec as P

F = 256
HEADS = 8
LAYERS = 2
SLOTS = 64
TILE = 128
GROUP = 8
ROWS = GROUP * SLOTS
QUAD = 128

NORM_EPS = 1e-05
PAIR_SOFTEN = 0.01
SCREEN_RATE = 0.1
COULOMB_UNIT = 14.4
CHARGE_SOFTEN = 1.0
FAR = 1e30
GAUSS = 2.0 * SCREEN_RATE / math.sqrt(math.pi)
ERFC_P = 0.6
ERFC_C = (
    0.33858295223558404,
    0.33681896467541816,
    0.2948193558779553,
    0.06093701313639673,
    0.3109940554359323,
    -0.6781244471753995,
    0.4339317702022656,
    -0.0979638654555287,
)
MIB = 1024 * 1024


def dot(a, b):
    return lax.dot_general(a, b, (((1,), (0,)), ((), ())), preferred_element_type=jnp.float32)


def dot_nt(a, b):
    return lax.dot_general(a, b, (((1,), (1,)), ((), ())), preferred_element_type=jnp.float32)


def dot_tn(a, b):
    return lax.dot_general(a, b, (((0,), (0,)), ((), ())), preferred_element_type=jnp.float32)


def recip(x):
    return pl.reciprocal(x, approx=True)


def pair_body(pairs_ref, count_ref, own_ref, near_ref, force_ref, energy_ref, own_cols, total):
    own_tiles = own_ref.shape[0]
    total[...] = jnp.zeros_like(total)
    energy_ref[...] = jnp.zeros_like(energy_ref)
    for t in range(own_tiles):
        cols = jnp.transpose(own_ref[t])
        for c in range(4):
            own_cols[t, c] = jnp.broadcast_to(cols[:, c : c + 1], (TILE, TILE))
    chunk = 32
    lane = lax.broadcasted_iota(jnp.int32, (chunk, TILE), 1)
    row = lax.broadcasted_iota(jnp.int32, (chunk, TILE), 0)
    rel = lane - row

    def one_pair(p, carry):
        own = pairs_ref[0, p]
        near = pairs_ref[1, p]
        n = near_ref[near]
        xj, yj, zj, qj = (n[c : c + 1, :] for c in range(4))
        same = jnp.where(near - 4 * own_tiles == own, 0, 4 * TILE)
        en = jnp.zeros((8, TILE), jnp.float32)
        for start in range(0, TILE, chunk):
            at = pl.ds(start, chunk)
            dx = own_cols[own, 0, at, :] - xj
            dy = own_cols[own, 1, at, :] - yj
            dz = own_cols[own, 2, at, :] - zj
            qq = jnp.where(rel == same + start, 0.0, own_cols[own, 3, at, :] * qj)
            s = dx * dx + dy * dy + dz * dz + CHARGE_SOFTEN
            s = jnp.minimum(s, 1e6)
            rinv = lax.rsqrt(s)
            t = recip(1.0 + (ERFC_P * SCREEN_RATE) * (s * rinv))
            g = ERFC_C[-1]
            for coef in ERFC_C[-2::-1]:
                g = g * t + coef
            gauss = qq * jnp.exp2((-SCREEN_RATE * SCREEN_RATE * math.log2(math.e)) * s)
            screened = (g * t) * rinv
            en += jnp.sum((gauss * screened).reshape(chunk // 8, 8, TILE), axis=0)
            w = (gauss * (screened + GAUSS)) * (rinv * rinv)
            total[own, 0, at, :] += w * dx
            total[own, 1, at, :] += w * dy
            total[own, 2, at, :] += w * dz
        energy_ref[...] += en
        return carry

    lax.fori_loop(0, count_ref[0], one_pair, 0)
    for t in range(own_tiles):
        for c in range(3):
            force_ref[c, t : t + 1, :] = jnp.sum(
                jnp.transpose(total[t, c]), axis=0, keepdims=True
            )


def solvent_pairs(own8, near8, pairs, count):
    tiles = own8.shape[0]
    smem = pl.BlockSpec(memory_space=pltpu.SMEM)
    vmem = pl.BlockSpec(memory_space=pltpu.VMEM)
    return pl.pallas_call(
        pair_body,
        out_shape=(
            jax.ShapeDtypeStruct((3, tiles, TILE), jnp.float32),
            jax.ShapeDtypeStruct((8, TILE), jnp.float32),
        ),
        in_specs=[smem, smem, vmem, vmem],
        out_specs=(vmem, vmem),
        scratch_shapes=[
            pltpu.VMEM((tiles, 4, TILE, TILE), jnp.float32),
            pltpu.VMEM((tiles, 3, TILE, TILE), jnp.float32),
        ],
        compiler_params=pltpu.CompilerParams(vmem_limit_bytes=16 * MIB),
        name="pair_tiles",
    )(pairs, count, own8, near8)


def norm_parts(hidden):
    centre = jnp.mean(hidden, axis=-1, keepdims=True)
    shifted = hidden - centre
    spread = jnp.mean(shifted * shifted, axis=-1, keepdims=True)
    scale = lax.rsqrt(spread + NORM_EPS)
    return shifted * scale, scale


def norm_back(grad, gain, unit, scale):
    g = grad * gain
    mean_g = jnp.mean(g, axis=-1, keepdims=True)
    mean_gu = jnp.mean(g * unit, axis=-1, keepdims=True)
    return scale * (g - mean_g - unit * mean_gu)


def bf16(x):
    return x.astype(jnp.bfloat16)


def fragment_body(
    order_ref,
    slot_ref,
    near_ref,
    feat_ref,
    cap_ref,
    wqkv_ref,
    wout_ref,
    gains_ref,
    span_ref,
    span_cols_ref,
    wread_ref,
    wen_ref,
    force_ref,
    energy_ref,
    table,
    slots,
    slot_force,
    bins,
):
    tiles = near_ref.shape[0]
    frags = order_ref.shape[0]

    def widen(i, carry):
        for k in range(8):
            at = pl.multiple_of(i * 8 * TILE + k * TILE, TILE)
            both = feat_ref[pl.ds(at, TILE), :].astype(jnp.float32)
            table[0, pl.ds(at, TILE), :] = both[:, :QUAD]
            table[1, pl.ds(at, TILE), :] = both[:, QUAD:]
            n = jnp.transpose(near_ref[i * 8 + k])
            table[2, pl.ds(at, TILE), :] = jnp.concatenate(
                [n, jnp.zeros((TILE, TILE - 8), jnp.float32)], axis=1
            )
        return carry

    lax.fori_loop(0, tiles // 8, widen, 0)
    slot_force[...] = jnp.zeros_like(slot_force)
    energy_ref[...] = jnp.zeros_like(energy_ref)

    def fill(i, state):
        low, high, made = state
        big = order_ref[jnp.minimum(low, frags - 1)]
        small = order_ref[jnp.maximum(high, 0)]
        big_live, small_live = big >> 6, small >> 6
        start = (big_live + 7) & -8
        fits = start + ((small_live + 7) & -8) <= SLOTS
        both = jnp.logical_and(low < high, fits)
        bins[0, made] = big & 63
        bins[1, made] = small & 63
        bins[2, made] = big_live
        bins[3, made] = jnp.where(both, start, SLOTS)
        bins[4, made] = jnp.where(both, small_live, 0)
        one = jnp.where(low <= high, 1, 0)
        return low + one, high - jnp.where(both, 1, 0), made + one

    _, _, made = lax.fori_loop(0, frags, fill, (0, frags - 1, 0))
    for k in range(GROUP - 1):
        bins[0, made + k] = 0
        bins[1, made + k] = 0
        bins[2, made + k] = 0
        bins[3, made + k] = SLOTS
        bins[4, made + k] = 0

    lane = lax.broadcasted_iota(jnp.int32, (1, QUAD), 1)
    head_mask = [(lane // 32 == h).astype(jnp.bfloat16) for h in range(4)]
    head_pick = [lane // 32 == h for h in range(4)]
    slot_row = lax.broadcasted_iota(jnp.int32, (SLOTS, QUAD), 0)
    slot_lane = lax.broadcasted_iota(jnp.int32, (SLOTS, QUAD), 1) % SLOTS

    def spread_heads(x):
        return jnp.concatenate([x * head_mask[h] for h in range(4)], axis=0)

    def fold_heads(x):
        out = jnp.where(head_pick[0], x[0:SLOTS], 0.0)
        for h in range(1, 4):
            out = jnp.where(head_pick[h], x[h * SLOTS : (h + 1) * SLOTS], out)
        return out

    half = 0.5 / math.sqrt(32.0)
    units = [(f, quad) for f in range(GROUP) for quad in range(2)]

    def rows_of(f):
        return slice(f * SLOTS, (f + 1) * SLOTS)

    def one_block(b, carry):
        info = []
        for f in range(GROUP):
            big, small, first, start, second = (bins[c, b * GROUP + f] for c in range(5))
            bases = [
                pl.multiple_of(
                    jnp.where(k * 8 < start, big * SLOTS, small * SLOTS - start) + k * 8, 8
                )
                for k in range(SLOTS // 8)
            ]
            info.append((first, start, second, bases))

        for f in range(GROUP):
            for k, base in enumerate(info[f][3]):
                for j in range(8):
                    r = slot_ref[base + j]
                    at = f * SLOTS + k * 8 + j
                    for c in range(3):
                        slots[c, at : at + 1, :] = table[c, pl.ds(r, 1), :]

        atom_rows = jnp.transpose(slots[2])
        dists, inverses, offsets, weights = [], [], [], []
        for f in range(GROUP):
            first, start, second, bases = info[f]
            col = slots[2, rows_of(f), :]
            row = atom_rows[0:8, rows_of(f)]
            row = jnp.concatenate([row, row], axis=1)
            off = [col[:, c : c + 1] - row[c : c + 1, :] for c in range(3)]
            square = off[0] * off[0] + off[1] * off[1] + off[2] * off[2] + PAIR_SOFTEN
            inverse = lax.rsqrt(square)

            def owner(i, dead):
                late = jnp.logical_and(i >= start, i < start + second)
                return jnp.where(i < first, 1, jnp.where(late, 2, dead))

            mine = owner(slot_row, 0)
            dists.append(jnp.where(mine == owner(slot_lane, -1), square * inverse, FAR))
            inverses.append(inverse)
            offsets.append(off)
            cap = jnp.concatenate([cap_ref[pl.ds(base, 8), :] for base in bases], axis=0)
            weights.append(jnp.where(mine > 0, cap, 0.0))
        dist2 = [jnp.concatenate([d, d], axis=1) for d in dists]
        weight = jnp.concatenate(weights, axis=0)

        def attention(layer, project):
            def part(f, quad, which):
                at = which * F + quad * QUAD
                return project[rows_of(f), at : at + QUAD]

            qs = [part(f, quad, 0) for f, quad in units]
            kbs = [spread_heads(part(f, quad, 1)) for f, quad in units]
            vbs = [spread_heads(part(f, quad, 2)) for f, quad in units]
            scores = [dot_nt(q, kb) for q, kb in zip(qs, kbs)]
            atts, by_dist, by_score = [], [], []
            for (f, quad), score in zip(units, scores):
                u = score * half
                th = jnp.tanh(u)
                silu = u + u * th
                span = span_ref[layer : layer + 1, quad * 256 : (quad + 1) * 256]
                damp = recip(dist2[f] + span)
                att = silu * damp
                atts.append(bf16(att))
                by_dist.append(att * damp)
                if layer == 1:
                    by_score.append(damp * ((1.0 + th) + (silu - silu * th)))
            span_cols = span_cols_ref[layer : layer + 1, :]
            message = [dot(att, vb) for att, vb in zip(atts, vbs)]
            message = jnp.concatenate(
                [jnp.concatenate(message[2 * f : 2 * f + 2], axis=1) for f in range(GROUP)], axis=0
            )
            return bf16(message * span_cols), (qs, kbs, vbs, atts, by_dist, by_score)

        gain = [gains_ref[i : i + 1, :] for i in range(LAYERS + 1)]
        h0 = jnp.concatenate([slots[0], slots[1]], axis=1)
        unit0, _ = norm_parts(h0)
        project0 = bf16(dot(bf16(unit0 * gain[0]), wqkv_ref[0]))
        message0, kept0 = attention(0, project0)
        h1 = h0 + dot(message0, wout_ref[0])
        unit1, scale1 = norm_parts(h1)
        project1 = bf16(dot(bf16(unit1 * gain[1]), wqkv_ref[1]))
        message1, kept1 = attention(1, project1)
        h2 = h1 + dot(message1, wout_ref[1])
        unit2, scale2 = norm_parts(h2)
        u = 0.5 * dot(bf16(unit2 * gain[2]), wread_ref[...])
        th = jnp.tanh(u)
        silu = u + u * th
        weighted = weight * wen_ref[...]
        energy_ref[...] += jnp.sum((weighted * silu).reshape(ROWS // 8, 8, QUAD), axis=0)

        dread = bf16((0.5 * weighted) * ((1.0 + th) + (silu - silu * th)))
        dh2 = norm_back(dot_nt(dread, wread_ref[...]), gain[2], unit2, scale2)
        dmsg1 = bf16(dot_nt(bf16(dh2), wout_ref[1]) * span_cols_ref[1:2, :])
        qs, kbs, vbs, atts, by_dist, by_score = kept1
        dms = [dmsg1[rows_of(f), quad * QUAD : (quad + 1) * QUAD] for f, quad in units]
        datts = [dot_nt(dm, vb) for dm, vb in zip(dms, vbs)]
        dvs = [bf16(fold_heads(dot_tn(att, dm))) for att, dm in zip(atts, dms)]
        dss = [bf16(datt * slope) for datt, slope in zip(datts, by_score)]
        dqs = [bf16(dot(ds, kb) * half) for ds, kb in zip(dss, kbs)]
        dks = [bf16(fold_heads(dot_tn(ds, q)) * half) for ds, q in zip(dss, qs)]
        pulls = [datt * slope for datt, slope in zip(datts, by_dist)]
        dproject = jnp.concatenate(
            [
                jnp.concatenate(
                    [x[2 * f + quad] for x in (dqs, dks, dvs) for quad in range(2)], axis=1
                )
                for f in range(GROUP)
            ],
            axis=0,
        )
        dh1 = dh2 + norm_back(dot_nt(dproject, wqkv_ref[1]), gain[1], unit1, scale1)
        dmsg0 = bf16(dot_nt(bf16(dh1), wout_ref[0]) * span_cols_ref[0:1, :])
        datts = [
            dot_nt(dmsg0[rows_of(f), quad * QUAD : (quad + 1) * QUAD], vb)
            for (f, quad), vb in zip(units, kept0[2])
        ]
        pulls = [old + datt * slope for old, datt, slope in zip(pulls, datts, kept0[4])]
        force_rows = []
        for f in range(GROUP):
            pull = pulls[2 * f] + pulls[2 * f + 1]
            pull = (pull[:, :QUAD] + pull[:, QUAD:]) * inverses[f]
            pull = pull[:, :SLOTS] + pull[:, SLOTS:]
            pull = pull + jnp.transpose(pull)
            for c in range(3):
                force_rows.append(
                    -jnp.sum(pull * offsets[f][c][:, :SLOTS], axis=0, keepdims=True)
                )
        packed = jnp.concatenate(
            [
                jnp.concatenate([force_rows[3 * f + c] for f in range(GROUP)], axis=1)
                for c in range(3)
            ]
            + [jnp.zeros((5, ROWS), jnp.float32)],
            axis=0,
        )
        slot_force[:, 8:16] = jnp.transpose(packed)

        for f in range(GROUP):
            for k, base in enumerate(info[f][3]):
                rs = [slot_ref[base + j] for j in range(8)]
                old = [table[2, pl.ds(r, 1), :] for r in rs]
                for j in range(8):
                    at = f * SLOTS + k * 8 + j
                    table[2, pl.ds(rs[j], 1), :] = old[j] + slot_force[at : at + 1, :]
        return carry

    lax.fori_loop(0, (made + GROUP - 1) // GROUP, one_block, 0)

    pick = (
        lax.broadcasted_iota(jnp.int32, (16, TILE), 0) + 8
        == lax.broadcasted_iota(jnp.int32, (16, TILE), 1)
    ).astype(jnp.bfloat16)
    for i in range(tiles // 8):
        rows = dot_nt(pick, bf16(table[2, i * 1024 : (i + 1) * 1024, :]))
        for c in range(3):
            for k in range(8):
                force_ref[i, c, k : k + 1, :] = rows[c : c + 1, k * TILE : (k + 1) * TILE]


def fragment_model(near8, near_features, slot_index, atom_count, cap_weight, weights):
    w_qkv, w_out, gains, rates, w_read, w_energy = weights
    tiles = near8.shape[0]
    frags = atom_count.shape[0]
    smem = pl.BlockSpec(memory_space=pltpu.SMEM)
    vmem = pl.BlockSpec(memory_space=pltpu.VMEM)
    ids = jnp.arange(frags, dtype=jnp.int32)
    key = atom_count * 64 + ids
    place = jnp.sum(key[None, :] > key[:, None], axis=1)
    order = jnp.sum(jnp.where(place[None, :] == ids[:, None], key[None, :], 0), axis=1)
    spans = 1.0 / rates
    force, energy = pl.pallas_call(
        fragment_body,
        out_shape=(
            jax.ShapeDtypeStruct((tiles // 8, 3, 8, TILE), jnp.float32),
            jax.ShapeDtypeStruct((8, TILE), jnp.float32),
        ),
        in_specs=[smem, smem] + [vmem] * 10,
        out_specs=(vmem, vmem),
        scratch_shapes=[
            pltpu.VMEM((3, tiles * TILE, TILE), jnp.float32),
            pltpu.VMEM((3, ROWS, TILE), jnp.float32),
            pltpu.VMEM((ROWS, TILE), jnp.float32),
            pltpu.SMEM((5, frags + GROUP + 1), jnp.int32),
        ],
        compiler_params=pltpu.CompilerParams(vmem_limit_bytes=56 * MIB),
        name="fragments",
    )(
        order,
        slot_index.reshape(-1),
        near8,
        near_features,
        jnp.broadcast_to(cap_weight.reshape(-1, 1), (frags * SLOTS, TILE)),
        w_qkv,
        w_out,
        gains,
        jnp.repeat(spans, SLOTS, axis=1),
        jnp.repeat(spans, F // HEADS, axis=1),
        w_read,
        w_energy.reshape(1, -1),
    )
    return force, energy


def home_body(
    force_ref,
    pair_ref,
    frag_energy_ref,
    pair_energy_ref,
    out_ref,
    energy_ref,
    landing,
    by_sub,
    by_brick,
    force_send,
    force_recv,
    sub_send,
    sub_recv,
    brick_send,
    brick_recv,
):
    bricks, subs = by_brick.shape[0], by_sub.shape[0]
    brick, sub = lax.axis_index("brick"), lax.axis_index("sub")
    mesh_id = pl.DeviceIdType.MESH
    around = [(u, v) for u in (-1, 0, 1) for v in (-1, 0, 1) if (u, v) != (0, 0)]

    def inside(u, v):
        b, s = brick + u, sub + v
        return (b >= 0) & (b < bricks) & (s >= 0) & (s < subs)

    sub_peers = [(brick, lax.rem(sub + d, subs)) for d in range(1, subs)]
    brick_peers = [(lax.rem(brick + d, bricks), sub) for d in range(1, bricks)]

    barrier = pltpu.get_barrier_semaphore()
    for peer in sub_peers + brick_peers:
        pl.semaphore_signal(barrier, inc=1, device_id=peer, device_id_type=mesh_id)
    corners = [(u, v) for u, v in around if u != 0 and v != 0]
    for u, v in corners:

        @pl.when(inside(u, v))
        def _(u=u, v=v):
            pl.semaphore_signal(
                barrier, inc=1, device_id=(brick + u, sub + v), device_id_type=mesh_id
            )

    beside = [
        jnp.where(at > 0, 1, 0) + jnp.where(at < size - 1, 1, 0)
        for at, size in ((brick, bricks), (sub, subs))
    ]
    pl.semaphore_wait(barrier, subs + bricks - 2 + beside[0] * beside[1])

    def energy_copy(store, send, recv, k, slot, peer):
        return pltpu.make_async_remote_copy(
            src_ref=store.at[slot],
            dst_ref=store.at[slot],
            send_sem=send.at[k],
            recv_sem=recv.at[slot],
            device_id=peer,
            device_id_type=mesh_id,
        )

    by_sub[sub] = frag_energy_ref[...] + (0.5 * COULOMB_UNIT) * pair_energy_ref[...]
    for k, peer in enumerate(sub_peers):
        energy_copy(by_sub, sub_send, sub_recv, k, sub, peer).start()

    def force_copy(u, v):
        k = (u + 1) * 3 + v + 1
        return pltpu.make_async_remote_copy(
            src_ref=force_ref.at[k],
            dst_ref=landing.at[k],
            send_sem=force_send.at[k],
            recv_sem=force_recv.at[k],
            device_id=(brick + u, sub + v),
            device_id_type=mesh_id,
        )

    for u, v in around:

        @pl.when(inside(u, v))
        def _(u=u, v=v):
            force_copy(u, v).start()

    for k, peer in enumerate(sub_peers):
        energy_copy(by_sub, sub_send, sub_recv, k, peer[1], peer).wait_recv()
    by_brick[brick] = jnp.sum(by_sub[...], axis=0)
    for k, peer in enumerate(brick_peers):
        energy_copy(by_brick, brick_send, brick_recv, k, brick, peer).start()

    out_ref[...] = force_ref[4] + COULOMB_UNIT * pair_ref[...]
    for u, v in around:
        @pl.when(inside(-u, -v))
        def _(u=u, v=v):
            force_copy(u, v).wait_recv()
            out_ref[...] += landing[(u + 1) * 3 + v + 1]

    for k, peer in enumerate(brick_peers):
        energy_copy(by_brick, brick_send, brick_recv, k, peer[0], peer).wait_recv()
    energy_ref[0, 0] = jnp.sum(jnp.sum(by_brick[...], axis=0))

    for u, v in around:

        @pl.when(inside(u, v))
        def _(u=u, v=v):
            force_copy(u, v).wait_send()

    for k, peer in enumerate(sub_peers):
        energy_copy(by_sub, sub_send, sub_recv, k, sub, peer).wait_send()
    for k, peer in enumerate(brick_peers):
        energy_copy(by_brick, brick_send, brick_recv, k, brick, peer).wait_send()


def bring_home(row_force, pair_force, frag_energy, pair_energy):
    bricks, subs = lax.axis_size("brick"), lax.axis_size("sub")
    vmem = pl.BlockSpec(memory_space=pltpu.VMEM)
    block = row_force.shape[1:]
    dma = pltpu.SemaphoreType.DMA
    return pl.pallas_call(
        home_body,
        out_shape=(
            jax.ShapeDtypeStruct(block, jnp.float32),
            jax.ShapeDtypeStruct((1, 1), jnp.float32),
        ),
        in_specs=[vmem] * 4,
        out_specs=(vmem, pl.BlockSpec(memory_space=pltpu.SMEM)),
        scratch_shapes=[
            pltpu.VMEM((9,) + block, jnp.float32),
            pltpu.VMEM((subs, 8, TILE), jnp.float32),
            pltpu.VMEM((bricks, 8, TILE), jnp.float32),
            dma((9,)),
            dma((9,)),
            dma((subs,)),
            dma((subs,)),
            dma((bricks,)),
            dma((bricks,)),
        ],
        compiler_params=pltpu.CompilerParams(collective_id=1, has_side_effects=True),
        name="bring_home",
    )(row_force, pair_force, frag_energy, pair_energy)


def with_halo(x, sides, width):
    for axis, dim in sides:
        devices, length = (lax.axis_size(axis), x.shape[dim])
        up = [(i, (i + 1) % devices) for i in range(devices - 1)]
        down = [(j, i) for i, j in up]
        last = lax.slice_in_dim(x, length - width, length, axis=dim)
        initial = lax.slice_in_dim(x, 0, width, axis=dim)
        before = lax.ppermute(last, axis, up)
        after = lax.ppermute(initial, axis, down)
        x = jnp.concatenate([before, x, after], axis=dim)
    return x


def body(
    atom_features,
    positions,
    charges,
    slot_index,
    atom_count,
    cap_weight,
    tile_pairs,
    tile_count,
    w_qkv,
    w_out,
    gains,
    rates,
    w_read,
    w_energy,
):
    own_size = atom_features.shape[2]
    own_tiles = own_size // TILE
    own8 = jnp.concatenate([positions.reshape(3, -1), charges.reshape(1, -1)], axis=0)
    own8 = jnp.pad(own8, ((0, 4), (0, 0))).reshape(8, own_tiles, TILE).transpose(1, 0, 2)
    near8 = with_halo(own8[None, None], (("brick", 0), ("sub", 1)), 1).reshape(-1, 8, TILE)
    near_features = with_halo(atom_features, (("brick", 0), ("sub", 1)), 1)
    pair_force, pair_energy = solvent_pairs(
        own8, near8, tile_pairs.reshape(2, -1), tile_count.reshape(1)
    )
    row_force, frag_energy = fragment_model(
        near8,
        near_features.reshape(-1, F),
        slot_index,
        atom_count,
        cap_weight,
        (w_qkv, w_out, gains, rates, w_read, w_energy),
    )
    forces, energy = bring_home(row_force, pair_force, frag_energy, pair_energy)
    return forces.reshape(3, 1, 1, own_size), energy.reshape(())


def solution(mesh):
    in_specs = (
        P("brick", "sub", None, None),
        P(None, "brick", "sub", None),
        P("brick", "sub", None),
        P(("brick", "sub"), None),
        P(("brick", "sub")),
        P(("brick", "sub"), None),
        P(None, "brick", "sub", None),
        P("brick", "sub"),
        P(),
        P(),
        P(),
        P(),
        P(),
        P(),
    )
    out_specs = (P(None, "brick", "sub", None), P())
    return jax.shard_map(body, mesh=mesh, in_specs=in_specs, out_specs=out_specs, check_vma=False)
```

```python
import math

import jax
import jax.numpy as jnp
from jax import lax
from jax.experimental import pallas as pl
from jax.experimental.pallas import tpu as pltpu
from jax.sharding import PartitionSpec as P

F = 256
HEADS = 8
LAYERS = 2
SLOTS = 64
TILE = 128
GROUP = 8
ROWS = GROUP * SLOTS
QUAD = 128

NORM_EPS = 1e-05
PAIR_SOFTEN = 0.01
SCREEN_RATE = 0.1
COULOMB_UNIT = 14.4
CHARGE_SOFTEN = 1.0
FAR = 1e30
GAUSS = 2.0 * SCREEN_RATE / math.sqrt(math.pi)
ERFC_P = 0.6
ERFC_C = (
    0.33858295223558404,
    0.33681896467541816,
    0.2948193558779553,
    0.06093701313639673,
    0.3109940554359323,
    -0.6781244471753995,
    0.4339317702022656,
    -0.0979638654555287,
)
MIB = 1024 * 1024


def dot(a, b):
    return lax.dot_general(a, b, (((1,), (0,)), ((), ())), preferred_element_type=jnp.float32)


def dot_nt(a, b):
    return lax.dot_general(a, b, (((1,), (1,)), ((), ())), preferred_element_type=jnp.float32)


def dot_tn(a, b):
    return lax.dot_general(a, b, (((0,), (0,)), ((), ())), preferred_element_type=jnp.float32)


def recip(x):
    return pl.reciprocal(x, approx=True)


def pair_body(pairs_ref, count_ref, own_ref, near_ref, force_ref, energy_ref, own_cols, total):
    own_tiles = own_ref.shape[0]
    total[...] = jnp.zeros_like(total)
    energy_ref[...] = jnp.zeros_like(energy_ref)
    for t in range(own_tiles):
        cols = jnp.transpose(own_ref[t])
        for c in range(4):
            own_cols[t, c] = jnp.broadcast_to(cols[:, c : c + 1], (TILE, TILE))
    chunk = 32
    lane = lax.broadcasted_iota(jnp.int32, (chunk, TILE), 1)
    row = lax.broadcasted_iota(jnp.int32, (chunk, TILE), 0)
    rel = lane - row

    def one_pair(p, carry):
        own = pairs_ref[0, p]
        near = pairs_ref[1, p]
        n = near_ref[near]
        xj, yj, zj, qj = (n[c : c + 1, :] for c in range(4))
        same = jnp.where(near - 4 * own_tiles == own, 0, 4 * TILE)
        en = jnp.zeros((8, TILE), jnp.float32)
        for start in range(0, TILE, chunk):
            at = pl.ds(start, chunk)
            dx = own_cols[own, 0, at, :] - xj
            dy = own_cols[own, 1, at, :] - yj
            dz = own_cols[own, 2, at, :] - zj
            qq = jnp.where(rel == same + start, 0.0, own_cols[own, 3, at, :] * qj)
            s = dx * dx + dy * dy + dz * dz + CHARGE_SOFTEN
            s = jnp.minimum(s, 1e6)
            rinv = lax.rsqrt(s)
            t = recip(1.0 + (ERFC_P * SCREEN_RATE) * (s * rinv))
            g = ERFC_C[-1]
            for coef in ERFC_C[-2::-1]:
                g = g * t + coef
            gauss = qq * jnp.exp2((-SCREEN_RATE * SCREEN_RATE * math.log2(math.e)) * s)
            screened = (g * t) * rinv
            en += jnp.sum((gauss * screened).reshape(chunk // 8, 8, TILE), axis=0)
            w = (gauss * (screened + GAUSS)) * (rinv * rinv)
            total[own, 0, at, :] += w * dx
            total[own, 1, at, :] += w * dy
            total[own, 2, at, :] += w * dz
        energy_ref[...] += en
        return carry

    lax.fori_loop(0, count_ref[0], one_pair, 0)
    for t in range(own_tiles):
        for c in range(3):
            force_ref[c, t : t + 1, :] = jnp.sum(
                jnp.transpose(total[t, c]), axis=0, keepdims=True
            )


def solvent_pairs(own8, near8, pairs, count):
    tiles = own8.shape[0]
    smem = pl.BlockSpec(memory_space=pltpu.SMEM)
    vmem = pl.BlockSpec(memory_space=pltpu.VMEM)
    return pl.pallas_call(
        pair_body,
        out_shape=(
            jax.ShapeDtypeStruct((3, tiles, TILE), jnp.float32),
            jax.ShapeDtypeStruct((8, TILE), jnp.float32),
        ),
        in_specs=[smem, smem, vmem, vmem],
        out_specs=(vmem, vmem),
        scratch_shapes=[
            pltpu.VMEM((tiles, 4, TILE, TILE), jnp.float32),
            pltpu.VMEM((tiles, 3, TILE, TILE), jnp.float32),
        ],
        compiler_params=pltpu.CompilerParams(vmem_limit_bytes=16 * MIB),
        name="pair_tiles",
    )(pairs, count, own8, near8)


def norm_parts(hidden):
    centre = jnp.mean(hidden, axis=-1, keepdims=True)
    shifted = hidden - centre
    spread = jnp.mean(shifted * shifted, axis=-1, keepdims=True)
    scale = lax.rsqrt(spread + NORM_EPS)
    return shifted * scale, scale


def norm_back(grad, gain, unit, scale):
    g = grad * gain
    mean_g = jnp.mean(g, axis=-1, keepdims=True)
    mean_gu = jnp.mean(g * unit, axis=-1, keepdims=True)
    return scale * (g - mean_g - unit * mean_gu)


def bf16(x):
    return x.astype(jnp.bfloat16)


def fragment_body(
    order_ref,
    slot_ref,
    near_ref,
    feat_ref,
    cap_ref,
    wqkv_ref,
    wout_ref,
    gains_ref,
    span_ref,
    span_cols_ref,
    wread_ref,
    wen_ref,
    force_ref,
    energy_ref,
    table,
    slots,
    slot_force,
    caps,
    bins,
):
    tiles = near_ref.shape[0]
    frags = cap_ref.shape[0]

    def widen(i, carry):
        for k in range(8):
            at = pl.multiple_of(i * 8 * TILE + k * TILE, TILE)
            both = feat_ref[i, k * TILE : (k + 1) * TILE, :].astype(jnp.float32)
            table[0, pl.ds(at, TILE), :] = both[:, :QUAD]
            table[1, pl.ds(at, TILE), :] = both[:, QUAD:]
            n = jnp.transpose(near_ref[i * 8 + k])
            table[2, pl.ds(at, TILE), :] = jnp.concatenate(
                [n, jnp.zeros((TILE, TILE - 8), jnp.float32)], axis=1
            )
        return carry

    lax.fori_loop(0, tiles // 8, widen, 0)
    slot_force[...] = jnp.zeros_like(slot_force)
    slots[0, :TILE, :] = jnp.zeros((TILE, TILE), jnp.float32)
    slots[0, :frags, :SLOTS] = cap_ref[...]
    cols = jnp.transpose(slots[0, :TILE, :])
    for f in range(frags):
        caps[f * SLOTS : (f + 1) * SLOTS, :] = jnp.broadcast_to(
            cols[:SLOTS, f : f + 1], (SLOTS, TILE)
        )
    energy_ref[...] = jnp.zeros_like(energy_ref)

    high = frags - 1
    made = 0
    runs = [order_ref[frags + k] for k in range(5)]
    for k in range(frags):
        fits = (
            ((k >= runs[0]) & (k < runs[1]))
            | ((k >= runs[2]) & (k < runs[3]))
            | (k >= runs[4])
        )
        both = fits & (k < high)
        big = order_ref[k]
        small = order_ref[jnp.maximum(high, 0)]
        bins[0, k] = big & 63
        bins[1, k] = small & 63
        bins[2, k] = big >> 6
        bins[3, k] = jnp.where(both, ((big >> 6) + 7) & -8, SLOTS)
        bins[4, k] = jnp.where(both, small >> 6, 0)
        made = jnp.where(k <= high, k + 1, made)
        high = high - jnp.where(both, 1, 0)
    for k in range(GROUP - 1):
        bins[0, made + k] = 0
        bins[1, made + k] = 0
        bins[2, made + k] = 0
        bins[3, made + k] = SLOTS
        bins[4, made + k] = 0

    lane = lax.broadcasted_iota(jnp.int32, (1, QUAD), 1)
    head_mask = [(lane // 32 == h).astype(jnp.bfloat16) for h in range(4)]
    head_pick = [lane // 32 == h for h in range(4)]
    slot_row = lax.broadcasted_iota(jnp.int32, (SLOTS, QUAD), 0)
    slot_lane = lax.broadcasted_iota(jnp.int32, (SLOTS, QUAD), 1) % SLOTS

    def spread_heads(x):
        return jnp.concatenate([x * head_mask[h] for h in range(4)], axis=0)

    def fold_heads(x):
        out = jnp.where(head_pick[0], x[0:SLOTS], 0.0)
        for h in range(1, 4):
            out = jnp.where(head_pick[h], x[h * SLOTS : (h + 1) * SLOTS], out)
        return out

    half = 0.5 / math.sqrt(32.0)
    units = [(f, quad) for f in range(GROUP) for quad in range(2)]

    def rows_of(f):
        return slice(f * SLOTS, (f + 1) * SLOTS)

    def one_block(b, carry):
        info = []
        for f in range(GROUP):
            big, small, first, start, second = (bins[c, b * GROUP + f] for c in range(5))
            bases = [
                pl.multiple_of(
                    jnp.where(k * 8 < start, big * SLOTS, small * SLOTS - start) + k * 8, 8
                )
                for k in range(SLOTS // 8)
            ]
            info.append((first, start, second, bases))

        for f in range(GROUP):
            for k, base in enumerate(info[f][3]):
                for j in range(8):
                    r = slot_ref[base + j]
                    at = f * SLOTS + k * 8 + j
                    for c in range(3):
                        slots[c, at : at + 1, :] = table[c, pl.ds(r, 1), :]

        atom_rows = jnp.transpose(slots[2])
        dists, inverses, offsets, weights = [], [], [], []
        for f in range(GROUP):
            first, start, second, bases = info[f]
            col = slots[2, rows_of(f), :]
            row = atom_rows[0:8, rows_of(f)]
            row = jnp.concatenate([row, row], axis=1)
            off = [col[:, c : c + 1] - row[c : c + 1, :] for c in range(3)]
            square = off[0] * off[0] + off[1] * off[1] + off[2] * off[2] + PAIR_SOFTEN
            inverse = lax.rsqrt(square)

            def owner(i, dead):
                late = jnp.logical_and(i >= start, i < start + second)
                return jnp.where(i < first, 1, jnp.where(late, 2, dead))

            mine = owner(slot_row, 0)
            dists.append(jnp.where(mine == owner(slot_lane, -1), square * inverse, FAR))
            inverses.append(inverse)
            offsets.append(off)
            cap = jnp.concatenate([caps[pl.ds(base, 8), :] for base in bases], axis=0)
            weights.append(jnp.where(mine > 0, cap, 0.0))
        dist2 = [jnp.concatenate([d, d], axis=1) for d in dists]
        weight = jnp.concatenate(weights, axis=0)

        def attention(layer, project):
            def part(f, quad, which):
                at = which * F + quad * QUAD
                return project[rows_of(f), at : at + QUAD]

            qs = [part(f, quad, 0) for f, quad in units]
            kbs = [spread_heads(part(f, quad, 1)) for f, quad in units]
            vbs = [spread_heads(part(f, quad, 2)) for f, quad in units]
            scores = [dot_nt(q, kb) for q, kb in zip(qs, kbs)]
            atts, by_dist, by_score = [], [], []
            for (f, quad), score in zip(units, scores):
                u = score * half
                th = jnp.tanh(u)
                silu = u + u * th
                span = span_ref[layer : layer + 1, quad * 256 : (quad + 1) * 256]
                damp = recip(dist2[f] + span)
                att = silu * damp
                atts.append(bf16(att))
                by_dist.append(att * damp)
                if layer == 1:
                    by_score.append(damp * ((1.0 + th) + (silu - silu * th)))
            span_cols = span_cols_ref[layer : layer + 1, :]
            message = [dot(att, vb) for att, vb in zip(atts, vbs)]
            message = jnp.concatenate(
                [jnp.concatenate(message[2 * f : 2 * f + 2], axis=1) for f in range(GROUP)], axis=0
            )
            return bf16(message * span_cols), (qs, kbs, vbs, atts, by_dist, by_score)

        gain = [gains_ref[i : i + 1, :] for i in range(LAYERS + 1)]
        h0 = jnp.concatenate([slots[0], slots[1]], axis=1)
        unit0, _ = norm_parts(h0)
        project0 = bf16(dot(bf16(unit0 * gain[0]), wqkv_ref[0]))
        message0, kept0 = attention(0, project0)
        h1 = h0 + dot(message0, wout_ref[0])
        unit1, scale1 = norm_parts(h1)
        project1 = bf16(dot(bf16(unit1 * gain[1]), wqkv_ref[1]))
        message1, kept1 = attention(1, project1)
        h2 = h1 + dot(message1, wout_ref[1])
        unit2, scale2 = norm_parts(h2)
        u = 0.5 * dot(bf16(unit2 * gain[2]), wread_ref[...])
        th = jnp.tanh(u)
        silu = u + u * th
        weighted = weight * wen_ref[...]
        energy_ref[...] += jnp.sum((weighted * silu).reshape(ROWS // 8, 8, QUAD), axis=0)

        dread = bf16((0.5 * weighted) * ((1.0 + th) + (silu - silu * th)))
        dh2 = norm_back(dot_nt(dread, wread_ref[...]), gain[2], unit2, scale2)
        dmsg1 = bf16(dot_nt(bf16(dh2), wout_ref[1]) * span_cols_ref[1:2, :])
        qs, kbs, vbs, atts, by_dist, by_score = kept1
        dms = [dmsg1[rows_of(f), quad * QUAD : (quad + 1) * QUAD] for f, quad in units]
        datts = [dot_nt(dm, vb) for dm, vb in zip(dms, vbs)]
        dvs = [bf16(fold_heads(dot_tn(att, dm))) for att, dm in zip(atts, dms)]
        dss = [bf16(datt * slope) for datt, slope in zip(datts, by_score)]
        dqs = [bf16(dot(ds, kb) * half) for ds, kb in zip(dss, kbs)]
        dks = [bf16(fold_heads(dot_tn(ds, q)) * half) for ds, q in zip(dss, qs)]
        pulls = [datt * slope for datt, slope in zip(datts, by_dist)]
        dproject = jnp.concatenate(
            [
                jnp.concatenate(
                    [x[2 * f + quad] for x in (dqs, dks, dvs) for quad in range(2)], axis=1
                )
                for f in range(GROUP)
            ],
            axis=0,
        )
        dh1 = dh2 + norm_back(dot_nt(dproject, wqkv_ref[1]), gain[1], unit1, scale1)
        dmsg0 = bf16(dot_nt(bf16(dh1), wout_ref[0]) * span_cols_ref[0:1, :])
        datts = [
            dot_nt(dmsg0[rows_of(f), quad * QUAD : (quad + 1) * QUAD], vb)
            for (f, quad), vb in zip(units, kept0[2])
        ]
        pulls = [old + datt * slope for old, datt, slope in zip(pulls, datts, kept0[4])]
        force_rows = []
        for f in range(GROUP):
            pull = pulls[2 * f] + pulls[2 * f + 1]
            pull = (pull[:, :QUAD] + pull[:, QUAD:]) * inverses[f]
            pull = pull[:, :SLOTS] + pull[:, SLOTS:]
            pull = pull + jnp.transpose(pull)
            for c in range(3):
                force_rows.append(
                    -jnp.sum(pull * offsets[f][c][:, :SLOTS], axis=0, keepdims=True)
                )
        packed = jnp.concatenate(
            [
                jnp.concatenate([force_rows[3 * f + c] for f in range(GROUP)], axis=1)
                for c in range(3)
            ]
            + [jnp.zeros((5, ROWS), jnp.float32)],
            axis=0,
        )
        slot_force[:, 8:16] = jnp.transpose(packed)

        for f in range(GROUP):
            for k, base in enumerate(info[f][3]):
                rs = [slot_ref[base + j] for j in range(8)]
                old = [table[2, pl.ds(r, 1), :] for r in rs]
                for j in range(8):
                    at = f * SLOTS + k * 8 + j
                    table[2, pl.ds(rs[j], 1), :] = old[j] + slot_force[at : at + 1, :]
        return carry

    lax.fori_loop(0, (made + GROUP - 1) // GROUP, one_block, 0)

    pick = (
        lax.broadcasted_iota(jnp.int32, (16, TILE), 0) + 8
        == lax.broadcasted_iota(jnp.int32, (16, TILE), 1)
    ).astype(jnp.bfloat16)
    for i in range(tiles // 8):
        rows = dot_nt(pick, bf16(table[2, i * 1024 : (i + 1) * 1024, :]))
        for c in range(3):
            for k in range(8):
                force_ref[i, c, k : k + 1, :] = rows[c : c + 1, k * TILE : (k + 1) * TILE]


def fragment_model(near8, near_features, slot_index, atom_count, cap_weight, weights):
    w_qkv, w_out, gains, rates, w_read, w_energy = weights
    tiles = near8.shape[0]
    frags = atom_count.shape[0]
    smem = pl.BlockSpec(memory_space=pltpu.SMEM)
    vmem = pl.BlockSpec(memory_space=pltpu.VMEM)
    ids = jnp.arange(frags, dtype=jnp.int32)
    key = atom_count * 64 + ids
    place = jnp.sum(key[None, :] > key[:, None], axis=1)
    order = jnp.sum(jnp.where(place[None, :] == ids[:, None], key[None, :], 0), axis=1)
    eighths = (atom_count + 7) // 8
    alone = jnp.sum((eighths >= 7).astype(jnp.int32))
    n6, n5, n3, n2 = (jnp.sum((eighths == k).astype(jnp.int32)) for k in (6, 5, 3, 2))
    with6 = jnp.minimum(n6, n2)
    with5 = jnp.minimum(n5, n2 - with6 + n3)
    runs = [alone, alone + with6, alone + n6, alone + n6 + with5, alone + n6 + n5]
    order = jnp.concatenate([order, jnp.stack(runs)])
    spans = 1.0 / rates
    force, energy = pl.pallas_call(
        fragment_body,
        out_shape=(
            jax.ShapeDtypeStruct((tiles // 8, 3, 8, TILE), jnp.float32),
            jax.ShapeDtypeStruct((8, TILE), jnp.float32),
        ),
        in_specs=[smem, smem] + [vmem] * 10,
        out_specs=(vmem, vmem),
        scratch_shapes=[
            pltpu.VMEM((3, tiles * TILE, TILE), jnp.float32),
            pltpu.VMEM((3, ROWS, TILE), jnp.float32),
            pltpu.VMEM((ROWS, TILE), jnp.float32),
            pltpu.VMEM((frags * SLOTS, TILE), jnp.float32),
            pltpu.SMEM((5, frags + GROUP + 1), jnp.int32),
        ],
        compiler_params=pltpu.CompilerParams(vmem_limit_bytes=56 * MIB),
        name="fragments",
    )(
        order,
        slot_index.reshape(-1),
        near8,
        near_features,
        cap_weight,
        w_qkv,
        w_out,
        gains,
        jnp.repeat(spans, SLOTS, axis=1),
        jnp.repeat(spans, F // HEADS, axis=1),
        w_read,
        w_energy.reshape(1, -1),
    )
    return force, energy


def home_body(
    force_ref,
    pair_ref,
    frag_energy_ref,
    pair_energy_ref,
    out_ref,
    energy_ref,
    landing,
    by_sub,
    by_brick,
    force_send,
    force_recv,
    sub_send,
    sub_recv,
    brick_send,
    brick_recv,
):
    bricks, subs = by_brick.shape[0], by_sub.shape[0]
    brick, sub = lax.axis_index("brick"), lax.axis_index("sub")
    mesh_id = pl.DeviceIdType.MESH
    around = [(u, v) for u in (-1, 0, 1) for v in (-1, 0, 1) if (u, v) != (0, 0)]

    def inside(u, v):
        b, s = brick + u, sub + v
        return (b >= 0) & (b < bricks) & (s >= 0) & (s < subs)

    sub_peers = [(brick, lax.rem(sub + d, subs)) for d in range(1, subs)]
    brick_peers = [(lax.rem(brick + d, bricks), sub) for d in range(1, bricks)]

    barrier = pltpu.get_barrier_semaphore()
    for peer in sub_peers + brick_peers:
        pl.semaphore_signal(barrier, inc=1, device_id=peer, device_id_type=mesh_id)
    corners = [(u, v) for u, v in around if u != 0 and v != 0]
    for u, v in corners:

        @pl.when(inside(u, v))
        def _(u=u, v=v):
            pl.semaphore_signal(
                barrier, inc=1, device_id=(brick + u, sub + v), device_id_type=mesh_id
            )

    beside = [
        jnp.where(at > 0, 1, 0) + jnp.where(at < size - 1, 1, 0)
        for at, size in ((brick, bricks), (sub, subs))
    ]
    pl.semaphore_wait(barrier, subs + bricks - 2 + beside[0] * beside[1])

    def energy_copy(store, send, recv, k, slot, peer):
        return pltpu.make_async_remote_copy(
            src_ref=store.at[slot],
            dst_ref=store.at[slot],
            send_sem=send.at[k],
            recv_sem=recv.at[slot],
            device_id=peer,
            device_id_type=mesh_id,
        )

    by_sub[sub] = frag_energy_ref[...] + (0.5 * COULOMB_UNIT) * pair_energy_ref[...]
    for k, peer in enumerate(sub_peers):
        energy_copy(by_sub, sub_send, sub_recv, k, sub, peer).start()

    def force_copy(u, v):
        k = (u + 1) * 3 + v + 1
        return pltpu.make_async_remote_copy(
            src_ref=force_ref.at[k],
            dst_ref=landing.at[k],
            send_sem=force_send.at[k],
            recv_sem=force_recv.at[k],
            device_id=(brick + u, sub + v),
            device_id_type=mesh_id,
        )

    for u, v in around:

        @pl.when(inside(u, v))
        def _(u=u, v=v):
            force_copy(u, v).start()

    for k, peer in enumerate(sub_peers):
        energy_copy(by_sub, sub_send, sub_recv, k, peer[1], peer).wait_recv()
    by_brick[brick] = jnp.sum(by_sub[...], axis=0)
    for k, peer in enumerate(brick_peers):
        energy_copy(by_brick, brick_send, brick_recv, k, brick, peer).start()

    out_ref[...] = force_ref[4] + COULOMB_UNIT * pair_ref[...]
    for u, v in around:
        @pl.when(inside(-u, -v))
        def _(u=u, v=v):
            force_copy(u, v).wait_recv()
            out_ref[...] += landing[(u + 1) * 3 + v + 1]

    for k, peer in enumerate(brick_peers):
        energy_copy(by_brick, brick_send, brick_recv, k, peer[0], peer).wait_recv()
    energy_ref[0, 0] = jnp.sum(jnp.sum(by_brick[...], axis=0))

    for u, v in around:

        @pl.when(inside(u, v))
        def _(u=u, v=v):
            force_copy(u, v).wait_send()

    for k, peer in enumerate(sub_peers):
        energy_copy(by_sub, sub_send, sub_recv, k, sub, peer).wait_send()
    for k, peer in enumerate(brick_peers):
        energy_copy(by_brick, brick_send, brick_recv, k, brick, peer).wait_send()


def bring_home(row_force, pair_force, frag_energy, pair_energy):
    bricks, subs = lax.axis_size("brick"), lax.axis_size("sub")
    vmem = pl.BlockSpec(memory_space=pltpu.VMEM)
    block = row_force.shape[1:]
    dma = pltpu.SemaphoreType.DMA
    return pl.pallas_call(
        home_body,
        out_shape=(
            jax.ShapeDtypeStruct(block, jnp.float32),
            jax.ShapeDtypeStruct((1, 1), jnp.float32),
        ),
        in_specs=[vmem] * 4,
        out_specs=(vmem, pl.BlockSpec(memory_space=pltpu.SMEM)),
        scratch_shapes=[
            pltpu.VMEM((9,) + block, jnp.float32),
            pltpu.VMEM((subs, 8, TILE), jnp.float32),
            pltpu.VMEM((bricks, 8, TILE), jnp.float32),
            dma((9,)),
            dma((9,)),
            dma((subs,)),
            dma((subs,)),
            dma((bricks,)),
            dma((bricks,)),
        ],
        compiler_params=pltpu.CompilerParams(collective_id=1, has_side_effects=True),
        name="bring_home",
    )(row_force, pair_force, frag_energy, pair_energy)


AROUND = [(u, v) for u in (-1, 0, 1) for v in (-1, 0, 1) if (u, v) != (0, 0)]
CHUNKS = 4


def block_of(u, v):
    return (u + 1) * 3 + v + 1


def halo_body(
    own_ref,
    feat_ref,
    near_ref,
    near_feat_ref,
    atom_send,
    atom_recv,
    side_send,
    side_recv,
    ahead_send,
    ahead_recv,
    corner_send,
    corner_recv,
    local_sem,
):
    bricks, subs = lax.axis_size("brick"), lax.axis_size("sub")
    brick, sub = lax.axis_index("brick"), lax.axis_index("sub")
    mesh_id = pl.DeviceIdType.MESH
    rows = feat_ref.shape[0]
    tiles = own_ref.shape[0]
    part = rows // CHUNKS

    def inside(u, v):
        b, s = brick + u, sub + v
        return (b >= 0) & (b < bricks) & (s >= 0) & (s < subs)

    barrier = pltpu.get_barrier_semaphore()
    for u, v in AROUND:

        @pl.when(inside(u, v))
        def _(u=u, v=v):
            pl.semaphore_signal(
                barrier, inc=1, device_id=(brick + u, sub + v), device_id_type=mesh_id
            )

    beside = [
        jnp.where(at > 0, 1, 0) + jnp.where(at < size - 1, 1, 0)
        for at, size in ((brick, bricks), (sub, subs))
    ]
    pl.semaphore_wait(barrier, beside[0] + beside[1] + beside[0] * beside[1])

    def atom_copy(u, v):
        k = block_of(-u, -v)
        return pltpu.make_async_remote_copy(
            src_ref=own_ref,
            dst_ref=near_ref.at[pl.ds(k * tiles, tiles)],
            send_sem=atom_send.at[k],
            recv_sem=atom_recv.at[k],
            device_id=(brick + u, sub + v),
            device_id_type=mesh_id,
        )

    def ahead_copy(u, c):
        i = (u + 1) // 2
        return pltpu.make_async_remote_copy(
            src_ref=feat_ref.at[pl.ds(c * part, part)],
            dst_ref=near_feat_ref.at[block_of(-u, 0), pl.ds(c * part, part)],
            send_sem=ahead_send.at[i, c],
            recv_sem=ahead_recv.at[i, c],
            device_id=(brick + u, sub),
            device_id_type=mesh_id,
        )

    def side_copy(v):
        i = (v + 1) // 2
        return pltpu.make_async_remote_copy(
            src_ref=feat_ref,
            dst_ref=near_feat_ref.at[block_of(0, -v)],
            send_sem=side_send.at[i],
            recv_sem=side_recv.at[i],
            device_id=(brick, sub + v),
            device_id_type=mesh_id,
        )

    def corner_copy(w, v, c):
        i = (w + 1) + (v + 1) // 2
        at = pl.ds(c * part, part)
        return pltpu.make_async_remote_copy(
            src_ref=near_feat_ref.at[block_of(w, 0), at],
            dst_ref=near_feat_ref.at[block_of(w, -v), at],
            send_sem=corner_send.at[i, c],
            recv_sem=corner_recv.at[i, c],
            device_id=(brick, sub + v),
            device_id_type=mesh_id,
        )

    for u, v in AROUND:

        @pl.when(inside(u, v))
        def _(u=u, v=v):
            atom_copy(u, v).start()

    for c in range(CHUNKS):
        for u in (-1, 1):

            @pl.when(inside(u, 0))
            def _(u=u, c=c):
                ahead_copy(u, c).start()

        if c == 0:
            for v in (-1, 1):

                @pl.when(inside(0, v))
                def _(v=v):
                    side_copy(v).start()

    local = pltpu.make_async_copy(feat_ref, near_feat_ref.at[block_of(0, 0)], local_sem)
    local.start()
    near_ref[pl.ds(block_of(0, 0) * tiles, tiles)] = own_ref[...]
    for u, v in AROUND:
        k = block_of(u, v)

        @pl.when(jnp.logical_not(inside(u, v)))
        def _(k=k):
            near_ref[pl.ds(k * tiles, tiles)] = jnp.zeros_like(own_ref)

    def forward(c):
        for w in (-1, 1):

            @pl.when(inside(w, 0))
            def _(w=w):
                ahead_copy(-w, c).wait_recv()
                for v in (-1, 1):

                    @pl.when(inside(0, v))
                    def _(w=w, v=v):
                        corner_copy(w, v, c).start()

    for c in range(CHUNKS):
        forward(c)

    for u, v in AROUND:

        @pl.when(inside(-u, -v))
        def _(u=u, v=v):
            atom_copy(u, v).wait_recv()

    for v in (-1, 1):

        @pl.when(inside(0, -v))
        def _(v=v):
            side_copy(v).wait_recv()

    for w in (-1, 1):
        for v in (-1, 1):

            @pl.when(inside(w, -v))
            def _(w=w, v=v):
                for c in range(CHUNKS):
                    corner_copy(w, v, c).wait_recv()

    local.wait()
    for u, v in AROUND:

        @pl.when(inside(u, v))
        def _(u=u, v=v):
            atom_copy(u, v).wait_send()

    for u in (-1, 1):

        @pl.when(inside(u, 0))
        def _(u=u):
            for c in range(CHUNKS):
                ahead_copy(u, c).wait_send()

    for v in (-1, 1):

        @pl.when(inside(0, v))
        def _(v=v):
            side_copy(v).wait_send()

    for w in (-1, 1):
        for v in (-1, 1):

            @pl.when(inside(w, v))
            def _(w=w, v=v):
                for c in range(CHUNKS):
                    corner_copy(w, v, c).wait_send()


def halo(own8, features):
    vmem = pl.BlockSpec(memory_space=pltpu.VMEM)
    hbm = pl.BlockSpec(memory_space=pl.ANY)
    dma = pltpu.SemaphoreType.DMA
    return pl.pallas_call(
        halo_body,
        out_shape=(
            jax.ShapeDtypeStruct((9 * own8.shape[0],) + own8.shape[1:], own8.dtype),
            jax.ShapeDtypeStruct((9,) + features.shape, features.dtype),
        ),
        in_specs=[vmem, hbm],
        out_specs=(vmem, hbm),
        scratch_shapes=[
            dma((9,)),
            dma((9,)),
            dma((2,)),
            dma((2,)),
            dma((2, CHUNKS)),
            dma((2, CHUNKS)),
            dma((4, CHUNKS)),
            dma((4, CHUNKS)),
            dma(()),
        ],
        compiler_params=pltpu.CompilerParams(collective_id=2, has_side_effects=True),
        name="halo",
    )(own8, features)


def body(
    atom_features,
    positions,
    charges,
    slot_index,
    atom_count,
    cap_weight,
    tile_pairs,
    tile_count,
    w_qkv,
    w_out,
    gains,
    rates,
    w_read,
    w_energy,
):
    own_size = atom_features.shape[2]
    own_tiles = own_size // TILE
    own8 = jnp.concatenate([positions.reshape(3, -1), charges.reshape(1, -1)], axis=0)
    own8 = jnp.pad(own8, ((0, 4), (0, 0))).reshape(8, own_tiles, TILE).transpose(1, 0, 2)
    near8, near_features = halo(own8, atom_features.reshape(own_size, -1))
    pair_force, pair_energy = solvent_pairs(
        own8, near8, tile_pairs.reshape(2, -1), tile_count.reshape(1)
    )
    row_force, frag_energy = fragment_model(
        near8,
        near_features,
        slot_index,
        atom_count,
        cap_weight,
        (w_qkv, w_out, gains, rates, w_read, w_energy),
    )
    forces, energy = bring_home(row_force, pair_force, frag_energy, pair_energy)
    return forces.reshape(3, 1, 1, own_size), energy.reshape(())


def solution(mesh):
    in_specs = (
        P("brick", "sub", None, None),
        P(None, "brick", "sub", None),
        P("brick", "sub", None),
        P(("brick", "sub"), None),
        P(("brick", "sub")),
        P(("brick", "sub"), None),
        P(None, "brick", "sub", None),
        P("brick", "sub"),
        P(),
        P(),
        P(),
        P(),
        P(),
        P(),
    )
    out_specs = (P(None, "brick", "sub", None), P())
    return jax.shard_map(body, mesh=mesh, in_specs=in_specs, out_specs=out_specs, check_vma=False)
```

```python
import math

import jax
import jax.numpy as jnp
from jax import lax
from jax.experimental import pallas as pl
from jax.experimental.pallas import tpu as pltpu
from jax.sharding import PartitionSpec as P

F = 256
HEADS = 8
LAYERS = 2
SLOTS = 64
TILE = 128
GROUP = 8
ROWS = GROUP * SLOTS
QUAD = 128

NORM_EPS = 1e-05
PAIR_SOFTEN = 0.01
SCREEN_RATE = 0.1
COULOMB_UNIT = 14.4
CHARGE_SOFTEN = 1.0
FAR = 1e30
GAUSS = 2.0 * SCREEN_RATE / math.sqrt(math.pi)
ERFC_P = 0.6
ERFC_C = (
    0.33858295223558404,
    0.33681896467541816,
    0.2948193558779553,
    0.06093701313639673,
    0.3109940554359323,
    -0.6781244471753995,
    0.4339317702022656,
    -0.0979638654555287,
)
MIB = 1024 * 1024


def dot(a, b):
    return lax.dot_general(a, b, (((1,), (0,)), ((), ())), preferred_element_type=jnp.float32)


def dot_nt(a, b):
    return lax.dot_general(a, b, (((1,), (1,)), ((), ())), preferred_element_type=jnp.float32)


def dot_tn(a, b):
    return lax.dot_general(a, b, (((0,), (0,)), ((), ())), preferred_element_type=jnp.float32)


def recip(x):
    return pl.reciprocal(x, approx=True)


def norm_parts(hidden):
    centre = jnp.mean(hidden, axis=-1, keepdims=True)
    shifted = hidden - centre
    spread = jnp.mean(shifted * shifted, axis=-1, keepdims=True)
    scale = lax.rsqrt(spread + NORM_EPS)
    return shifted * scale, scale


def norm_back(grad, gain, unit, scale):
    g = grad * gain
    mean_g = jnp.mean(g, axis=-1, keepdims=True)
    mean_gu = jnp.mean(g * unit, axis=-1, keepdims=True)
    return scale * (g - mean_g - unit * mean_gu)


def bf16(x):
    return x.astype(jnp.bfloat16)


def fragment_body(
    count_ref,
    slot_ref,
    rate_ref,
    near_ref,
    feat_ref,
    cap_ref,
    wqkv_ref,
    wout_ref,
    gains_ref,
    wread_ref,
    wen_ref,
    force_ref,
    energy_ref,
    table,
    slots,
    slot_force,
    caps,
    span_ref,
    span_cols_ref,
    order_ref,
    bins,
):
    tiles = near_ref.shape[0]
    frags = cap_ref.shape[0]

    def widen(i, carry):
        for k in range(8):
            at = pl.multiple_of(i * 8 * TILE + k * TILE, TILE)
            both = feat_ref[i, k * TILE : (k + 1) * TILE, :].astype(jnp.float32)
            table[0, pl.ds(at, TILE), :] = both[:, :QUAD]
            table[1, pl.ds(at, TILE), :] = both[:, QUAD:]
            n = jnp.transpose(near_ref[i * 8 + k])
            table[2, pl.ds(at, TILE), :] = jnp.concatenate(
                [n, jnp.zeros((TILE, TILE - 8), jnp.float32)], axis=1
            )
        return carry

    lax.fori_loop(0, tiles // 8, widen, 0)
    slot_force[...] = jnp.zeros_like(slot_force)
    head = lax.broadcasted_iota(jnp.int32, (1, HEADS * SLOTS), 1) // SLOTS
    head_col = lax.broadcasted_iota(jnp.int32, (1, F), 1) // (F // HEADS)
    for layer in range(LAYERS):
        wide = jnp.ones((1, HEADS * SLOTS), jnp.float32)
        cols = jnp.ones((1, F), jnp.float32)
        for h in range(HEADS):
            wide = jnp.where(head == h, rate_ref[layer, h], wide)
            cols = jnp.where(head_col == h, rate_ref[layer, h], cols)
        span_ref[layer : layer + 1, :] = 1.0 / wide
        span_cols_ref[layer : layer + 1, :] = 1.0 / cols
    slots[0, :TILE, :] = jnp.zeros((TILE, TILE), jnp.float32)
    slots[0, :frags, :SLOTS] = cap_ref[...]
    cols = jnp.transpose(slots[0, :TILE, :])
    for f in range(frags):
        caps[f] = jnp.broadcast_to(
            cols[:SLOTS, f : f + 1], (SLOTS, TILE)
        )
    energy_ref[...] = jnp.zeros_like(energy_ref)

    ends = {9: 0}
    made = 0
    for size in range(8, 1, -1):
        for k in range(frags):
            live = count_ref[k]
            order_ref[made] = live * 64 + k
            made += jnp.where((live + 7) >> 3 == size, 1, 0)
        ends[size] = made
    n6, n5, n3, n2 = (ends[k] - ends[k + 1] for k in (6, 5, 3, 2))
    with6 = jnp.minimum(n6, n2)
    with5 = jnp.minimum(n5, n2 - with6 + n3)
    runs = [ends[7], ends[7] + with6, ends[6], ends[6] + with5, ends[5]]
    high = frags - 1
    made = 0
    for k in range(frags):
        fits = (
            ((k >= runs[0]) & (k < runs[1]))
            | ((k >= runs[2]) & (k < runs[3]))
            | (k >= runs[4])
        )
        both = fits & (k < high)
        big = order_ref[k]
        small = order_ref[jnp.maximum(high, 0)]
        bins[0, k] = big & 63
        bins[1, k] = small & 63
        bins[2, k] = big >> 6
        bins[3, k] = jnp.where(both, ((big >> 6) + 7) & -8, SLOTS)
        bins[4, k] = jnp.where(both, small >> 6, 0)
        made = jnp.where(k <= high, k + 1, made)
        high = high - jnp.where(both, 1, 0)
    for k in range(GROUP - 1):
        bins[0, made + k] = 0
        bins[1, made + k] = 0
        bins[2, made + k] = 0
        bins[3, made + k] = SLOTS
        bins[4, made + k] = 0

    lane = lax.broadcasted_iota(jnp.int32, (1, QUAD), 1)
    head_mask = [(lane // 32 == h).astype(jnp.bfloat16) for h in range(4)]
    head_pick = [lane // 32 == h for h in range(4)]
    slot_row = lax.broadcasted_iota(jnp.int32, (SLOTS, QUAD), 0)
    slot_lane = lax.broadcasted_iota(jnp.int32, (SLOTS, QUAD), 1) % SLOTS

    def spread_heads(x):
        return jnp.concatenate([x * head_mask[h] for h in range(4)], axis=0)

    def fold_heads(x):
        out = jnp.where(head_pick[0], x[0:SLOTS], 0.0)
        for h in range(1, 4):
            out = jnp.where(head_pick[h], x[h * SLOTS : (h + 1) * SLOTS], out)
        return out

    half = 0.5 / math.sqrt(32.0)
    units = [(f, quad) for f in range(GROUP) for quad in range(2)]

    def rows_of(f):
        return slice(f * SLOTS, (f + 1) * SLOTS)

    def one_block(b, carry):
        info = []
        for f in range(GROUP):
            big, small, first, start, second = (bins[c, b * GROUP + f] for c in range(5))
            bases = []
            for k in range(SLOTS // 8):
                early = k * 8 < start
                at = pl.multiple_of(k * 8 - jnp.where(early, 0, start), 8)
                bases.append((jnp.where(early, big, small), at))
            info.append((first, start, second, bases))

        for f in range(GROUP):
            for k, (frag, first) in enumerate(info[f][3]):
                for j in range(8):
                    r = slot_ref[frag, first + j]
                    at = f * SLOTS + k * 8 + j
                    for c in range(3):
                        slots[c, at : at + 1, :] = table[c, pl.ds(r, 1), :]

        atom_rows = jnp.transpose(slots[2])
        dists, inverses, offsets, weights = [], [], [], []
        for f in range(GROUP):
            first, start, second, bases = info[f]
            col = slots[2, rows_of(f), :]
            row = atom_rows[0:8, rows_of(f)]
            row = jnp.concatenate([row, row], axis=1)
            off = [col[:, c : c + 1] - row[c : c + 1, :] for c in range(3)]
            square = off[0] * off[0] + off[1] * off[1] + off[2] * off[2] + PAIR_SOFTEN
            inverse = lax.rsqrt(square)

            def owner(i, dead):
                late = jnp.logical_and(i >= start, i < start + second)
                return jnp.where(i < first, 1, jnp.where(late, 2, dead))

            mine = owner(slot_row, 0)
            dists.append(jnp.where(mine == owner(slot_lane, -1), square * inverse, FAR))
            inverses.append(inverse)
            offsets.append(off)
            cap = jnp.concatenate([caps[frag, pl.ds(at, 8), :] for frag, at in bases], axis=0)
            weights.append(jnp.where(mine > 0, cap, 0.0))
        dist2 = [jnp.concatenate([d, d], axis=1) for d in dists]
        weight = jnp.concatenate(weights, axis=0)

        def attention(layer, project):
            def part(f, quad, which):
                at = which * F + quad * QUAD
                return project[rows_of(f), at : at + QUAD]

            qs = [part(f, quad, 0) for f, quad in units]
            kbs = [spread_heads(part(f, quad, 1)) for f, quad in units]
            vbs = [spread_heads(part(f, quad, 2)) for f, quad in units]
            scores = [dot_nt(q, kb) for q, kb in zip(qs, kbs)]
            atts, by_dist, by_score = [], [], []
            for (f, quad), score in zip(units, scores):
                u = score * half
                th = jnp.tanh(u)
                silu = u + u * th
                span = span_ref[layer : layer + 1, quad * 256 : (quad + 1) * 256]
                damp = recip(dist2[f] + span)
                att = silu * damp
                atts.append(bf16(att))
                by_dist.append(att * damp)
                if layer == 1:
                    by_score.append(damp * ((1.0 + th) + (silu - silu * th)))
            span_cols = span_cols_ref[layer : layer + 1, :]
            message = [dot(att, vb) for att, vb in zip(atts, vbs)]
            message = jnp.concatenate(
                [jnp.concatenate(message[2 * f : 2 * f + 2], axis=1) for f in range(GROUP)], axis=0
            )
            return bf16(message * span_cols), (qs, kbs, vbs, atts, by_dist, by_score)

        gain = [gains_ref[i : i + 1, :] for i in range(LAYERS + 1)]
        h0 = jnp.concatenate([slots[0], slots[1]], axis=1)
        unit0, _ = norm_parts(h0)
        project0 = bf16(dot(bf16(unit0 * gain[0]), wqkv_ref[0]))
        message0, kept0 = attention(0, project0)
        h1 = h0 + dot(message0, wout_ref[0])
        unit1, scale1 = norm_parts(h1)
        project1 = bf16(dot(bf16(unit1 * gain[1]), wqkv_ref[1]))
        message1, kept1 = attention(1, project1)
        h2 = h1 + dot(message1, wout_ref[1])
        unit2, scale2 = norm_parts(h2)
        u = 0.5 * dot(bf16(unit2 * gain[2]), wread_ref[...])
        th = jnp.tanh(u)
        silu = u + u * th
        weighted = weight * wen_ref[...]
        energy_ref[...] += jnp.sum((weighted * silu).reshape(ROWS // 8, 8, QUAD), axis=0)

        dread = bf16((0.5 * weighted) * ((1.0 + th) + (silu - silu * th)))
        dh2 = norm_back(dot_nt(dread, wread_ref[...]), gain[2], unit2, scale2)
        dmsg1 = bf16(dot_nt(bf16(dh2), wout_ref[1]) * span_cols_ref[1:2, :])
        qs, kbs, vbs, atts, by_dist, by_score = kept1
        dms = [dmsg1[rows_of(f), quad * QUAD : (quad + 1) * QUAD] for f, quad in units]
        datts = [dot_nt(dm, vb) for dm, vb in zip(dms, vbs)]
        dvs = [bf16(fold_heads(dot_tn(att, dm))) for att, dm in zip(atts, dms)]
        dss = [bf16(datt * slope) for datt, slope in zip(datts, by_score)]
        dqs = [bf16(dot(ds, kb) * half) for ds, kb in zip(dss, kbs)]
        dks = [bf16(fold_heads(dot_tn(ds, q)) * half) for ds, q in zip(dss, qs)]
        pulls = [datt * slope for datt, slope in zip(datts, by_dist)]
        dproject = jnp.concatenate(
            [
                jnp.concatenate(
                    [x[2 * f + quad] for x in (dqs, dks, dvs) for quad in range(2)], axis=1
                )
                for f in range(GROUP)
            ],
            axis=0,
        )
        dh1 = dh2 + norm_back(dot_nt(dproject, wqkv_ref[1]), gain[1], unit1, scale1)
        dmsg0 = bf16(dot_nt(bf16(dh1), wout_ref[0]) * span_cols_ref[0:1, :])
        datts = [
            dot_nt(dmsg0[rows_of(f), quad * QUAD : (quad + 1) * QUAD], vb)
            for (f, quad), vb in zip(units, kept0[2])
        ]
        pulls = [old + datt * slope for old, datt, slope in zip(pulls, datts, kept0[4])]
        force_rows = []
        for f in range(GROUP):
            pull = pulls[2 * f] + pulls[2 * f + 1]
            pull = (pull[:, :QUAD] + pull[:, QUAD:]) * inverses[f]
            pull = pull[:, :SLOTS] + pull[:, SLOTS:]
            pull = pull + jnp.transpose(pull)
            for c in range(3):
                force_rows.append(
                    -jnp.sum(pull * offsets[f][c][:, :SLOTS], axis=0, keepdims=True)
                )
        packed = jnp.concatenate(
            [
                jnp.concatenate([force_rows[3 * f + c] for f in range(GROUP)], axis=1)
                for c in range(3)
            ]
            + [jnp.zeros((5, ROWS), jnp.float32)],
            axis=0,
        )
        slot_force[:, 8:16] = jnp.transpose(packed)

        for f in range(GROUP):
            for k, (frag, first) in enumerate(info[f][3]):
                rs = [slot_ref[frag, first + j] for j in range(8)]
                old = [table[2, pl.ds(r, 1), :] for r in rs]
                for j in range(8):
                    at = f * SLOTS + k * 8 + j
                    table[2, pl.ds(rs[j], 1), :] = old[j] + slot_force[at : at + 1, :]
        return carry

    lax.fori_loop(0, (made + GROUP - 1) // GROUP, one_block, 0)

    pick = (
        lax.broadcasted_iota(jnp.int32, (16, TILE), 0) + 8
        == lax.broadcasted_iota(jnp.int32, (16, TILE), 1)
    ).astype(jnp.bfloat16)
    for i in range(tiles // 8):
        rows = dot_nt(pick, bf16(table[2, i * 1024 : (i + 1) * 1024, :]))
        for c in range(3):
            for k in range(8):
                force_ref[i, c, k : k + 1, :] = rows[c : c + 1, k * TILE : (k + 1) * TILE]


def fragment_model(near8, near_features, slot_index, atom_count, cap_weight, weights):
    w_qkv, w_out, gains, rates, w_read, w_energy = weights
    tiles = near8.shape[0]
    frags = atom_count.shape[0]
    smem = pl.BlockSpec(memory_space=pltpu.SMEM)
    vmem = pl.BlockSpec(memory_space=pltpu.VMEM)
    force, energy = pl.pallas_call(
        fragment_body,
        out_shape=(
            jax.ShapeDtypeStruct((tiles // 8, 3, 8, TILE), jnp.float32),
            jax.ShapeDtypeStruct((8, TILE), jnp.float32),
        ),
        in_specs=[smem, smem, smem] + [vmem] * 8,
        out_specs=(vmem, vmem),
        scratch_shapes=[
            pltpu.VMEM((3, tiles * TILE, TILE), jnp.float32),
            pltpu.VMEM((3, ROWS, TILE), jnp.float32),
            pltpu.VMEM((ROWS, TILE), jnp.float32),
            pltpu.VMEM((frags, SLOTS, TILE), jnp.float32),
            pltpu.VMEM((LAYERS, HEADS * SLOTS), jnp.float32),
            pltpu.VMEM((LAYERS, F), jnp.float32),
            pltpu.SMEM((frags + 1,), jnp.int32),
            pltpu.SMEM((5, frags + GROUP + 1), jnp.int32),
        ],
        compiler_params=pltpu.CompilerParams(vmem_limit_bytes=56 * MIB),
        name="fragments",
    )(
        atom_count,
        slot_index,
        rates,
        near8,
        near_features,
        cap_weight,
        w_qkv,
        w_out,
        gains,
        w_read,
        w_energy.reshape(1, -1),
    )
    return force, energy


def home_body(
    force_ref,
    pair_ref,
    frag_energy_ref,
    pair_energy_ref,
    out_ref,
    energy_ref,
    landing,
    by_sub,
    by_brick,
    force_send,
    force_recv,
    sub_send,
    sub_recv,
    brick_send,
    brick_recv,
):
    bricks, subs = by_brick.shape[0], by_sub.shape[0]
    brick, sub = lax.axis_index("brick"), lax.axis_index("sub")
    mesh_id = pl.DeviceIdType.MESH
    around = [(u, v) for u in (-1, 0, 1) for v in (-1, 0, 1) if (u, v) != (0, 0)]

    def inside(u, v):
        b, s = brick + u, sub + v
        return (b >= 0) & (b < bricks) & (s >= 0) & (s < subs)

    sub_peers = [(brick, lax.rem(sub + d, subs)) for d in range(1, subs)]
    brick_peers = [(lax.rem(brick + d, bricks), sub) for d in range(1, bricks)]

    barrier = pltpu.get_barrier_semaphore()
    for peer in sub_peers + brick_peers:
        pl.semaphore_signal(barrier, inc=1, device_id=peer, device_id_type=mesh_id)
    corners = [(u, v) for u, v in around if u != 0 and v != 0]
    for u, v in corners:

        @pl.when(inside(u, v))
        def _(u=u, v=v):
            pl.semaphore_signal(
                barrier, inc=1, device_id=(brick + u, sub + v), device_id_type=mesh_id
            )

    beside = [
        jnp.where(at > 0, 1, 0) + jnp.where(at < size - 1, 1, 0)
        for at, size in ((brick, bricks), (sub, subs))
    ]
    pl.semaphore_wait(barrier, subs + bricks - 2 + beside[0] * beside[1])

    def energy_copy(store, send, recv, k, slot, peer):
        return pltpu.make_async_remote_copy(
            src_ref=store.at[slot],
            dst_ref=store.at[slot],
            send_sem=send.at[k],
            recv_sem=recv.at[slot],
            device_id=peer,
            device_id_type=mesh_id,
        )

    by_sub[sub] = frag_energy_ref[...] + pair_energy_ref[...]
    for k, peer in enumerate(sub_peers):
        energy_copy(by_sub, sub_send, sub_recv, k, sub, peer).start()

    def force_copy(u, v):
        k = (u + 1) * 3 + v + 1
        return pltpu.make_async_remote_copy(
            src_ref=force_ref.at[k],
            dst_ref=landing.at[k],
            send_sem=force_send.at[k],
            recv_sem=force_recv.at[k],
            device_id=(brick + u, sub + v),
            device_id_type=mesh_id,
        )

    for u, v in around:

        @pl.when(inside(u, v))
        def _(u=u, v=v):
            force_copy(u, v).start()

    for k, peer in enumerate(sub_peers):
        energy_copy(by_sub, sub_send, sub_recv, k, peer[1], peer).wait_recv()
    by_brick[brick] = jnp.sum(by_sub[...], axis=0)
    for k, peer in enumerate(brick_peers):
        energy_copy(by_brick, brick_send, brick_recv, k, brick, peer).start()

    out_ref[...] = force_ref[4] + pair_ref[...]
    for u, v in around:
        @pl.when(inside(-u, -v))
        def _(u=u, v=v):
            force_copy(u, v).wait_recv()
            out_ref[...] += landing[(u + 1) * 3 + v + 1]

    for k, peer in enumerate(brick_peers):
        energy_copy(by_brick, brick_send, brick_recv, k, peer[0], peer).wait_recv()
    energy_ref[0, 0] = jnp.sum(jnp.sum(by_brick[...], axis=0))

    for u, v in around:

        @pl.when(inside(u, v))
        def _(u=u, v=v):
            force_copy(u, v).wait_send()

    for k, peer in enumerate(sub_peers):
        energy_copy(by_sub, sub_send, sub_recv, k, sub, peer).wait_send()
    for k, peer in enumerate(brick_peers):
        energy_copy(by_brick, brick_send, brick_recv, k, brick, peer).wait_send()


def bring_home(row_force, pair_force, frag_energy, pair_energy):
    bricks, subs = lax.axis_size("brick"), lax.axis_size("sub")
    vmem = pl.BlockSpec(memory_space=pltpu.VMEM)
    block = row_force.shape[1:]
    dma = pltpu.SemaphoreType.DMA
    return pl.pallas_call(
        home_body,
        out_shape=(
            jax.ShapeDtypeStruct(block, jnp.float32),
            jax.ShapeDtypeStruct((1, 1), jnp.float32),
        ),
        in_specs=[vmem] * 4,
        out_specs=(vmem, pl.BlockSpec(memory_space=pltpu.SMEM)),
        scratch_shapes=[
            pltpu.VMEM((9,) + block, jnp.float32),
            pltpu.VMEM((subs, 8, TILE), jnp.float32),
            pltpu.VMEM((bricks, 8, TILE), jnp.float32),
            dma((9,)),
            dma((9,)),
            dma((subs,)),
            dma((subs,)),
            dma((bricks,)),
            dma((bricks,)),
        ],
        compiler_params=pltpu.CompilerParams(
            collective_id=1, has_side_effects=True, vmem_limit_bytes=56 * MIB
        ),
        name="bring_home",
    )(row_force, pair_force, frag_energy, pair_energy)


AROUND = [(u, v) for u in (-1, 0, 1) for v in (-1, 0, 1) if (u, v) != (0, 0)]
CHUNKS = 4


STEP_PAIRS = 16


def three_parts(x):
    a = bf16(x).astype(jnp.float32)
    b = bf16(x - a).astype(jnp.float32)
    return [a, b, x - a - b, jnp.zeros_like(x)]


def block_of(u, v):
    return (u + 1) * 3 + v + 1


def halo_body(
    pairs_ref,
    count_ref,
    pos_ref,
    charge_ref,
    own_list_ref,
    feat_ref,
    near_ref,
    near_feat_ref,
    pair_force_ref,
    pair_energy_ref,
    parts,
    atom_send,
    atom_recv,
    side_send,
    side_recv,
    ahead_send,
    ahead_recv,
    corner_send,
    corner_recv,
    local_sem,
):
    bricks, subs = lax.axis_size("brick"), lax.axis_size("sub")
    brick, sub = lax.axis_index("brick"), lax.axis_index("sub")
    mesh_id = pl.DeviceIdType.MESH
    rows = feat_ref.shape[0]
    tiles = charge_ref.shape[0]
    part = rows // CHUNKS
    centre = block_of(0, 0) * tiles

    near_ref[pl.ds(centre, tiles)] = jnp.zeros((tiles, 8, TILE), jnp.float32)
    for t in range(tiles):
        for c in range(3):
            near_ref[centre + t, c : c + 1, :] = pos_ref[c, t : t + 1, :]
        near_ref[centre + t, 3:4, :] = charge_ref[t : t + 1, :]

    def inside(u, v):
        b, s = brick + u, sub + v
        return (b >= 0) & (b < bricks) & (s >= 0) & (s < subs)

    barrier = pltpu.get_barrier_semaphore()
    for u, v in AROUND:

        @pl.when(inside(u, v))
        def _(u=u, v=v):
            pl.semaphore_signal(
                barrier, inc=1, device_id=(brick + u, sub + v), device_id_type=mesh_id
            )

    beside = [
        jnp.where(at > 0, 1, 0) + jnp.where(at < size - 1, 1, 0)
        for at, size in ((brick, bricks), (sub, subs))
    ]
    pl.semaphore_wait(barrier, beside[0] + beside[1] + beside[0] * beside[1])

    def atom_copy(u, v):
        k = block_of(-u, -v)
        return pltpu.make_async_remote_copy(
            src_ref=near_ref.at[pl.ds(centre, tiles)],
            dst_ref=near_ref.at[pl.ds(k * tiles, tiles)],
            send_sem=atom_send.at[k],
            recv_sem=atom_recv.at[k],
            device_id=(brick + u, sub + v),
            device_id_type=mesh_id,
        )

    def ahead_copy(u, c):
        i = (u + 1) // 2
        return pltpu.make_async_remote_copy(
            src_ref=feat_ref.at[pl.ds(c * part, part)],
            dst_ref=near_feat_ref.at[block_of(-u, 0), pl.ds(c * part, part)],
            send_sem=ahead_send.at[i, c],
            recv_sem=ahead_recv.at[i, c],
            device_id=(brick + u, sub),
            device_id_type=mesh_id,
        )

    def side_copy(v):
        i = (v + 1) // 2
        return pltpu.make_async_remote_copy(
            src_ref=feat_ref,
            dst_ref=near_feat_ref.at[block_of(0, -v)],
            send_sem=side_send.at[i],
            recv_sem=side_recv.at[i],
            device_id=(brick, sub + v),
            device_id_type=mesh_id,
        )

    def corner_copy(w, v, c):
        i = (w + 1) + (v + 1) // 2
        at = pl.ds(c * part, part)
        return pltpu.make_async_remote_copy(
            src_ref=near_feat_ref.at[block_of(w, 0), at],
            dst_ref=near_feat_ref.at[block_of(w, -v), at],
            send_sem=corner_send.at[i, c],
            recv_sem=corner_recv.at[i, c],
            device_id=(brick, sub + v),
            device_id_type=mesh_id,
        )

    for u, v in AROUND:

        @pl.when(inside(u, v))
        def _(u=u, v=v):
            atom_copy(u, v).start()

    for c in range(CHUNKS):
        for u in (-1, 1):

            @pl.when(inside(u, 0))
            def _(u=u, c=c):
                ahead_copy(u, c).start()

        if c == 0:
            for v in (-1, 1):

                @pl.when(inside(0, v))
                def _(v=v):
                    side_copy(v).start()

    local = pltpu.make_async_copy(feat_ref, near_feat_ref.at[block_of(0, 0)], local_sem)
    local.start()
    for u, v in AROUND:
        k = block_of(u, v)

        @pl.when(jnp.logical_not(inside(u, v)))
        def _(k=k):
            near_ref[pl.ds(k * tiles, tiles)] = jnp.zeros((tiles, 8, TILE), jnp.float32)

    def forward(c):
        for w in (-1, 1):

            @pl.when(inside(w, 0))
            def _(w=w):
                ahead_copy(-w, c).wait_recv()
                for v in (-1, 1):

                    @pl.when(inside(0, v))
                    def _(w=w, v=v):
                        corner_copy(w, v, c).start()

    for u, v in AROUND:

        @pl.when(inside(-u, -v))
        def _(u=u, v=v):
            atom_copy(u, v).wait_recv()

    spread = (
        lax.broadcasted_iota(jnp.int32, (32, 4 * TILE), 0) % 8
        == lax.broadcasted_iota(jnp.int32, (32, 4 * TILE), 1) // TILE
    ).astype(jnp.bfloat16)
    chunk = 32
    rel = lax.broadcasted_iota(jnp.int32, (chunk, TILE), 1) - lax.broadcasted_iota(
        jnp.int32, (chunk, TILE), 0
    )

    def one_pair(p, carry):
        own = pairs_ref[0, p]
        near = pairs_ref[1, p]
        o = near_ref[centre + own]
        xi, yi, zi, qi = (o[c : c + 1, :] for c in range(4))
        cols = dot_tn(bf16(jnp.concatenate(three_parts(near_ref[near]), axis=0)), spread)
        same = jnp.where(near == own + centre, 0, 4 * TILE)
        sums = [jnp.zeros((8, TILE), jnp.float32) for _ in range(4)]
        for start in range(0, TILE, chunk):
            xj, yj, zj, qj = (
                cols[start : start + chunk, c * TILE : (c + 1) * TILE] for c in range(4)
            )
            dx, dy, dz = xi - xj, yi - yj, zi - zj
            qq = jnp.where(rel == same + start, 0.0, qi * qj)
            square = dx * dx + dy * dy + dz * dz + CHARGE_SOFTEN
            square = jnp.minimum(square, 1e6)
            rinv = lax.rsqrt(square)
            t = recip(1.0 + (ERFC_P * SCREEN_RATE) * (square * rinv))
            g = ERFC_C[-1]
            for coef in ERFC_C[-2::-1]:
                g = g * t + coef
            gauss = qq * jnp.exp2((-SCREEN_RATE * SCREEN_RATE * math.log2(math.e)) * square)
            screened = (g * t) * rinv
            w = (gauss * (screened + GAUSS)) * (rinv * rinv)
            for k, term in enumerate((w * dx, w * dy, w * dz, gauss * screened)):
                sums[k] += jnp.sum(term.reshape(chunk // 8, 8, TILE), axis=0)
        for k in range(4):
            parts[k, pl.ds(p, 1), :] = jnp.sum(sums[k], axis=0, keepdims=True)
        return carry

    pairs = own_list_ref.shape[1]
    done = 0
    for c in range(CHUNKS):
        forward(c)
        upto = (c + 1) * STEP_PAIRS if c < CHUNKS - 1 else pairs
        lax.fori_loop(done, upto, one_pair, 0)
        done = upto

    pick = (
        (own_list_ref[0:1, :] == lax.broadcasted_iota(jnp.int32, (16, pairs), 0))
        & (lax.broadcasted_iota(jnp.int32, (16, pairs), 1) < count_ref[0, 0])
    ).astype(jnp.bfloat16)
    for k in range(4):
        whole = sum(dot(pick, bf16(x)) for x in three_parts(parts[k])[:3])[:tiles]
        if k < 3:
            pair_force_ref[k] = COULOMB_UNIT * whole
        else:
            pair_energy_ref[...] = (0.5 * COULOMB_UNIT) * whole

    for v in (-1, 1):

        @pl.when(inside(0, -v))
        def _(v=v):
            side_copy(v).wait_recv()

    for w in (-1, 1):
        for v in (-1, 1):

            @pl.when(inside(w, -v))
            def _(w=w, v=v):
                for c in range(CHUNKS):
                    corner_copy(w, v, c).wait_recv()

    local.wait()
    for u, v in AROUND:

        @pl.when(inside(u, v))
        def _(u=u, v=v):
            atom_copy(u, v).wait_send()

    for u in (-1, 1):

        @pl.when(inside(u, 0))
        def _(u=u):
            for c in range(CHUNKS):
                ahead_copy(u, c).wait_send()

    for v in (-1, 1):

        @pl.when(inside(0, v))
        def _(v=v):
            side_copy(v).wait_send()

    for w in (-1, 1):
        for v in (-1, 1):

            @pl.when(inside(w, v))
            def _(w=w, v=v):
                for c in range(CHUNKS):
                    corner_copy(w, v, c).wait_send()


def halo(positions, charges, features, pairs, count):
    tiles = charges.shape[0]
    smem = pl.BlockSpec(memory_space=pltpu.SMEM)
    vmem = pl.BlockSpec(memory_space=pltpu.VMEM)
    hbm = pl.BlockSpec(memory_space=pl.ANY)
    dma = pltpu.SemaphoreType.DMA
    return pl.pallas_call(
        halo_body,
        out_shape=(
            jax.ShapeDtypeStruct((9 * tiles, 8, TILE), jnp.float32),
            jax.ShapeDtypeStruct((9,) + features.shape, features.dtype),
            jax.ShapeDtypeStruct((3, tiles, TILE), jnp.float32),
            jax.ShapeDtypeStruct((tiles, TILE), jnp.float32),
        ),
        in_specs=[smem, smem, vmem, vmem, vmem, hbm],
        out_specs=(vmem, hbm, vmem, vmem),
        scratch_shapes=[
            pltpu.VMEM((4, pairs.shape[1], TILE), jnp.float32),
            dma((9,)),
            dma((9,)),
            dma((2,)),
            dma((2,)),
            dma((2, CHUNKS)),
            dma((2, CHUNKS)),
            dma((4, CHUNKS)),
            dma((4, CHUNKS)),
            dma(()),
        ],
        compiler_params=pltpu.CompilerParams(
            collective_id=2, has_side_effects=True, vmem_limit_bytes=56 * MIB
        ),
        name="halo",
    )(pairs, count, positions, charges, pairs, features)


def body(
    atom_features,
    positions,
    charges,
    slot_index,
    atom_count,
    cap_weight,
    tile_pairs,
    tile_count,
    w_qkv,
    w_out,
    gains,
    rates,
    w_read,
    w_energy,
):
    own_size = atom_features.shape[2]
    own_tiles = own_size // TILE
    near8, near_features, pair_force, pair_energy = halo(
        positions.reshape(3, own_tiles, TILE),
        charges.reshape(own_tiles, TILE),
        atom_features.reshape(own_size, -1),
        tile_pairs.reshape(2, -1),
        tile_count,
    )
    row_force, frag_energy = fragment_model(
        near8,
        near_features,
        slot_index,
        atom_count,
        cap_weight,
        (w_qkv, w_out, gains, rates, w_read, w_energy),
    )
    forces, energy = bring_home(row_force, pair_force, frag_energy, pair_energy)
    return forces.reshape(3, 1, 1, own_size), energy.reshape(())


def solution(mesh):
    in_specs = (
        P("brick", "sub", None, None),
        P(None, "brick", "sub", None),
        P("brick", "sub", None),
        P(("brick", "sub"), None),
        P(("brick", "sub")),
        P(("brick", "sub"), None),
        P(None, "brick", "sub", None),
        P("brick", "sub"),
        P(),
        P(),
        P(),
        P(),
        P(),
        P(),
    )
    out_specs = (P(None, "brick", "sub", None), P())
    return jax.shard_map(body, mesh=mesh, in_specs=in_specs, out_specs=out_specs, check_vma=False)
```

```python
import math

import jax
import jax.numpy as jnp
from jax import lax
from jax.experimental import pallas as pl
from jax.experimental.pallas import tpu as pltpu
from jax.sharding import PartitionSpec as P

F = 256
HEADS = 8
LAYERS = 2
SLOTS = 64
TILE = 128
GROUP = 8
ROWS = GROUP * SLOTS
QUAD = 128

NORM_EPS = 1e-05
PAIR_SOFTEN = 0.01
SCREEN_RATE = 0.1
COULOMB_UNIT = 14.4
CHARGE_SOFTEN = 1.0
FAR = 1e30
GAUSS = 2.0 * SCREEN_RATE / math.sqrt(math.pi)
ERFC_P = 0.6
ERFC_C = (
    0.33858295223558404,
    0.33681896467541816,
    0.2948193558779553,
    0.06093701313639673,
    0.3109940554359323,
    -0.6781244471753995,
    0.4339317702022656,
    -0.0979638654555287,
)
MIB = 1024 * 1024


def dot(a, b):
    return lax.dot_general(a, b, (((1,), (0,)), ((), ())), preferred_element_type=jnp.float32)


def dot_nt(a, b):
    return lax.dot_general(a, b, (((1,), (1,)), ((), ())), preferred_element_type=jnp.float32)


def dot_tn(a, b):
    return lax.dot_general(a, b, (((0,), (0,)), ((), ())), preferred_element_type=jnp.float32)


def recip(x):
    return pl.reciprocal(x, approx=True)


def norm_parts(hidden):
    centre = jnp.mean(hidden, axis=-1, keepdims=True)
    shifted = hidden - centre
    spread = jnp.mean(shifted * shifted, axis=-1, keepdims=True)
    scale = lax.rsqrt(spread + NORM_EPS)
    return shifted * scale, scale


def norm_back(grad, gain, unit, scale):
    g = grad * gain
    mean_g = jnp.mean(g, axis=-1, keepdims=True)
    mean_gu = jnp.mean(g * unit, axis=-1, keepdims=True)
    return scale * (g - mean_g - unit * mean_gu)


def bf16(x):
    return x.astype(jnp.bfloat16)


def fragment_body(
    count_ref,
    slot_ref,
    rate_ref,
    near_ref,
    feat_ref,
    cap_ref,
    wqkv_ref,
    wout_ref,
    gains_ref,
    wread_ref,
    wen_ref,
    force_ref,
    energy_ref,
    table,
    forces,
    slots,
    slot_force,
    caps,
    span_ref,
    span_cols_ref,
    order_ref,
    bins,
):
    tiles = near_ref.shape[0]
    frags = cap_ref.shape[0]

    def widen(i, carry):
        for k in range(8):
            at = pl.multiple_of(i * 8 * TILE + k * TILE, TILE)
            both = feat_ref[i, k * TILE : (k + 1) * TILE, :].astype(jnp.float32)
            table[0, pl.ds(at, TILE), :] = both[:, :QUAD]
            table[1, pl.ds(at, TILE), :] = both[:, QUAD:]
            n = jnp.transpose(near_ref[i * 8 + k])
            table[2, pl.ds(at, TILE), :] = jnp.concatenate(
                [n, jnp.zeros((TILE, TILE - 8), jnp.float32)], axis=1
            )
            forces[pl.ds(at, TILE), :] = jnp.zeros((TILE, TILE), jnp.float32)
        return carry

    lax.fori_loop(0, tiles // 8, widen, 0)
    slot_force[...] = jnp.zeros_like(slot_force)
    head = lax.broadcasted_iota(jnp.int32, (1, HEADS * SLOTS), 1) // SLOTS
    head_col = lax.broadcasted_iota(jnp.int32, (1, F), 1) // (F // HEADS)
    for layer in range(LAYERS):
        wide = jnp.ones((1, HEADS * SLOTS), jnp.float32)
        cols = jnp.ones((1, F), jnp.float32)
        for h in range(HEADS):
            wide = jnp.where(head == h, rate_ref[layer, h], wide)
            cols = jnp.where(head_col == h, rate_ref[layer, h], cols)
        span_ref[layer : layer + 1, :] = 1.0 / wide
        span_cols_ref[layer : layer + 1, :] = 1.0 / cols
    slots[0, :TILE, :] = jnp.zeros((TILE, TILE), jnp.float32)
    slots[0, :frags, :SLOTS] = cap_ref[...]
    cols = jnp.transpose(slots[0, :TILE, :])
    for f in range(frags):
        wide = jnp.broadcast_to(cols[:SLOTS, f : f + 1], (SLOTS, TILE))
        for k in range(SLOTS // 8):
            caps[k, f] = wide[k * 8 : (k + 1) * 8]
    energy_ref[...] = jnp.zeros_like(energy_ref)

    ends = {9: 0}
    made = 0
    for size in range(8, 1, -1):
        for k in range(frags):
            live = count_ref[k]
            order_ref[made] = live * 64 + k
            made += jnp.where((live + 7) >> 3 == size, 1, 0)
        ends[size] = made
    n6, n5, n3, n2 = (ends[k] - ends[k + 1] for k in (6, 5, 3, 2))
    with6 = jnp.minimum(n6, n2)
    with5 = jnp.minimum(n5, n2 - with6 + n3)
    runs = [ends[7], ends[7] + with6, ends[6], ends[6] + with5, ends[5]]
    high = frags - 1
    made = 0
    for k in range(frags):
        fits = (
            ((k >= runs[0]) & (k < runs[1]))
            | ((k >= runs[2]) & (k < runs[3]))
            | (k >= runs[4])
        )
        both = fits & (k < high)
        big = order_ref[k]
        small = order_ref[jnp.maximum(high, 0)]
        bins[0, k] = big & 63
        bins[1, k] = small & 63
        bins[2, k] = big >> 6
        bins[3, k] = jnp.where(both, ((big >> 6) + 7) & -8, SLOTS)
        bins[4, k] = jnp.where(both, small >> 6, 0)
        made = jnp.where(k <= high, k + 1, made)
        high = high - jnp.where(both, 1, 0)
    for k in range(2 * GROUP - 1):
        bins[0, made + k] = 0
        bins[1, made + k] = 0
        bins[2, made + k] = 0
        bins[3, made + k] = SLOTS
        bins[4, made + k] = 0

    lane = lax.broadcasted_iota(jnp.int32, (1, QUAD), 1)
    head_mask = [(lane // 32 == h).astype(jnp.bfloat16) for h in range(4)]
    head_pick = [lane // 32 == h for h in range(4)]
    slot_row = lax.broadcasted_iota(jnp.int32, (SLOTS, QUAD), 0)
    slot_lane = lax.broadcasted_iota(jnp.int32, (SLOTS, QUAD), 1) % SLOTS

    def spread_heads(x):
        return jnp.concatenate([x * head_mask[h] for h in range(4)], axis=0)

    def fold_heads(x):
        out = jnp.where(head_pick[0], x[0:SLOTS], 0.0)
        for h in range(1, 4):
            out = jnp.where(head_pick[h], x[h * SLOTS : (h + 1) * SLOTS], out)
        return out

    half = 0.5 / math.sqrt(32.0)
    units = [(f, quad) for f in range(GROUP) for quad in range(2)]

    def rows_of(f):
        return slice(f * SLOTS, (f + 1) * SLOTS)

    def eighths(which):
        big, small, start = (bins[c, which] for c in (0, 1, 3))
        start = start >> 3
        for k in range(SLOTS // 8):
            early = k < start
            yield k, jnp.where(early, big, small), k - jnp.where(early, 0, start)

    def gather(b):
        for f in range(GROUP):
            for k, frag, part in eighths(b * GROUP + f):
                rs = [slot_ref[part, frag, j] for j in range(8)]
                at = f * SLOTS + k * 8
                for j in range(8):
                    for c in range(3):
                        slots[c, at + j : at + j + 1, :] = table[c, pl.ds(rs[j], 1), :]

    def scatter(b):
        for f in range(GROUP):
            for k, frag, part in eighths(b * GROUP + f):
                rs = [slot_ref[part, frag, j] for j in range(8)]
                old = [forces[pl.ds(r, 1), :] for r in rs]
                for j in range(8):
                    at = f * SLOTS + k * 8 + j
                    forces[pl.ds(rs[j], 1), :] = old[j] + slot_force[at : at + 1, :]

    def one_block(b, carry):
        info = [tuple(bins[c, b * GROUP + f] for c in (2, 3, 4)) for f in range(GROUP)]
        h0 = jnp.concatenate([slots[0], slots[1]], axis=1)
        atoms = slots[2]
        gather(b + 1)
        scatter(jnp.maximum(b - 1, 0))

        atom_rows = jnp.transpose(atoms)
        dists, inverses, offsets, weights = [], [], [], []
        for f in range(GROUP):
            first, start, second = info[f]
            col = atoms[rows_of(f), :]
            row = atom_rows[0:8, rows_of(f)]
            row = jnp.concatenate([row, row], axis=1)
            off = [col[:, c : c + 1] - row[c : c + 1, :] for c in range(3)]
            square = off[0] * off[0] + off[1] * off[1] + off[2] * off[2] + PAIR_SOFTEN
            inverse = lax.rsqrt(square)

            def owner(i, dead):
                late = jnp.logical_and(i >= start, i < start + second)
                return jnp.where(i < first, 1, jnp.where(late, 2, dead))

            mine = owner(slot_row, 0)
            dists.append(jnp.where(mine == owner(slot_lane, -1), square * inverse, FAR))
            inverses.append(inverse)
            offsets.append(off)
            cap = jnp.concatenate([caps[part, frag] for _, frag, part in eighths(b * GROUP + f)], axis=0)
            weights.append(jnp.where(mine > 0, cap, 0.0))
        dist2 = [jnp.concatenate([d, d], axis=1) for d in dists]
        weight = jnp.concatenate(weights, axis=0)

        def attention(layer, project):
            def part(f, quad, which):
                at = which * F + quad * QUAD
                return project[rows_of(f), at : at + QUAD]

            qs = [part(f, quad, 0) for f, quad in units]
            kbs = [spread_heads(part(f, quad, 1)) for f, quad in units]
            vbs = [spread_heads(part(f, quad, 2)) for f, quad in units]
            scores = [dot_nt(q, kb) for q, kb in zip(qs, kbs)]
            atts, by_dist, by_score = [], [], []
            for (f, quad), score in zip(units, scores):
                u = score * half
                th = jnp.tanh(u)
                silu = u + u * th
                span = span_ref[layer : layer + 1, quad * 256 : (quad + 1) * 256]
                damp = recip(dist2[f] + span)
                att = silu * damp
                atts.append(bf16(att))
                by_dist.append(att * damp)
                if layer == 1:
                    by_score.append(damp * ((1.0 + th) + (silu - silu * th)))
            span_cols = span_cols_ref[layer : layer + 1, :]
            message = [dot(att, vb) for att, vb in zip(atts, vbs)]
            message = jnp.concatenate(
                [jnp.concatenate(message[2 * f : 2 * f + 2], axis=1) for f in range(GROUP)], axis=0
            )
            return bf16(message * span_cols), (qs, kbs, vbs, atts, by_dist, by_score)

        gain = [gains_ref[i : i + 1, :] for i in range(LAYERS + 1)]
        unit0, _ = norm_parts(h0)
        project0 = bf16(dot(bf16(unit0 * gain[0]), wqkv_ref[0]))
        message0, kept0 = attention(0, project0)
        h1 = h0 + dot(message0, wout_ref[0])
        unit1, scale1 = norm_parts(h1)
        project1 = bf16(dot(bf16(unit1 * gain[1]), wqkv_ref[1]))
        message1, kept1 = attention(1, project1)
        h2 = h1 + dot(message1, wout_ref[1])
        unit2, scale2 = norm_parts(h2)
        u = 0.5 * dot(bf16(unit2 * gain[2]), wread_ref[...])
        th = jnp.tanh(u)
        silu = u + u * th
        weighted = weight * wen_ref[...]
        energy_ref[...] += jnp.sum((weighted * silu).reshape(ROWS // 8, 8, QUAD), axis=0)

        dread = bf16((0.5 * weighted) * ((1.0 + th) + (silu - silu * th)))
        dh2 = norm_back(dot_nt(dread, wread_ref[...]), gain[2], unit2, scale2)
        dmsg1 = bf16(dot_nt(bf16(dh2), wout_ref[1]) * span_cols_ref[1:2, :])
        qs, kbs, vbs, atts, by_dist, by_score = kept1
        dms = [dmsg1[rows_of(f), quad * QUAD : (quad + 1) * QUAD] for f, quad in units]
        datts = [dot_nt(dm, vb) for dm, vb in zip(dms, vbs)]
        dvs = [bf16(fold_heads(dot_tn(att, dm))) for att, dm in zip(atts, dms)]
        dss = [bf16(datt * slope) for datt, slope in zip(datts, by_score)]
        dqs = [bf16(dot(ds, kb) * half) for ds, kb in zip(dss, kbs)]
        dks = [bf16(fold_heads(dot_tn(ds, q)) * half) for ds, q in zip(dss, qs)]
        pulls = [datt * slope for datt, slope in zip(datts, by_dist)]
        dproject = jnp.concatenate(
            [
                jnp.concatenate(
                    [x[2 * f + quad] for x in (dqs, dks, dvs) for quad in range(2)], axis=1
                )
                for f in range(GROUP)
            ],
            axis=0,
        )
        dh1 = dh2 + norm_back(dot_nt(dproject, wqkv_ref[1]), gain[1], unit1, scale1)
        dmsg0 = bf16(dot_nt(bf16(dh1), wout_ref[0]) * span_cols_ref[0:1, :])
        datts = [
            dot_nt(dmsg0[rows_of(f), quad * QUAD : (quad + 1) * QUAD], vb)
            for (f, quad), vb in zip(units, kept0[2])
        ]
        pulls = [old + datt * slope for old, datt, slope in zip(pulls, datts, kept0[4])]
        force_rows = []
        for f in range(GROUP):
            pull = pulls[2 * f] + pulls[2 * f + 1]
            pull = (pull[:, :QUAD] + pull[:, QUAD:]) * inverses[f]
            pull = pull[:, :SLOTS] + pull[:, SLOTS:]
            pull = pull + jnp.transpose(pull)
            for c in range(3):
                force_rows.append(
                    -jnp.sum(pull * offsets[f][c][:, :SLOTS], axis=0, keepdims=True)
                )
        packed = jnp.concatenate(
            [
                jnp.concatenate([force_rows[3 * f + c] for f in range(GROUP)], axis=1)
                for c in range(3)
            ]
            + [jnp.zeros((5, ROWS), jnp.float32)],
            axis=0,
        )
        slot_force[:, 0:8] = jnp.transpose(packed)
        return carry

    gather(0)
    groups = (made + GROUP - 1) // GROUP
    lax.fori_loop(0, groups, one_block, 0)
    scatter(groups - 1)

    pick = (
        lax.broadcasted_iota(jnp.int32, (16, TILE), 0)
        == lax.broadcasted_iota(jnp.int32, (16, TILE), 1)
    ).astype(jnp.bfloat16)
    for i in range(tiles // 8):
        rows = dot_nt(pick, bf16(forces[i * 1024 : (i + 1) * 1024, :]))
        for c in range(3):
            for k in range(8):
                force_ref[i, c, k : k + 1, :] = rows[c : c + 1, k * TILE : (k + 1) * TILE]


def fragment_model(near8, near_features, slot_rows, atom_count, cap_weight, weights):
    w_qkv, w_out, gains, rates, w_read, w_energy = weights
    tiles = near8.shape[0]
    frags = atom_count.shape[0]
    smem = pl.BlockSpec(memory_space=pltpu.SMEM)
    vmem = pl.BlockSpec(memory_space=pltpu.VMEM)
    force, energy = pl.pallas_call(
        fragment_body,
        out_shape=(
            jax.ShapeDtypeStruct((tiles // 8, 3, 8, TILE), jnp.float32),
            jax.ShapeDtypeStruct((8, TILE), jnp.float32),
        ),
        in_specs=[smem, smem, smem] + [vmem] * 8,
        out_specs=(vmem, vmem),
        scratch_shapes=[
            pltpu.VMEM((3, tiles * TILE, TILE), jnp.float32),
            pltpu.VMEM((tiles * TILE, TILE), jnp.float32),
            pltpu.VMEM((3, ROWS, TILE), jnp.float32),
            pltpu.VMEM((ROWS, TILE), jnp.float32),
            pltpu.VMEM((SLOTS // 8, frags, 8, TILE), jnp.float32),
            pltpu.VMEM((LAYERS, HEADS * SLOTS), jnp.float32),
            pltpu.VMEM((LAYERS, F), jnp.float32),
            pltpu.SMEM((frags + 1,), jnp.int32),
            pltpu.SMEM((5, frags + 2 * GROUP), jnp.int32),
        ],
        compiler_params=pltpu.CompilerParams(vmem_limit_bytes=56 * MIB),
        name="fragments",
    )(
        atom_count,
        slot_rows,
        rates,
        near8,
        near_features,
        cap_weight,
        w_qkv,
        w_out,
        gains,
        w_read,
        w_energy.reshape(1, -1),
    )
    return force, energy


def home_body(
    force_ref,
    pair_ref,
    frag_energy_ref,
    pair_energy_ref,
    out_ref,
    energy_ref,
    landing,
    by_sub,
    by_brick,
    force_send,
    force_recv,
    sub_send,
    sub_recv,
    brick_send,
    brick_recv,
):
    bricks, subs = by_brick.shape[0], by_sub.shape[0]
    brick, sub = lax.axis_index("brick"), lax.axis_index("sub")
    mesh_id = pl.DeviceIdType.MESH
    around = [(u, v) for u in (-1, 0, 1) for v in (-1, 0, 1) if (u, v) != (0, 0)]

    def inside(u, v):
        b, s = brick + u, sub + v
        return (b >= 0) & (b < bricks) & (s >= 0) & (s < subs)

    sub_peers = [(brick, lax.rem(sub + d, subs)) for d in range(1, subs)]
    brick_peers = [(lax.rem(brick + d, bricks), sub) for d in range(1, bricks)]

    barrier = pltpu.get_barrier_semaphore()
    for peer in sub_peers + brick_peers:
        pl.semaphore_signal(barrier, inc=1, device_id=peer, device_id_type=mesh_id)
    corners = [(u, v) for u, v in around if u != 0 and v != 0]
    for u, v in corners:

        @pl.when(inside(u, v))
        def _(u=u, v=v):
            pl.semaphore_signal(
                barrier, inc=1, device_id=(brick + u, sub + v), device_id_type=mesh_id
            )

    beside = [
        jnp.where(at > 0, 1, 0) + jnp.where(at < size - 1, 1, 0)
        for at, size in ((brick, bricks), (sub, subs))
    ]
    pl.semaphore_wait(barrier, subs + bricks - 2 + beside[0] * beside[1])

    def energy_copy(store, send, recv, k, slot, peer):
        return pltpu.make_async_remote_copy(
            src_ref=store.at[slot],
            dst_ref=store.at[slot],
            send_sem=send.at[k],
            recv_sem=recv.at[slot],
            device_id=peer,
            device_id_type=mesh_id,
        )

    by_sub[sub] = frag_energy_ref[...] + pair_energy_ref[...]
    for k, peer in enumerate(sub_peers):
        energy_copy(by_sub, sub_send, sub_recv, k, sub, peer).start()

    def force_copy(u, v):
        k = (u + 1) * 3 + v + 1
        return pltpu.make_async_remote_copy(
            src_ref=force_ref.at[k],
            dst_ref=landing.at[k],
            send_sem=force_send.at[k],
            recv_sem=force_recv.at[k],
            device_id=(brick + u, sub + v),
            device_id_type=mesh_id,
        )

    for u, v in around:

        @pl.when(inside(u, v))
        def _(u=u, v=v):
            force_copy(u, v).start()

    for k, peer in enumerate(sub_peers):
        energy_copy(by_sub, sub_send, sub_recv, k, peer[1], peer).wait_recv()
    by_brick[brick] = jnp.sum(by_sub[...], axis=0)
    for k, peer in enumerate(brick_peers):
        energy_copy(by_brick, brick_send, brick_recv, k, brick, peer).start()

    out_ref[...] = force_ref[4] + pair_ref[...]
    for u, v in around:
        @pl.when(inside(-u, -v))
        def _(u=u, v=v):
            force_copy(u, v).wait_recv()
            out_ref[...] += landing[(u + 1) * 3 + v + 1]

    for k, peer in enumerate(brick_peers):
        energy_copy(by_brick, brick_send, brick_recv, k, peer[0], peer).wait_recv()
    energy_ref[0, 0] = jnp.sum(jnp.sum(by_brick[...], axis=0))

    for u, v in around:

        @pl.when(inside(u, v))
        def _(u=u, v=v):
            force_copy(u, v).wait_send()

    for k, peer in enumerate(sub_peers):
        energy_copy(by_sub, sub_send, sub_recv, k, sub, peer).wait_send()
    for k, peer in enumerate(brick_peers):
        energy_copy(by_brick, brick_send, brick_recv, k, brick, peer).wait_send()


def bring_home(row_force, pair_force, frag_energy, pair_energy):
    bricks, subs = lax.axis_size("brick"), lax.axis_size("sub")
    vmem = pl.BlockSpec(memory_space=pltpu.VMEM)
    block = row_force.shape[1:]
    dma = pltpu.SemaphoreType.DMA
    return pl.pallas_call(
        home_body,
        out_shape=(
            jax.ShapeDtypeStruct(block, jnp.float32),
            jax.ShapeDtypeStruct((1, 1), jnp.float32),
        ),
        in_specs=[vmem] * 4,
        out_specs=(vmem, pl.BlockSpec(memory_space=pltpu.SMEM)),
        scratch_shapes=[
            pltpu.VMEM((9,) + block, jnp.float32),
            pltpu.VMEM((subs, 8, TILE), jnp.float32),
            pltpu.VMEM((bricks, 8, TILE), jnp.float32),
            dma((9,)),
            dma((9,)),
            dma((subs,)),
            dma((subs,)),
            dma((bricks,)),
            dma((bricks,)),
        ],
        compiler_params=pltpu.CompilerParams(
            collective_id=1, has_side_effects=True, vmem_limit_bytes=56 * MIB
        ),
        name="bring_home",
    )(row_force, pair_force, frag_energy, pair_energy)


AROUND = [(u, v) for u in (-1, 0, 1) for v in (-1, 0, 1) if (u, v) != (0, 0)]
CHUNKS = 4


STEP_PAIRS = 16


def three_parts(x):
    a = bf16(x).astype(jnp.float32)
    b = bf16(x - a).astype(jnp.float32)
    return [a, b, x - a - b, jnp.zeros_like(x)]


def block_of(u, v):
    return (u + 1) * 3 + v + 1


def halo_body(
    pairs_ref,
    count_ref,
    pos_ref,
    charge_ref,
    own_list_ref,
    slot_ref,
    feat_ref,
    near_ref,
    near_feat_ref,
    pair_force_ref,
    pair_energy_ref,
    rows_ref,
    parts,
    cols_a,
    cols_b,
    atom_send,
    atom_recv,
    side_send,
    side_recv,
    ahead_send,
    ahead_recv,
    corner_send,
    corner_recv,
    local_sem,
):
    bricks, subs = lax.axis_size("brick"), lax.axis_size("sub")
    brick, sub = lax.axis_index("brick"), lax.axis_index("sub")
    mesh_id = pl.DeviceIdType.MESH
    rows = feat_ref.shape[0]
    tiles = charge_ref.shape[0]
    part = rows // CHUNKS
    centre = block_of(0, 0) * tiles

    for k in range(SLOTS // 8):
        rows_ref[k] = slot_ref[:, k * 8 : (k + 1) * 8]
    near_ref[pl.ds(centre, tiles)] = jnp.zeros((tiles, 8, TILE), jnp.float32)
    for t in range(tiles):
        for c in range(3):
            near_ref[centre + t, c : c + 1, :] = pos_ref[c, t : t + 1, :]
        near_ref[centre + t, 3:4, :] = charge_ref[t : t + 1, :]

    def inside(u, v):
        b, s = brick + u, sub + v
        return (b >= 0) & (b < bricks) & (s >= 0) & (s < subs)

    barrier = pltpu.get_barrier_semaphore()
    for u, v in AROUND:

        @pl.when(inside(u, v))
        def _(u=u, v=v):
            pl.semaphore_signal(
                barrier, inc=1, device_id=(brick + u, sub + v), device_id_type=mesh_id
            )

    beside = [
        jnp.where(at > 0, 1, 0) + jnp.where(at < size - 1, 1, 0)
        for at, size in ((brick, bricks), (sub, subs))
    ]
    pl.semaphore_wait(barrier, beside[0] + beside[1] + beside[0] * beside[1])

    def atom_copy(u, v):
        k = block_of(-u, -v)
        return pltpu.make_async_remote_copy(
            src_ref=near_ref.at[pl.ds(centre, tiles)],
            dst_ref=near_ref.at[pl.ds(k * tiles, tiles)],
            send_sem=atom_send.at[k],
            recv_sem=atom_recv.at[k],
            device_id=(brick + u, sub + v),
            device_id_type=mesh_id,
        )

    def ahead_copy(u, c):
        i = (u + 1) // 2
        return pltpu.make_async_remote_copy(
            src_ref=feat_ref.at[pl.ds(c * part, part)],
            dst_ref=near_feat_ref.at[block_of(-u, 0), pl.ds(c * part, part)],
            send_sem=ahead_send.at[i, c],
            recv_sem=ahead_recv.at[i, c],
            device_id=(brick + u, sub),
            device_id_type=mesh_id,
        )

    def side_copy(v):
        i = (v + 1) // 2
        return pltpu.make_async_remote_copy(
            src_ref=feat_ref,
            dst_ref=near_feat_ref.at[block_of(0, -v)],
            send_sem=side_send.at[i],
            recv_sem=side_recv.at[i],
            device_id=(brick, sub + v),
            device_id_type=mesh_id,
        )

    def corner_copy(w, v, c):
        i = (w + 1) + (v + 1) // 2
        at = pl.ds(c * part, part)
        return pltpu.make_async_remote_copy(
            src_ref=near_feat_ref.at[block_of(w, 0), at],
            dst_ref=near_feat_ref.at[block_of(w, -v), at],
            send_sem=corner_send.at[i, c],
            recv_sem=corner_recv.at[i, c],
            device_id=(brick, sub + v),
            device_id_type=mesh_id,
        )

    for u, v in AROUND:

        @pl.when(inside(u, v))
        def _(u=u, v=v):
            atom_copy(u, v).start()

    for c in range(CHUNKS):
        for u in (-1, 1):

            @pl.when(inside(u, 0))
            def _(u=u, c=c):
                ahead_copy(u, c).start()

        if c == 0:
            for v in (-1, 1):

                @pl.when(inside(0, v))
                def _(v=v):
                    side_copy(v).start()

    local = pltpu.make_async_copy(feat_ref, near_feat_ref.at[block_of(0, 0)], local_sem)
    local.start()
    for u, v in AROUND:
        k = block_of(u, v)

        @pl.when(jnp.logical_not(inside(u, v)))
        def _(k=k):
            near_ref[pl.ds(k * tiles, tiles)] = jnp.zeros((tiles, 8, TILE), jnp.float32)

    def forward(c):
        for w in (-1, 1):

            @pl.when(inside(w, 0))
            def _(w=w):
                ahead_copy(-w, c).wait_recv()
                for v in (-1, 1):

                    @pl.when(inside(0, v))
                    def _(w=w, v=v):
                        corner_copy(w, v, c).start()

    for u, v in AROUND:

        @pl.when(inside(-u, -v))
        def _(u=u, v=v):
            atom_copy(u, v).wait_recv()

    spread = (
        lax.broadcasted_iota(jnp.int32, (32, 4 * TILE), 0) % 8
        == lax.broadcasted_iota(jnp.int32, (32, 4 * TILE), 1) // TILE
    ).astype(jnp.bfloat16)
    chunk = 32
    rel = lax.broadcasted_iota(jnp.int32, (chunk, TILE), 1) - lax.broadcasted_iota(
        jnp.int32, (chunk, TILE), 0
    )

    def spread_near(cols, first):
        for k in range(4):
            near = pairs_ref[1, jnp.minimum(first + k, pairs - 1)]
            cols[k] = dot_tn(bf16(jnp.concatenate(three_parts(near_ref[near]), axis=0)), spread)

    def one_pair(p, cols, k):
        own = pairs_ref[0, p]
        near = pairs_ref[1, p]
        o = near_ref[centre + own]
        xi, yi, zi, qi = (o[c : c + 1, :] for c in range(4))
        same = jnp.where(near == own + centre, 0, 4 * TILE)
        sums = [jnp.zeros((8, TILE), jnp.float32) for _ in range(4)]
        for start in range(0, TILE, chunk):
            xj, yj, zj, qj = (
                cols[k, start : start + chunk, c * TILE : (c + 1) * TILE] for c in range(4)
            )
            dx, dy, dz = xi - xj, yi - yj, zi - zj
            qq = jnp.where(rel == same + start, 0.0, qi * qj)
            square = dx * dx + dy * dy + dz * dz + CHARGE_SOFTEN
            square = jnp.minimum(square, 1e6)
            rinv = lax.rsqrt(square)
            t = recip(1.0 + (ERFC_P * SCREEN_RATE) * (square * rinv))
            g = ERFC_C[-1]
            for coef in ERFC_C[-2::-1]:
                g = g * t + coef
            gauss = qq * jnp.exp2((-SCREEN_RATE * SCREEN_RATE * math.log2(math.e)) * square)
            screened = (g * t) * rinv
            w = (gauss * (screened + GAUSS)) * (rinv * rinv)
            for c, term in enumerate((w * dx, w * dy, w * dz, gauss * screened)):
                sums[c] += jnp.sum(term.reshape(chunk // 8, 8, TILE), axis=0)
        for c in range(4):
            parts[c, pl.ds(p, 1), :] = jnp.sum(sums[c], axis=0, keepdims=True)

    def eight_pairs(i, carry):
        p = 8 * i
        spread_near(cols_b, p + 4)
        for k in range(4):
            one_pair(p + k, cols_a, k)
        spread_near(cols_a, p + 8)
        for k in range(4):
            one_pair(p + 4 + k, cols_b, k)
        return carry

    pairs = own_list_ref.shape[1]
    spread_near(cols_a, 0)
    done = 0
    for c in range(CHUNKS):
        forward(c)
        upto = (c + 1) * STEP_PAIRS if c < CHUNKS - 1 else pairs
        lax.fori_loop(done // 8, upto // 8, eight_pairs, 0)
        done = upto

    pick = (
        (own_list_ref[0:1, :] == lax.broadcasted_iota(jnp.int32, (16, pairs), 0))
        & (lax.broadcasted_iota(jnp.int32, (16, pairs), 1) < count_ref[0, 0])
    ).astype(jnp.bfloat16)
    for k in range(4):
        whole = sum(dot(pick, bf16(x)) for x in three_parts(parts[k])[:3])[:tiles]
        if k < 3:
            pair_force_ref[k] = COULOMB_UNIT * whole
        else:
            pair_energy_ref[...] = (0.5 * COULOMB_UNIT) * whole

    for v in (-1, 1):

        @pl.when(inside(0, -v))
        def _(v=v):
            side_copy(v).wait_recv()

    for w in (-1, 1):
        for v in (-1, 1):

            @pl.when(inside(w, -v))
            def _(w=w, v=v):
                for c in range(CHUNKS):
                    corner_copy(w, v, c).wait_recv()

    local.wait()
    for u, v in AROUND:

        @pl.when(inside(u, v))
        def _(u=u, v=v):
            atom_copy(u, v).wait_send()

    for u in (-1, 1):

        @pl.when(inside(u, 0))
        def _(u=u):
            for c in range(CHUNKS):
                ahead_copy(u, c).wait_send()

    for v in (-1, 1):

        @pl.when(inside(0, v))
        def _(v=v):
            side_copy(v).wait_send()

    for w in (-1, 1):
        for v in (-1, 1):

            @pl.when(inside(w, v))
            def _(w=w, v=v):
                for c in range(CHUNKS):
                    corner_copy(w, v, c).wait_send()


def halo(positions, charges, features, pairs, count, slot_index):
    tiles = charges.shape[0]
    smem = pl.BlockSpec(memory_space=pltpu.SMEM)
    vmem = pl.BlockSpec(memory_space=pltpu.VMEM)
    hbm = pl.BlockSpec(memory_space=pl.ANY)
    dma = pltpu.SemaphoreType.DMA
    return pl.pallas_call(
        halo_body,
        out_shape=(
            jax.ShapeDtypeStruct((9 * tiles, 8, TILE), jnp.float32),
            jax.ShapeDtypeStruct((9,) + features.shape, features.dtype),
            jax.ShapeDtypeStruct((3, tiles, TILE), jnp.float32),
            jax.ShapeDtypeStruct((tiles, TILE), jnp.float32),
            jax.ShapeDtypeStruct((SLOTS // 8, slot_index.shape[0], 8), jnp.int32),
        ),
        in_specs=[smem, smem, vmem, vmem, vmem, vmem, hbm],
        out_specs=(vmem, hbm, vmem, vmem, vmem),
        scratch_shapes=[
            pltpu.VMEM((4, pairs.shape[1], TILE), jnp.float32),
            pltpu.VMEM((4, TILE, 4 * TILE), jnp.float32),
            pltpu.VMEM((4, TILE, 4 * TILE), jnp.float32),
            dma((9,)),
            dma((9,)),
            dma((2,)),
            dma((2,)),
            dma((2, CHUNKS)),
            dma((2, CHUNKS)),
            dma((4, CHUNKS)),
            dma((4, CHUNKS)),
            dma(()),
        ],
        compiler_params=pltpu.CompilerParams(
            collective_id=2, has_side_effects=True, vmem_limit_bytes=56 * MIB
        ),
        name="halo",
    )(pairs, count, positions, charges, pairs, slot_index, features)


def body(
    atom_features,
    positions,
    charges,
    slot_index,
    atom_count,
    cap_weight,
    tile_pairs,
    tile_count,
    w_qkv,
    w_out,
    gains,
    rates,
    w_read,
    w_energy,
):
    own_size = atom_features.shape[2]
    own_tiles = own_size // TILE
    near8, near_features, pair_force, pair_energy, slot_rows = halo(
        positions.reshape(3, own_tiles, TILE),
        charges.reshape(own_tiles, TILE),
        atom_features.reshape(own_size, -1),
        tile_pairs.reshape(2, -1),
        tile_count,
        slot_index,
    )
    row_force, frag_energy = fragment_model(
        near8,
        near_features,
        slot_rows,
        atom_count,
        cap_weight,
        (w_qkv, w_out, gains, rates, w_read, w_energy),
    )
    forces, energy = bring_home(row_force, pair_force, frag_energy, pair_energy)
    return forces.reshape(3, 1, 1, own_size), energy.reshape(())


def solution(mesh):
    in_specs = (
        P("brick", "sub", None, None),
        P(None, "brick", "sub", None),
        P("brick", "sub", None),
        P(("brick", "sub"), None),
        P(("brick", "sub")),
        P(("brick", "sub"), None),
        P(None, "brick", "sub", None),
        P("brick", "sub"),
        P(),
        P(),
        P(),
        P(),
        P(),
        P(),
    )
    out_specs = (P(None, "brick", "sub", None), P())
    return jax.shard_map(body, mesh=mesh, in_specs=in_specs, out_specs=out_specs, check_vma=False)
```

```python
import math

import jax
import jax.numpy as jnp
from jax import lax
from jax.experimental import pallas as pl
from jax.experimental.pallas import tpu as pltpu
from jax.sharding import PartitionSpec as P

F = 256
HEADS = 8
LAYERS = 2
SLOTS = 64
TILE = 128
GROUP = 8
ROWS = GROUP * SLOTS
QUAD = 128

NORM_EPS = 1e-05
PAIR_SOFTEN = 0.01
SCREEN_RATE = 0.1
COULOMB_UNIT = 14.4
CHARGE_SOFTEN = 1.0
FAR = 1e30
GAUSS = 2.0 * SCREEN_RATE / math.sqrt(math.pi)
ERFC_P = 0.6
ERFC_C = (
    0.33858295223558404,
    0.33681896467541816,
    0.2948193558779553,
    0.06093701313639673,
    0.3109940554359323,
    -0.6781244471753995,
    0.4339317702022656,
    -0.0979638654555287,
)
MIB = 1024 * 1024


def dot(a, b):
    return lax.dot_general(a, b, (((1,), (0,)), ((), ())), preferred_element_type=jnp.float32)


def dot_nt(a, b):
    return lax.dot_general(a, b, (((1,), (1,)), ((), ())), preferred_element_type=jnp.float32)


def dot_tn(a, b):
    return lax.dot_general(a, b, (((0,), (0,)), ((), ())), preferred_element_type=jnp.float32)


def recip(x):
    return pl.reciprocal(x, approx=True)


def norm_parts(hidden):
    centre = jnp.mean(hidden, axis=-1, keepdims=True)
    shifted = hidden - centre
    spread = jnp.mean(shifted * shifted, axis=-1, keepdims=True)
    scale = lax.rsqrt(spread + NORM_EPS)
    return shifted * scale, scale


def norm_back(grad, gain, unit, scale):
    g = grad * gain
    mean_g = jnp.mean(g, axis=-1, keepdims=True)
    mean_gu = jnp.mean(g * unit, axis=-1, keepdims=True)
    return scale * (g - mean_g - unit * mean_gu)


def bf16(x):
    return x.astype(jnp.bfloat16)


def fragment_body(
    count_ref,
    slot_ref,
    rate_ref,
    near_ref,
    feat_ref,
    cap_ref,
    wqkv_ref,
    wout_ref,
    gains_ref,
    wread_ref,
    wen_ref,
    force_ref,
    energy_ref,
    table,
    forces,
    slots,
    slot_force,
    caps,
    span_ref,
    span_cols_ref,
    order_ref,
    tally,
    bins,
    landed,
    landed_sem,
):
    tiles = near_ref.shape[0]
    frags = cap_ref.shape[0]

    def eighth_of(f):
        return (f % (frags // 2)) * (2 * SLOTS // 8) + f // (frags // 2) * (SLOTS // 8)


    def feature_copy(i):
        return pltpu.make_async_copy(feat_ref.at[i], landed.at[i], landed_sem.at[i])

    for i in range(tiles // 8):
        feature_copy(i).start()

    def widen(i, carry):
        feature_copy(i).wait()
        for k in range(8):
            at = pl.multiple_of(i * 8 * TILE + k * TILE, TILE)
            both = landed[i, k * TILE : (k + 1) * TILE, :].astype(jnp.float32)
            table[0, pl.ds(at, TILE), :] = both[:, :QUAD]
            table[1, pl.ds(at, TILE), :] = both[:, QUAD:]
            n = jnp.transpose(near_ref[i * 8 + k])
            table[2, pl.ds(at, TILE), :] = jnp.concatenate(
                [n, jnp.zeros((TILE, TILE - 8), jnp.float32)], axis=1
            )
            forces[pl.ds(at, TILE), :] = jnp.zeros((TILE, TILE), jnp.float32)
        return carry

    slot_force[...] = jnp.zeros_like(slot_force)
    head = lax.broadcasted_iota(jnp.int32, (1, HEADS * SLOTS), 1) // SLOTS
    head_col = lax.broadcasted_iota(jnp.int32, (1, F), 1) // (F // HEADS)
    for layer in range(LAYERS):
        wide = jnp.ones((1, HEADS * SLOTS), jnp.float32)
        cols = jnp.ones((1, F), jnp.float32)
        for h in range(HEADS):
            wide = jnp.where(head == h, rate_ref[layer, h], wide)
            cols = jnp.where(head_col == h, rate_ref[layer, h], cols)
        span_ref[layer : layer + 1, :] = 1.0 / wide
        span_cols_ref[layer : layer + 1, :] = 1.0 / cols
    slots[0, :TILE, :] = jnp.zeros((TILE, TILE), jnp.float32)
    slots[0, :frags, :SLOTS] = cap_ref[...]
    cols = jnp.transpose(slots[0, :TILE, :])
    for f in range(frags):
        wide = jnp.broadcast_to(cols[:SLOTS, f : f + 1], (SLOTS, TILE))
        for k in range(SLOTS // 8):
            caps[eighth_of(f) + k] = wide[k * 8 : (k + 1) * 8]
    energy_ref[...] = jnp.zeros_like(energy_ref)

    for size in range(16):
        tally[size] = 0
    for k in range(frags):
        size = (count_ref[k] + 7) >> 3
        tally[size] = tally[size] + 1
    ends = {9: 0}
    for size in range(8, 1, -1):
        ends[size] = ends[size + 1] + tally[size]
        tally[size] = ends[size + 1]
    for k in range(frags):
        live = count_ref[k]
        size = (live + 7) >> 3
        at = tally[size]
        order_ref[at] = live * 512 + eighth_of(k)
        tally[size] = at + 1
    n6, n5, n3, n2 = (ends[k] - ends[k + 1] for k in (6, 5, 3, 2))
    with6 = jnp.minimum(n6, n2)
    with5 = jnp.minimum(n5, n2 - with6 + n3)
    runs = [ends[7], ends[7] + with6, ends[6], ends[6] + with5, ends[5]]
    high = frags - 1
    made = 0
    for k in range(frags):
        fits = (
            ((k >= runs[0]) & (k < runs[1]))
            | ((k >= runs[2]) & (k < runs[3]))
            | (k >= runs[4])
        )
        both = fits & (k < high)
        big = order_ref[k]
        small = order_ref[jnp.maximum(high, 0)]
        bins[0, k] = big & 511
        bins[1, k] = small & 511
        bins[2, k] = big >> 9
        bins[3, k] = jnp.where(both, ((big >> 9) + 7) & -8, SLOTS)
        bins[4, k] = jnp.where(both, small >> 9, 0)
        made = jnp.where(k <= high, k + 1, made)
        high = high - jnp.where(both, 1, 0)
    for k in range(2 * GROUP - 1):
        bins[0, made + k] = 0
        bins[1, made + k] = 0
        bins[2, made + k] = 0
        bins[3, made + k] = SLOTS
        bins[4, made + k] = 0

    lane = lax.broadcasted_iota(jnp.int32, (1, QUAD), 1)
    head_mask = [(lane // 32 == h).astype(jnp.bfloat16) for h in range(4)]
    head_pick = [lane // 32 == h for h in range(4)]
    slot_row = lax.broadcasted_iota(jnp.int32, (SLOTS, QUAD), 0)
    slot_lane = lax.broadcasted_iota(jnp.int32, (SLOTS, QUAD), 1) % SLOTS

    def spread_heads(x):
        return jnp.concatenate([x * head_mask[h] for h in range(4)], axis=0)

    def fold_heads(x):
        out = jnp.where(head_pick[0], x[0:SLOTS], 0.0)
        for h in range(1, 4):
            out = jnp.where(head_pick[h], x[h * SLOTS : (h + 1) * SLOTS], out)
        return out

    half = 0.5 / math.sqrt(32.0)
    units = [(f, quad) for f in range(GROUP) for quad in range(2)]

    def rows_of(f):
        return slice(f * SLOTS, (f + 1) * SLOTS)

    def eighths(which):
        big, small, start = (bins[c, which] for c in (0, 1, 3))
        start = start >> 3
        for k in range(SLOTS // 8):
            yield k, jnp.where(k < start, big, small - start) + k

    def gather(b):
        for f in range(GROUP):
            for k, part in eighths(b * GROUP + f):
                rs = [slot_ref[part * 8 + j] for j in range(8)]
                at = f * SLOTS + k * 8
                for j in range(8):
                    for c in range(3):
                        slots[c, at + j : at + j + 1, :] = table[c, pl.ds(rs[j], 1), :]

    def scatter(b):
        for f in range(GROUP):
            for k, part in eighths(b * GROUP + f):
                rs = [slot_ref[part * 8 + j] for j in range(8)]
                old = [forces[pl.ds(r, 1), :] for r in rs]
                for j in range(8):
                    at = f * SLOTS + k * 8 + j
                    forces[pl.ds(rs[j], 1), :] = old[j] + slot_force[at : at + 1, :]

    def one_block(b, carry):
        info = [tuple(bins[c, b * GROUP + f] for c in (2, 3, 4)) for f in range(GROUP)]
        h0 = jnp.concatenate([slots[0], slots[1]], axis=1)
        atoms = slots[2]
        gather(b + 1)
        scatter(jnp.maximum(b - 1, 0))

        atom_rows = jnp.transpose(atoms)
        dists, inverses, offsets, weights = [], [], [], []
        for f in range(GROUP):
            first, start, second = info[f]
            col = atoms[rows_of(f), :]
            row = atom_rows[0:8, rows_of(f)]
            row = jnp.concatenate([row, row], axis=1)
            off = [col[:, c : c + 1] - row[c : c + 1, :] for c in range(3)]
            square = off[0] * off[0] + off[1] * off[1] + off[2] * off[2] + PAIR_SOFTEN
            inverse = lax.rsqrt(square)

            def owner(i, dead):
                late = jnp.logical_and(i >= start, i < start + second)
                return jnp.where(i < first, 1, jnp.where(late, 2, dead))

            mine = owner(slot_row, 0)
            dists.append(jnp.where(mine == owner(slot_lane, -1), square * inverse, FAR))
            inverses.append(inverse)
            offsets.append(off)
            cap = jnp.concatenate([caps[part] for _, part in eighths(b * GROUP + f)], axis=0)
            weights.append(jnp.where(mine > 0, cap, 0.0))
        dist2 = [jnp.concatenate([d, d], axis=1) for d in dists]
        weight = jnp.concatenate(weights, axis=0)

        def attention(layer, project):
            def part(f, quad, which):
                at = which * F + quad * QUAD
                return project[rows_of(f), at : at + QUAD]

            qs = [part(f, quad, 0) for f, quad in units]
            kbs = [spread_heads(part(f, quad, 1)) for f, quad in units]
            vbs = [spread_heads(part(f, quad, 2)) for f, quad in units]
            scores = [dot_nt(q, kb) for q, kb in zip(qs, kbs)]
            atts, by_dist, by_score = [], [], []
            for (f, quad), score in zip(units, scores):
                u = score * half
                th = jnp.tanh(u)
                silu = u + u * th
                span = span_ref[layer : layer + 1, quad * 256 : (quad + 1) * 256]
                damp = recip(dist2[f] + span)
                att = silu * damp
                atts.append(bf16(att))
                by_dist.append(att * damp)
                if layer == 1:
                    by_score.append(damp * ((1.0 + th) + (silu - silu * th)))
            span_cols = span_cols_ref[layer : layer + 1, :]
            message = [dot(att, vb) for att, vb in zip(atts, vbs)]
            message = jnp.concatenate(
                [jnp.concatenate(message[2 * f : 2 * f + 2], axis=1) for f in range(GROUP)], axis=0
            )
            return bf16(message * span_cols), (qs, kbs, vbs, atts, by_dist, by_score)

        gain = [gains_ref[i : i + 1, :] for i in range(LAYERS + 1)]
        unit0, _ = norm_parts(h0)
        project0 = bf16(dot(bf16(unit0 * gain[0]), wqkv_ref[0]))
        message0, kept0 = attention(0, project0)
        h1 = h0 + dot(message0, wout_ref[0])
        unit1, scale1 = norm_parts(h1)
        project1 = bf16(dot(bf16(unit1 * gain[1]), wqkv_ref[1]))
        message1, kept1 = attention(1, project1)
        h2 = h1 + dot(message1, wout_ref[1])
        unit2, scale2 = norm_parts(h2)
        u = 0.5 * dot(bf16(unit2 * gain[2]), wread_ref[...])
        th = jnp.tanh(u)
        silu = u + u * th
        weighted = weight * wen_ref[...]
        energy_ref[...] += jnp.sum((weighted * silu).reshape(ROWS // 8, 8, QUAD), axis=0)

        dread = bf16((0.5 * weighted) * ((1.0 + th) + (silu - silu * th)))
        dh2 = norm_back(dot_nt(dread, wread_ref[...]), gain[2], unit2, scale2)
        dmsg1 = bf16(dot_nt(bf16(dh2), wout_ref[1]) * span_cols_ref[1:2, :])
        qs, kbs, vbs, atts, by_dist, by_score = kept1
        dms = [dmsg1[rows_of(f), quad * QUAD : (quad + 1) * QUAD] for f, quad in units]
        datts = [dot_nt(dm, vb) for dm, vb in zip(dms, vbs)]
        dvs = [bf16(fold_heads(dot_tn(att, dm))) for att, dm in zip(atts, dms)]
        dss = [bf16(datt * slope) for datt, slope in zip(datts, by_score)]
        dqs = [bf16(dot(ds, kb) * half) for ds, kb in zip(dss, kbs)]
        dks = [bf16(fold_heads(dot_tn(ds, q)) * half) for ds, q in zip(dss, qs)]
        pulls = [datt * slope for datt, slope in zip(datts, by_dist)]
        dproject = jnp.concatenate(
            [
                jnp.concatenate(
                    [x[2 * f + quad] for x in (dqs, dks, dvs) for quad in range(2)], axis=1
                )
                for f in range(GROUP)
            ],
            axis=0,
        )
        dh1 = dh2 + norm_back(dot_nt(dproject, wqkv_ref[1]), gain[1], unit1, scale1)
        dmsg0 = bf16(dot_nt(bf16(dh1), wout_ref[0]) * span_cols_ref[0:1, :])
        datts = [
            dot_nt(dmsg0[rows_of(f), quad * QUAD : (quad + 1) * QUAD], vb)
            for (f, quad), vb in zip(units, kept0[2])
        ]
        pulls = [old + datt * slope for old, datt, slope in zip(pulls, datts, kept0[4])]
        force_rows = []
        for f in range(GROUP):
            pull = pulls[2 * f] + pulls[2 * f + 1]
            pull = (pull[:, :QUAD] + pull[:, QUAD:]) * inverses[f]
            pull = pull[:, :SLOTS] + pull[:, SLOTS:]
            pull = pull + jnp.transpose(pull)
            for c in range(3):
                force_rows.append(
                    -jnp.sum(pull * offsets[f][c][:, :SLOTS], axis=0, keepdims=True)
                )
        packed = jnp.concatenate(
            [
                jnp.concatenate([force_rows[3 * f + c] for f in range(GROUP)], axis=1)
                for c in range(3)
            ]
            + [jnp.zeros((5, ROWS), jnp.float32)],
            axis=0,
        )
        slot_force[:, 0:8] = jnp.transpose(packed)
        return carry

    lax.fori_loop(0, tiles // 8, widen, 0)
    gather(0)
    groups = (made + GROUP - 1) // GROUP
    lax.fori_loop(0, groups, one_block, 0)
    scatter(groups - 1)

    pick = (
        lax.broadcasted_iota(jnp.int32, (16, TILE), 0)
        == lax.broadcasted_iota(jnp.int32, (16, TILE), 1)
    ).astype(jnp.bfloat16)
    for i in range(tiles // 8):
        rows = dot_nt(pick, bf16(forces[i * 1024 : (i + 1) * 1024, :]))
        for c in range(3):
            for k in range(8):
                force_ref[i, c, k : k + 1, :] = rows[c : c + 1, k * TILE : (k + 1) * TILE]


def fragment_model(near8, near_features, slot_rows, atom_count, cap_weight, weights):
    w_qkv, w_out, gains, rates, w_read, w_energy = weights
    tiles = near8.shape[0]
    frags = atom_count.shape[0]
    smem = pl.BlockSpec(memory_space=pltpu.SMEM)
    vmem = pl.BlockSpec(memory_space=pltpu.VMEM)
    force, energy = pl.pallas_call(
        fragment_body,
        out_shape=(
            jax.ShapeDtypeStruct((tiles // 8, 3, 8, TILE), jnp.float32),
            jax.ShapeDtypeStruct((8, TILE), jnp.float32),
        ),
        in_specs=[smem, smem, smem, vmem, pl.BlockSpec(memory_space=pl.ANY)] + [vmem] * 6,
        out_specs=(vmem, vmem),
        scratch_shapes=[
            pltpu.VMEM((3, tiles * TILE, TILE), jnp.float32),
            pltpu.VMEM((tiles * TILE, TILE), jnp.float32),
            pltpu.VMEM((3, ROWS, TILE), jnp.float32),
            pltpu.VMEM((ROWS, TILE), jnp.float32),
            pltpu.VMEM((SLOTS // 8 * frags, 8, TILE), jnp.float32),
            pltpu.VMEM((LAYERS, HEADS * SLOTS), jnp.float32),
            pltpu.VMEM((LAYERS, F), jnp.float32),
            pltpu.SMEM((frags,), jnp.int32),
            pltpu.SMEM((16,), jnp.int32),
            pltpu.SMEM((5, frags + 2 * GROUP), jnp.int32),
            pltpu.VMEM(near_features.shape, near_features.dtype),
            pltpu.SemaphoreType.DMA((tiles // 8,)),
        ],
        compiler_params=pltpu.CompilerParams(vmem_limit_bytes=56 * MIB),
        name="fragments",
    )(
        atom_count,
        slot_rows.reshape(-1),
        rates,
        near8,
        near_features,
        cap_weight,
        w_qkv,
        w_out,
        gains,
        w_read,
        w_energy.reshape(1, -1),
    )
    return force, energy


def home_body(
    force_ref,
    pair_ref,
    frag_energy_ref,
    pair_energy_ref,
    out_ref,
    energy_ref,
    landing,
    by_sub,
    by_brick,
    force_send,
    force_recv,
    sub_send,
    sub_recv,
    brick_send,
    brick_recv,
):
    bricks, subs = by_brick.shape[0], by_sub.shape[0]
    brick, sub = lax.axis_index("brick"), lax.axis_index("sub")
    mesh_id = pl.DeviceIdType.MESH
    around = [(u, v) for u in (-1, 0, 1) for v in (-1, 0, 1) if (u, v) != (0, 0)]

    def inside(u, v):
        b, s = brick + u, sub + v
        return (b >= 0) & (b < bricks) & (s >= 0) & (s < subs)

    sub_peers = [(brick, lax.rem(sub + d, subs)) for d in range(1, subs)]
    brick_peers = [(lax.rem(brick + d, bricks), sub) for d in range(1, bricks)]

    barrier = pltpu.get_barrier_semaphore()
    for peer in sub_peers + brick_peers:
        pl.semaphore_signal(barrier, inc=1, device_id=peer, device_id_type=mesh_id)
    corners = [(u, v) for u, v in around if u != 0 and v != 0]
    for u, v in corners:

        @pl.when(inside(u, v))
        def _(u=u, v=v):
            pl.semaphore_signal(
                barrier, inc=1, device_id=(brick + u, sub + v), device_id_type=mesh_id
            )

    beside = [
        jnp.where(at > 0, 1, 0) + jnp.where(at < size - 1, 1, 0)
        for at, size in ((brick, bricks), (sub, subs))
    ]
    pl.semaphore_wait(barrier, subs + bricks - 2 + beside[0] * beside[1])

    def energy_copy(store, send, recv, k, slot, peer):
        return pltpu.make_async_remote_copy(
            src_ref=store.at[slot],
            dst_ref=store.at[slot],
            send_sem=send.at[k],
            recv_sem=recv.at[slot],
            device_id=peer,
            device_id_type=mesh_id,
        )

    by_sub[sub] = frag_energy_ref[...] + pair_energy_ref[...]
    for k, peer in enumerate(sub_peers):
        energy_copy(by_sub, sub_send, sub_recv, k, sub, peer).start()

    def force_copy(u, v):
        k = (u + 1) * 3 + v + 1
        return pltpu.make_async_remote_copy(
            src_ref=force_ref.at[k],
            dst_ref=landing.at[k],
            send_sem=force_send.at[k],
            recv_sem=force_recv.at[k],
            device_id=(brick + u, sub + v),
            device_id_type=mesh_id,
        )

    for u, v in around:

        @pl.when(inside(u, v))
        def _(u=u, v=v):
            force_copy(u, v).start()

    for k, peer in enumerate(sub_peers):
        energy_copy(by_sub, sub_send, sub_recv, k, peer[1], peer).wait_recv()
    by_brick[brick] = jnp.sum(by_sub[...], axis=0)
    for k, peer in enumerate(brick_peers):
        energy_copy(by_brick, brick_send, brick_recv, k, brick, peer).start()

    out_ref[...] = force_ref[4] + pair_ref[...]
    for u, v in around:
        @pl.when(inside(-u, -v))
        def _(u=u, v=v):
            force_copy(u, v).wait_recv()
            out_ref[...] += landing[(u + 1) * 3 + v + 1]

    for k, peer in enumerate(brick_peers):
        energy_copy(by_brick, brick_send, brick_recv, k, peer[0], peer).wait_recv()
    energy_ref[0, 0] = jnp.sum(jnp.sum(by_brick[...], axis=0))

    for u, v in around:

        @pl.when(inside(u, v))
        def _(u=u, v=v):
            force_copy(u, v).wait_send()

    for k, peer in enumerate(sub_peers):
        energy_copy(by_sub, sub_send, sub_recv, k, sub, peer).wait_send()
    for k, peer in enumerate(brick_peers):
        energy_copy(by_brick, brick_send, brick_recv, k, brick, peer).wait_send()


def bring_home(row_force, pair_force, frag_energy, pair_energy):
    bricks, subs = lax.axis_size("brick"), lax.axis_size("sub")
    vmem = pl.BlockSpec(memory_space=pltpu.VMEM)
    block = row_force.shape[1:]
    dma = pltpu.SemaphoreType.DMA
    return pl.pallas_call(
        home_body,
        out_shape=(
            jax.ShapeDtypeStruct(block, jnp.float32),
            jax.ShapeDtypeStruct((1, 1), jnp.float32),
        ),
        in_specs=[vmem] * 4,
        out_specs=(vmem, pl.BlockSpec(memory_space=pltpu.SMEM)),
        scratch_shapes=[
            pltpu.VMEM((9,) + block, jnp.float32),
            pltpu.VMEM((subs, 8, TILE), jnp.float32),
            pltpu.VMEM((bricks, 8, TILE), jnp.float32),
            dma((9,)),
            dma((9,)),
            dma((subs,)),
            dma((subs,)),
            dma((bricks,)),
            dma((bricks,)),
        ],
        compiler_params=pltpu.CompilerParams(
            collective_id=1, has_side_effects=True, vmem_limit_bytes=56 * MIB
        ),
        name="bring_home",
    )(row_force, pair_force, frag_energy, pair_energy)


AROUND = [(u, v) for u in (-1, 0, 1) for v in (-1, 0, 1) if (u, v) != (0, 0)]
CHUNKS = 4


STEP_PAIRS = 16


def three_parts(x):
    a = bf16(x).astype(jnp.float32)
    b = bf16(x - a).astype(jnp.float32)
    return [a, b, x - a - b, jnp.zeros_like(x)]


def block_of(u, v):
    return (u + 1) * 3 + v + 1


def halo_body(
    pairs_ref,
    count_ref,
    pos_ref,
    charge_ref,
    own_list_ref,
    slot_ref,
    feat_ref,
    near_ref,
    near_feat_ref,
    pair_force_ref,
    pair_energy_ref,
    rows_ref,
    parts,
    cols_a,
    cols_b,
    atom_send,
    atom_recv,
    side_send,
    side_recv,
    ahead_send,
    ahead_recv,
    corner_send,
    corner_recv,
    local_sem,
):
    bricks, subs = lax.axis_size("brick"), lax.axis_size("sub")
    brick, sub = lax.axis_index("brick"), lax.axis_index("sub")
    mesh_id = pl.DeviceIdType.MESH
    rows = feat_ref.shape[0]
    tiles = charge_ref.shape[0]
    part = rows // CHUNKS
    centre = block_of(0, 0) * tiles

    rows_ref[:, :SLOTS] = slot_ref[: rows_ref.shape[0]]
    rows_ref[:, SLOTS:] = slot_ref[rows_ref.shape[0] :]
    near_ref[pl.ds(centre, tiles)] = jnp.zeros((tiles, 8, TILE), jnp.float32)
    for t in range(tiles):
        for c in range(3):
            near_ref[centre + t, c : c + 1, :] = pos_ref[c, t : t + 1, :]
        near_ref[centre + t, 3:4, :] = charge_ref[t : t + 1, :]

    def inside(u, v):
        b, s = brick + u, sub + v
        return (b >= 0) & (b < bricks) & (s >= 0) & (s < subs)

    barrier = pltpu.get_barrier_semaphore()
    for u, v in AROUND:

        @pl.when(inside(u, v))
        def _(u=u, v=v):
            pl.semaphore_signal(
                barrier, inc=1, device_id=(brick + u, sub + v), device_id_type=mesh_id
            )

    beside = [
        jnp.where(at > 0, 1, 0) + jnp.where(at < size - 1, 1, 0)
        for at, size in ((brick, bricks), (sub, subs))
    ]
    pl.semaphore_wait(barrier, beside[0] + beside[1] + beside[0] * beside[1])

    def atom_copy(u, v):
        k = block_of(-u, -v)
        return pltpu.make_async_remote_copy(
            src_ref=near_ref.at[pl.ds(centre, tiles)],
            dst_ref=near_ref.at[pl.ds(k * tiles, tiles)],
            send_sem=atom_send.at[k],
            recv_sem=atom_recv.at[k],
            device_id=(brick + u, sub + v),
            device_id_type=mesh_id,
        )

    def ahead_copy(u, c):
        i = (u + 1) // 2
        return pltpu.make_async_remote_copy(
            src_ref=feat_ref.at[pl.ds(c * part, part)],
            dst_ref=near_feat_ref.at[block_of(-u, 0), pl.ds(c * part, part)],
            send_sem=ahead_send.at[i, c],
            recv_sem=ahead_recv.at[i, c],
            device_id=(brick + u, sub),
            device_id_type=mesh_id,
        )

    def side_copy(v):
        i = (v + 1) // 2
        return pltpu.make_async_remote_copy(
            src_ref=feat_ref,
            dst_ref=near_feat_ref.at[block_of(0, -v)],
            send_sem=side_send.at[i],
            recv_sem=side_recv.at[i],
            device_id=(brick, sub + v),
            device_id_type=mesh_id,
        )

    def corner_copy(w, v, c):
        i = (w + 1) + (v + 1) // 2
        at = pl.ds(c * part, part)
        return pltpu.make_async_remote_copy(
            src_ref=near_feat_ref.at[block_of(w, 0), at],
            dst_ref=near_feat_ref.at[block_of(w, -v), at],
            send_sem=corner_send.at[i, c],
            recv_sem=corner_recv.at[i, c],
            device_id=(brick, sub + v),
            device_id_type=mesh_id,
        )

    for u, v in AROUND:

        @pl.when(inside(u, v))
        def _(u=u, v=v):
            atom_copy(u, v).start()

    for c in range(CHUNKS):
        for u in (-1, 1):

            @pl.when(inside(u, 0))
            def _(u=u, c=c):
                ahead_copy(u, c).start()

        if c == 0:
            for v in (-1, 1):

                @pl.when(inside(0, v))
                def _(v=v):
                    side_copy(v).start()

    local = pltpu.make_async_copy(feat_ref, near_feat_ref.at[block_of(0, 0)], local_sem)
    local.start()
    for u, v in AROUND:
        k = block_of(u, v)

        @pl.when(jnp.logical_not(inside(u, v)))
        def _(k=k):
            near_ref[pl.ds(k * tiles, tiles)] = jnp.zeros((tiles, 8, TILE), jnp.float32)

    def forward(c):
        for w in (-1, 1):

            @pl.when(inside(w, 0))
            def _(w=w):
                ahead_copy(-w, c).wait_recv()
                for v in (-1, 1):

                    @pl.when(inside(0, v))
                    def _(w=w, v=v):
                        corner_copy(w, v, c).start()

    for u, v in AROUND:

        @pl.when(inside(-u, -v))
        def _(u=u, v=v):
            atom_copy(u, v).wait_recv()

    spread = (
        lax.broadcasted_iota(jnp.int32, (32, 4 * TILE), 0) % 8
        == lax.broadcasted_iota(jnp.int32, (32, 4 * TILE), 1) // TILE
    ).astype(jnp.bfloat16)
    chunk = 32

    def spread_near(cols, first):
        for k in range(4):
            near = pairs_ref[1, jnp.minimum(first + k, pairs - 1)]
            cols[k] = dot_tn(bf16(jnp.concatenate(three_parts(near_ref[near]), axis=0)), spread)

    def one_pair(p, cols, k):
        own = pairs_ref[0, p]
        near = pairs_ref[1, p]
        o = near_ref[centre + own]
        xi, yi, zi, qi = (o[c : c + 1, :] for c in range(4))
        sums = [jnp.zeros((8, TILE), jnp.float32) for _ in range(4)]
        for start in range(0, TILE, chunk):
            xj, yj, zj, qj = (
                cols[k, start : start + chunk, c * TILE : (c + 1) * TILE] for c in range(4)
            )
            dx, dy, dz = xi - xj, yi - yj, zi - zj
            square = dx * dx + dy * dy + dz * dz + CHARGE_SOFTEN
            rinv = lax.rsqrt(square)
            t = rinv * recip(rinv + ERFC_P * SCREEN_RATE)
            g = ERFC_C[-1]
            for coef in ERFC_C[-2::-1]:
                g = g * t + coef
            gauss = qj * jnp.exp2((-SCREEN_RATE * SCREEN_RATE * math.log2(math.e)) * square)
            screened = (g * t) * rinv
            w = (gauss * (screened + GAUSS)) * (rinv * rinv)
            for c, term in enumerate((w * dx, w * dy, w * dz, gauss * screened)):
                sums[c] += jnp.sum(term.reshape(chunk // 8, 8, TILE), axis=0)
        itself = jnp.where(near == own + centre, math.erfc(SCREEN_RATE), 0.0)
        for c in range(4):
            row = jnp.sum(sums[c], axis=0, keepdims=True)
            parts[c, pl.ds(p, 1), :] = qi * (row - itself * qi if c == 3 else row)

    def eight_pairs(i, carry):
        p = 8 * i
        spread_near(cols_b, p + 4)
        for k in range(4):
            one_pair(p + k, cols_a, k)
        spread_near(cols_a, p + 8)
        for k in range(4):
            one_pair(p + 4 + k, cols_b, k)
        return carry

    pairs = own_list_ref.shape[1]
    spread_near(cols_a, 0)
    done = 0
    for c in range(CHUNKS):
        forward(c)
        upto = (c + 1) * STEP_PAIRS if c < CHUNKS - 1 else pairs
        lax.fori_loop(done // 8, upto // 8, eight_pairs, 0)
        done = upto

    pick = (
        (own_list_ref[0:1, :] == lax.broadcasted_iota(jnp.int32, (16, pairs), 0))
        & (lax.broadcasted_iota(jnp.int32, (16, pairs), 1) < count_ref[0, 0])
    ).astype(jnp.bfloat16)
    for k in range(4):
        whole = sum(dot(pick, bf16(x)) for x in three_parts(parts[k])[:3])[:tiles]
        if k < 3:
            pair_force_ref[k] = COULOMB_UNIT * whole
        else:
            pair_energy_ref[...] = (0.5 * COULOMB_UNIT) * whole

    for v in (-1, 1):

        @pl.when(inside(0, -v))
        def _(v=v):
            side_copy(v).wait_recv()

    for w in (-1, 1):
        for v in (-1, 1):

            @pl.when(inside(w, -v))
            def _(w=w, v=v):
                for c in range(CHUNKS):
                    corner_copy(w, v, c).wait_recv()

    local.wait()
    for u, v in AROUND:

        @pl.when(inside(u, v))
        def _(u=u, v=v):
            atom_copy(u, v).wait_send()

    for u in (-1, 1):

        @pl.when(inside(u, 0))
        def _(u=u):
            for c in range(CHUNKS):
                ahead_copy(u, c).wait_send()

    for v in (-1, 1):

        @pl.when(inside(0, v))
        def _(v=v):
            side_copy(v).wait_send()

    for w in (-1, 1):
        for v in (-1, 1):

            @pl.when(inside(w, v))
            def _(w=w, v=v):
                for c in range(CHUNKS):
                    corner_copy(w, v, c).wait_send()


def halo(positions, charges, features, pairs, count, slot_index):
    tiles = charges.shape[0]
    smem = pl.BlockSpec(memory_space=pltpu.SMEM)
    vmem = pl.BlockSpec(memory_space=pltpu.VMEM)
    hbm = pl.BlockSpec(memory_space=pl.ANY)
    dma = pltpu.SemaphoreType.DMA
    return pl.pallas_call(
        halo_body,
        out_shape=(
            jax.ShapeDtypeStruct((9 * tiles, 8, TILE), jnp.float32),
            jax.ShapeDtypeStruct((9,) + features.shape, features.dtype),
            jax.ShapeDtypeStruct((3, tiles, TILE), jnp.float32),
            jax.ShapeDtypeStruct((tiles, TILE), jnp.float32),
            jax.ShapeDtypeStruct((slot_index.shape[0] // 2, 2 * SLOTS), jnp.int32),
        ),
        in_specs=[smem, smem, vmem, vmem, vmem, vmem, hbm],
        out_specs=(vmem, hbm, vmem, vmem, vmem),
        scratch_shapes=[
            pltpu.VMEM((4, pairs.shape[1], TILE), jnp.float32),
            pltpu.VMEM((4, TILE, 4 * TILE), jnp.float32),
            pltpu.VMEM((4, TILE, 4 * TILE), jnp.float32),
            dma((9,)),
            dma((9,)),
            dma((2,)),
            dma((2,)),
            dma((2, CHUNKS)),
            dma((2, CHUNKS)),
            dma((4, CHUNKS)),
            dma((4, CHUNKS)),
            dma(()),
        ],
        compiler_params=pltpu.CompilerParams(
            collective_id=2, has_side_effects=True, vmem_limit_bytes=56 * MIB
        ),
        name="halo",
    )(pairs, count, positions, charges, pairs, slot_index, features)


def body(
    atom_features,
    positions,
    charges,
    slot_index,
    atom_count,
    cap_weight,
    tile_pairs,
    tile_count,
    w_qkv,
    w_out,
    gains,
    rates,
    w_read,
    w_energy,
):
    own_size = atom_features.shape[2]
    own_tiles = own_size // TILE
    near8, near_features, pair_force, pair_energy, slot_rows = halo(
        positions.reshape(3, own_tiles, TILE),
        charges.reshape(own_tiles, TILE),
        atom_features.reshape(own_size, -1),
        tile_pairs.reshape(2, -1),
        tile_count,
        slot_index,
    )
    row_force, frag_energy = fragment_model(
        near8,
        near_features,
        slot_rows,
        atom_count,
        cap_weight,
        (w_qkv, w_out, gains, rates, w_read, w_energy),
    )
    forces, energy = bring_home(row_force, pair_force, frag_energy, pair_energy)
    return forces.reshape(3, 1, 1, own_size), energy.reshape(())


def solution(mesh):
    in_specs = (
        P("brick", "sub", None, None),
        P(None, "brick", "sub", None),
        P("brick", "sub", None),
        P(("brick", "sub"), None),
        P(("brick", "sub")),
        P(("brick", "sub"), None),
        P(None, "brick", "sub", None),
        P("brick", "sub"),
        P(),
        P(),
        P(),
        P(),
        P(),
        P(),
    )
    out_specs = (P(None, "brick", "sub", None), P())
    return jax.shard_map(body, mesh=mesh, in_specs=in_specs, out_specs=out_specs, check_vma=False)
```

```python
import math

import jax
import jax.numpy as jnp
from jax import lax
from jax.experimental import pallas as pl
from jax.experimental.pallas import tpu as pltpu
from jax.sharding import PartitionSpec as P

F = 256
HEADS = 8
LAYERS = 2
SLOTS = 64
TILE = 128
GROUP = 8
ROWS = GROUP * SLOTS
QUAD = 128

NORM_EPS = 1e-05
PAIR_SOFTEN = 0.01
SCREEN_RATE = 0.1
COULOMB_UNIT = 14.4
CHARGE_SOFTEN = 1.0
FAR = 1e30
GAUSS = 2.0 * SCREEN_RATE / math.sqrt(math.pi)
ERFC_P = 0.6
ERFC_C = (
    0.33858295223558404,
    0.33681896467541816,
    0.2948193558779553,
    0.06093701313639673,
    0.3109940554359323,
    -0.6781244471753995,
    0.4339317702022656,
    -0.0979638654555287,
)
MIB = 1024 * 1024


def dot(a, b):
    return lax.dot_general(a, b, (((1,), (0,)), ((), ())), preferred_element_type=jnp.float32)


def dot_nt(a, b):
    return lax.dot_general(a, b, (((1,), (1,)), ((), ())), preferred_element_type=jnp.float32)


def dot_tn(a, b):
    return lax.dot_general(a, b, (((0,), (0,)), ((), ())), preferred_element_type=jnp.float32)


def recip(x):
    return pl.reciprocal(x, approx=True)


def norm_parts(hidden):
    centre = jnp.mean(hidden, axis=-1, keepdims=True)
    shifted = hidden - centre
    spread = jnp.mean(shifted * shifted, axis=-1, keepdims=True)
    scale = lax.rsqrt(spread + NORM_EPS)
    return shifted * scale, scale


def norm_back(grad, gain, unit, scale):
    g = grad * gain
    mean_g = jnp.mean(g, axis=-1, keepdims=True)
    mean_gu = jnp.mean(g * unit, axis=-1, keepdims=True)
    return scale * (g - mean_g - unit * mean_gu)


def bf16(x):
    return x.astype(jnp.bfloat16)


def fragment_body(
    count_ref,
    slot_ref,
    rate_ref,
    near_ref,
    feat_ref,
    cap_ref,
    wqkv_ref,
    wout_ref,
    gains_ref,
    wread_ref,
    wen_ref,
    force_ref,
    energy_ref,
    table,
    forces,
    slots,
    slot_force,
    caps,
    span_ref,
    span_cols_ref,
    order_ref,
    tally,
    bins,
    landed,
    landed_sem,
):
    tiles = near_ref.shape[0]
    frags = cap_ref.shape[0]

    def eighth_of(f):
        return (f % (frags // 2)) * (2 * SLOTS // 8) + f // (frags // 2) * (SLOTS // 8)


    def feature_copy(i):
        return pltpu.make_async_copy(feat_ref.at[i], landed.at[i], landed_sem.at[i])

    for i in range(tiles // 8):
        feature_copy(i).start()

    def widen(i, carry):
        feature_copy(i).wait()
        for k in range(8):
            at = pl.multiple_of(i * 8 * TILE + k * TILE, TILE)
            both = landed[i, k * TILE : (k + 1) * TILE, :].astype(jnp.float32)
            n = jnp.transpose(near_ref[i * 8 + k])
            atoms = jnp.concatenate([n, jnp.zeros((TILE, TILE - 8), jnp.float32)], axis=1)
            for c, part in enumerate((both[:, :QUAD], both[:, QUAD:], atoms)):
                table[pl.ds(at * 4 + c, TILE, stride=4), :] = part
            forces[pl.ds(at, TILE), :] = jnp.zeros((TILE, TILE), jnp.float32)
        return carry

    slot_force[...] = jnp.zeros_like(slot_force)
    head = lax.broadcasted_iota(jnp.int32, (1, HEADS * SLOTS), 1) // SLOTS
    head_col = lax.broadcasted_iota(jnp.int32, (1, F), 1) // (F // HEADS)
    for layer in range(LAYERS):
        wide = jnp.ones((1, HEADS * SLOTS), jnp.float32)
        cols = jnp.ones((1, F), jnp.float32)
        for h in range(HEADS):
            wide = jnp.where(head == h, rate_ref[layer, h], wide)
            cols = jnp.where(head_col == h, rate_ref[layer, h], cols)
        span_ref[layer : layer + 1, :] = 1.0 / wide
        span_cols_ref[layer : layer + 1, :] = 1.0 / cols
    slots[:TILE, :] = jnp.zeros((TILE, TILE), jnp.float32)
    slots[:frags, :SLOTS] = cap_ref[...]
    cols = jnp.transpose(slots[:TILE, :])
    for f in range(frags):
        wide = jnp.broadcast_to(cols[:SLOTS, f : f + 1], (SLOTS, TILE))
        for k in range(SLOTS // 8):
            caps[eighth_of(f) + k] = wide[k * 8 : (k + 1) * 8]
    energy_ref[...] = jnp.zeros_like(energy_ref)

    for size in range(16):
        tally[size] = 0
    for k in range(frags):
        size = (count_ref[k] + 7) >> 3
        tally[size] = tally[size] + 1
    ends = {9: 0}
    for size in range(8, 1, -1):
        ends[size] = ends[size + 1] + tally[size]
        tally[size] = ends[size + 1]
    for k in range(frags):
        live = count_ref[k]
        size = (live + 7) >> 3
        at = tally[size]
        order_ref[at] = live * 512 + eighth_of(k)
        tally[size] = at + 1
    n6, n5, n3, n2 = (ends[k] - ends[k + 1] for k in (6, 5, 3, 2))
    with6 = jnp.minimum(n6, n2)
    with5 = jnp.minimum(n5, n2 - with6 + n3)
    runs = [ends[7], ends[7] + with6, ends[6], ends[6] + with5, ends[5]]
    high = frags - 1
    made = 0
    for k in range(frags):
        fits = (
            ((k >= runs[0]) & (k < runs[1]))
            | ((k >= runs[2]) & (k < runs[3]))
            | (k >= runs[4])
        )
        both = fits & (k < high)
        big = order_ref[k]
        small = order_ref[jnp.maximum(high, 0)]
        bins[0, k] = big & 511
        bins[1, k] = small & 511
        bins[2, k] = big >> 9
        bins[3, k] = jnp.where(both, ((big >> 9) + 7) & -8, SLOTS)
        bins[4, k] = jnp.where(both, small >> 9, 0)
        made = jnp.where(k <= high, k + 1, made)
        high = high - jnp.where(both, 1, 0)
    for k in range(2 * GROUP - 1):
        bins[0, made + k] = 0
        bins[1, made + k] = 0
        bins[2, made + k] = 0
        bins[3, made + k] = SLOTS
        bins[4, made + k] = 0

    lane = lax.broadcasted_iota(jnp.int32, (1, QUAD), 1)
    head_mask = [(lane // 32 == h).astype(jnp.bfloat16) for h in range(4)]
    head_pick = [lane // 32 == h for h in range(4)]
    slot_row = lax.broadcasted_iota(jnp.int32, (SLOTS, QUAD), 0)
    slot_lane = lax.broadcasted_iota(jnp.int32, (SLOTS, QUAD), 1) % SLOTS

    def spread_heads(x):
        return jnp.concatenate([x * head_mask[h] for h in range(4)], axis=0)

    def fold_heads(x):
        out = jnp.where(head_pick[0], x[0:SLOTS], 0.0)
        for h in range(1, 4):
            out = jnp.where(head_pick[h], x[h * SLOTS : (h + 1) * SLOTS], out)
        return out

    half = 0.5 / math.sqrt(32.0)
    units = [(f, quad) for f in range(GROUP) for quad in range(2)]

    def rows_of(f):
        return slice(f * SLOTS, (f + 1) * SLOTS)

    def eighths(which):
        big, small, start = (bins[c, which] for c in (0, 1, 3))
        start = start >> 3
        for k in range(SLOTS // 8):
            yield k, jnp.where(k < start, big, small - start) + k

    def gather(b):
        for f in range(GROUP):
            for k, part in eighths(b * GROUP + f):
                rs = [slot_ref[part * 8 + j] for j in range(8)]
                at = f * SLOTS + k * 8
                for j in range(8):
                    row = pl.multiple_of(rs[j] * 4, 4)
                    slots[4 * (at + j) : 4 * (at + j) + 4, :] = table[pl.ds(row, 4), :]

    def scatter(b):
        for f in range(GROUP):
            for k, part in eighths(b * GROUP + f):
                rs = [slot_ref[part * 8 + j] for j in range(8)]
                old = [forces[pl.ds(r, 1), :] for r in rs]
                for j in range(8):
                    at = f * SLOTS + k * 8 + j
                    forces[pl.ds(rs[j], 1), :] = old[j] + slot_force[at : at + 1, :]
        return forces[pl.ds(rs[7], 1), :]

    def one_block(b, carry):
        info = [tuple(bins[c, b * GROUP + f] for c in (2, 3, 4)) for f in range(GROUP)]
        h0 = jnp.concatenate([slots[pl.ds(c, ROWS, stride=4), :] for c in range(2)], axis=1)
        atoms = slots[pl.ds(2, ROWS, stride=4), :]
        gather(b + 1)
        last = scatter(jnp.maximum(b - 1, 0))

        atom_rows = jnp.transpose(atoms)
        dists, inverses, offsets, weights = [], [], [], []
        for f in range(GROUP):
            first, start, second = info[f]
            col = atoms[rows_of(f), :]
            row = atom_rows[0:8, rows_of(f)]
            row = jnp.concatenate([row, row], axis=1)
            off = [col[:, c : c + 1] - row[c : c + 1, :] for c in range(3)]
            square = off[0] * off[0] + off[1] * off[1] + off[2] * off[2] + PAIR_SOFTEN
            inverse = lax.rsqrt(square)

            def owner(i, dead):
                late = jnp.logical_and(i >= start, i < start + second)
                return jnp.where(i < first, 1, jnp.where(late, 2, dead))

            mine = owner(slot_row, 0)
            dists.append(jnp.where(mine == owner(slot_lane, -1), square * inverse, FAR))
            inverses.append(inverse)
            offsets.append(off)
            cap = jnp.concatenate([caps[part] for _, part in eighths(b * GROUP + f)], axis=0)
            weights.append(jnp.where(mine > 0, cap, 0.0))
        dist2 = [jnp.concatenate([d, d], axis=1) for d in dists]
        weight = jnp.concatenate(weights, axis=0)

        def attention(layer, project):
            def part(f, quad, which):
                at = which * F + quad * QUAD
                return project[rows_of(f), at : at + QUAD]

            qs = [part(f, quad, 0) for f, quad in units]
            kbs = [spread_heads(part(f, quad, 1)) for f, quad in units]
            vbs = [spread_heads(part(f, quad, 2)) for f, quad in units]
            scores = [dot_nt(q, kb) for q, kb in zip(qs, kbs)]
            atts, by_dist, by_score = [], [], []
            for (f, quad), score in zip(units, scores):
                u = score * half
                th = jnp.tanh(u)
                silu = u + u * th
                span = span_ref[layer : layer + 1, quad * 256 : (quad + 1) * 256]
                damp = recip(dist2[f] + span)
                att = silu * damp
                atts.append(bf16(att))
                by_dist.append(att * damp)
                if layer == 1:
                    by_score.append(damp * ((1.0 + th) + (silu - silu * th)))
            span_cols = span_cols_ref[layer : layer + 1, :]
            message = [dot(att, vb) for att, vb in zip(atts, vbs)]
            message = jnp.concatenate(
                [jnp.concatenate(message[2 * f : 2 * f + 2], axis=1) for f in range(GROUP)], axis=0
            )
            return bf16(message * span_cols), (qs, kbs, vbs, atts, by_dist, by_score)

        gain = [gains_ref[i : i + 1, :] for i in range(LAYERS + 1)]
        unit0, _ = norm_parts(h0)
        project0 = bf16(dot(bf16(unit0 * gain[0]), wqkv_ref[0]))
        message0, kept0 = attention(0, project0)
        h1 = h0 + dot(message0, wout_ref[0])
        unit1, scale1 = norm_parts(h1)
        project1 = bf16(dot(bf16(unit1 * gain[1]), wqkv_ref[1]))
        message1, kept1 = attention(1, project1)
        h2 = h1 + dot(message1, wout_ref[1])
        unit2, scale2 = norm_parts(h2)
        u = 0.5 * dot(bf16(unit2 * gain[2]), wread_ref[...])
        th = jnp.tanh(u)
        silu = u + u * th
        weighted = weight * (wen_ref[...] + 0.0 * last)
        energy_ref[...] += jnp.sum((weighted * silu).reshape(ROWS // 8, 8, QUAD), axis=0)

        dread = bf16((0.5 * weighted) * ((1.0 + th) + (silu - silu * th)))
        dh2 = norm_back(dot_nt(dread, wread_ref[...]), gain[2], unit2, scale2)
        dmsg1 = bf16(dot_nt(bf16(dh2), wout_ref[1]) * span_cols_ref[1:2, :])
        qs, kbs, vbs, atts, by_dist, by_score = kept1
        dms = [dmsg1[rows_of(f), quad * QUAD : (quad + 1) * QUAD] for f, quad in units]
        datts = [dot_nt(dm, vb) for dm, vb in zip(dms, vbs)]
        dvs = [bf16(fold_heads(dot_tn(att, dm))) for att, dm in zip(atts, dms)]
        dss = [bf16(datt * slope) for datt, slope in zip(datts, by_score)]
        dqs = [bf16(dot(ds, kb) * half) for ds, kb in zip(dss, kbs)]
        dks = [bf16(fold_heads(dot_tn(ds, q)) * half) for ds, q in zip(dss, qs)]
        pulls = [datt * slope for datt, slope in zip(datts, by_dist)]
        dproject = jnp.concatenate(
            [
                jnp.concatenate(
                    [x[2 * f + quad] for x in (dqs, dks, dvs) for quad in range(2)], axis=1
                )
                for f in range(GROUP)
            ],
            axis=0,
        )
        dh1 = dh2 + norm_back(dot_nt(dproject, wqkv_ref[1]), gain[1], unit1, scale1)
        dmsg0 = bf16(dot_nt(bf16(dh1), wout_ref[0]) * span_cols_ref[0:1, :])
        datts = [
            dot_nt(dmsg0[rows_of(f), quad * QUAD : (quad + 1) * QUAD], vb)
            for (f, quad), vb in zip(units, kept0[2])
        ]
        pulls = [old + datt * slope for old, datt, slope in zip(pulls, datts, kept0[4])]
        force_rows = []
        for f in range(GROUP):
            pull = pulls[2 * f] + pulls[2 * f + 1]
            pull = (pull[:, :QUAD] + pull[:, QUAD:]) * inverses[f]
            pull = pull[:, :SLOTS] + pull[:, SLOTS:]
            pull = pull + jnp.transpose(pull)
            for c in range(3):
                force_rows.append(
                    -jnp.sum(pull * offsets[f][c][:, :SLOTS], axis=0, keepdims=True)
                )
        packed = jnp.concatenate(
            [
                jnp.concatenate([force_rows[3 * f + c] for f in range(GROUP)], axis=1)
                for c in range(3)
            ]
            + [jnp.zeros((5, ROWS), jnp.float32)],
            axis=0,
        )
        slot_force[:, 0:8] = jnp.transpose(packed)
        return carry

    lax.fori_loop(0, tiles // 8, widen, 0)
    gather(0)
    groups = (made + GROUP - 1) // GROUP
    lax.fori_loop(0, groups, one_block, 0)
    scatter(groups - 1)

    pick = (
        lax.broadcasted_iota(jnp.int32, (16, TILE), 0)
        == lax.broadcasted_iota(jnp.int32, (16, TILE), 1)
    ).astype(jnp.bfloat16)
    for i in range(tiles // 8):
        rows = dot_nt(pick, bf16(forces[i * 1024 : (i + 1) * 1024, :]))
        for c in range(3):
            for k in range(8):
                force_ref[i, c, k : k + 1, :] = rows[c : c + 1, k * TILE : (k + 1) * TILE]


def fragment_model(near8, near_features, slot_rows, atom_count, cap_weight, weights):
    w_qkv, w_out, gains, rates, w_read, w_energy = weights
    tiles = near8.shape[0]
    frags = atom_count.shape[0]
    smem = pl.BlockSpec(memory_space=pltpu.SMEM)
    vmem = pl.BlockSpec(memory_space=pltpu.VMEM)
    force, energy = pl.pallas_call(
        fragment_body,
        out_shape=(
            jax.ShapeDtypeStruct((tiles // 8, 3, 8, TILE), jnp.float32),
            jax.ShapeDtypeStruct((8, TILE), jnp.float32),
        ),
        in_specs=[smem, smem, smem, vmem, pl.BlockSpec(memory_space=pl.ANY)] + [vmem] * 6,
        out_specs=(vmem, vmem),
        scratch_shapes=[
            pltpu.VMEM((4 * tiles * TILE, TILE), jnp.float32),
            pltpu.VMEM((tiles * TILE, TILE), jnp.float32),
            pltpu.VMEM((4 * ROWS, TILE), jnp.float32),
            pltpu.VMEM((ROWS, TILE), jnp.float32),
            pltpu.VMEM((SLOTS // 8 * frags, 8, TILE), jnp.float32),
            pltpu.VMEM((LAYERS, HEADS * SLOTS), jnp.float32),
            pltpu.VMEM((LAYERS, F), jnp.float32),
            pltpu.SMEM((frags,), jnp.int32),
            pltpu.SMEM((16,), jnp.int32),
            pltpu.SMEM((5, frags + 2 * GROUP), jnp.int32),
            pltpu.VMEM(near_features.shape, near_features.dtype),
            pltpu.SemaphoreType.DMA((tiles // 8,)),
        ],
        compiler_params=pltpu.CompilerParams(vmem_limit_bytes=56 * MIB),
        name="fragments",
    )(
        atom_count,
        slot_rows.reshape(-1),
        rates,
        near8,
        near_features,
        cap_weight,
        w_qkv,
        w_out,
        gains,
        w_read,
        w_energy.reshape(1, -1),
    )
    return force, energy


def home_body(
    force_ref,
    pair_ref,
    frag_energy_ref,
    pair_energy_ref,
    out_ref,
    energy_ref,
    landing,
    by_sub,
    by_brick,
    force_send,
    force_recv,
    sub_send,
    sub_recv,
    brick_send,
    brick_recv,
):
    bricks, subs = by_brick.shape[0], by_sub.shape[0]
    brick, sub = lax.axis_index("brick"), lax.axis_index("sub")
    mesh_id = pl.DeviceIdType.MESH
    around = [(u, v) for u in (-1, 0, 1) for v in (-1, 0, 1) if (u, v) != (0, 0)]

    def inside(u, v):
        b, s = brick + u, sub + v
        return (b >= 0) & (b < bricks) & (s >= 0) & (s < subs)

    sub_peers = [(brick, lax.rem(sub + d, subs)) for d in range(1, subs)]
    brick_peers = [(lax.rem(brick + d, bricks), sub) for d in range(1, bricks)]

    barrier = pltpu.get_barrier_semaphore()
    for peer in sub_peers + brick_peers:
        pl.semaphore_signal(barrier, inc=1, device_id=peer, device_id_type=mesh_id)
    corners = [(u, v) for u, v in around if u != 0 and v != 0]
    for u, v in corners:

        @pl.when(inside(u, v))
        def _(u=u, v=v):
            pl.semaphore_signal(
                barrier, inc=1, device_id=(brick + u, sub + v), device_id_type=mesh_id
            )

    beside = [
        jnp.where(at > 0, 1, 0) + jnp.where(at < size - 1, 1, 0)
        for at, size in ((brick, bricks), (sub, subs))
    ]
    pl.semaphore_wait(barrier, subs + bricks - 2 + beside[0] * beside[1])

    def energy_copy(store, send, recv, k, slot, peer):
        return pltpu.make_async_remote_copy(
            src_ref=store.at[slot],
            dst_ref=store.at[slot],
            send_sem=send.at[k],
            recv_sem=recv.at[slot],
            device_id=peer,
            device_id_type=mesh_id,
        )

    by_sub[sub] = frag_energy_ref[...] + pair_energy_ref[...]
    for k, peer in enumerate(sub_peers):
        energy_copy(by_sub, sub_send, sub_recv, k, sub, peer).start()

    def force_copy(u, v):
        k = (u + 1) * 3 + v + 1
        return pltpu.make_async_remote_copy(
            src_ref=force_ref.at[k],
            dst_ref=landing.at[k],
            send_sem=force_send.at[k],
            recv_sem=force_recv.at[k],
            device_id=(brick + u, sub + v),
            device_id_type=mesh_id,
        )

    for u, v in around:

        @pl.when(inside(u, v))
        def _(u=u, v=v):
            force_copy(u, v).start()

    for k, peer in enumerate(sub_peers):
        energy_copy(by_sub, sub_send, sub_recv, k, peer[1], peer).wait_recv()
    by_brick[brick] = jnp.sum(by_sub[...], axis=0)
    for k, peer in enumerate(brick_peers):
        energy_copy(by_brick, brick_send, brick_recv, k, brick, peer).start()

    out_ref[...] = force_ref[4] + pair_ref[...]
    for u, v in around:
        @pl.when(inside(-u, -v))
        def _(u=u, v=v):
            force_copy(u, v).wait_recv()
            out_ref[...] += landing[(u + 1) * 3 + v + 1]

    for k, peer in enumerate(brick_peers):
        energy_copy(by_brick, brick_send, brick_recv, k, peer[0], peer).wait_recv()
    energy_ref[0, 0] = jnp.sum(jnp.sum(by_brick[...], axis=0))

    for u, v in around:

        @pl.when(inside(u, v))
        def _(u=u, v=v):
            force_copy(u, v).wait_send()

    for k, peer in enumerate(sub_peers):
        energy_copy(by_sub, sub_send, sub_recv, k, sub, peer).wait_send()
    for k, peer in enumerate(brick_peers):
        energy_copy(by_brick, brick_send, brick_recv, k, brick, peer).wait_send()


def bring_home(row_force, pair_force, frag_energy, pair_energy):
    bricks, subs = lax.axis_size("brick"), lax.axis_size("sub")
    vmem = pl.BlockSpec(memory_space=pltpu.VMEM)
    block = row_force.shape[1:]
    dma = pltpu.SemaphoreType.DMA
    return pl.pallas_call(
        home_body,
        out_shape=(
            jax.ShapeDtypeStruct(block, jnp.float32),
            jax.ShapeDtypeStruct((1, 1), jnp.float32),
        ),
        in_specs=[vmem] * 4,
        out_specs=(vmem, pl.BlockSpec(memory_space=pltpu.SMEM)),
        scratch_shapes=[
            pltpu.VMEM((9,) + block, jnp.float32),
            pltpu.VMEM((subs, 8, TILE), jnp.float32),
            pltpu.VMEM((bricks, 8, TILE), jnp.float32),
            dma((9,)),
            dma((9,)),
            dma((subs,)),
            dma((subs,)),
            dma((bricks,)),
            dma((bricks,)),
        ],
        compiler_params=pltpu.CompilerParams(
            collective_id=1, has_side_effects=True, vmem_limit_bytes=56 * MIB
        ),
        name="bring_home",
    )(row_force, pair_force, frag_energy, pair_energy)


AROUND = [(u, v) for u in (-1, 0, 1) for v in (-1, 0, 1) if (u, v) != (0, 0)]
CHUNKS = 4


STEP_PAIRS = 16


def three_parts(x):
    a = bf16(x).astype(jnp.float32)
    b = bf16(x - a).astype(jnp.float32)
    return [a, b, x - a - b, jnp.zeros_like(x)]


def block_of(u, v):
    return (u + 1) * 3 + v + 1


def halo_body(
    pairs_ref,
    count_ref,
    pos_ref,
    charge_ref,
    own_list_ref,
    slot_ref,
    feat_ref,
    near_ref,
    near_feat_ref,
    pair_force_ref,
    pair_energy_ref,
    rows_ref,
    parts,
    cols_a,
    cols_b,
    atom_send,
    atom_recv,
    side_send,
    side_recv,
    ahead_send,
    ahead_recv,
    corner_send,
    corner_recv,
    local_sem,
):
    bricks, subs = lax.axis_size("brick"), lax.axis_size("sub")
    brick, sub = lax.axis_index("brick"), lax.axis_index("sub")
    mesh_id = pl.DeviceIdType.MESH
    rows = feat_ref.shape[0]
    tiles = charge_ref.shape[0]
    part = rows // CHUNKS
    centre = block_of(0, 0) * tiles

    rows_ref[:, :SLOTS] = slot_ref[: rows_ref.shape[0]]
    rows_ref[:, SLOTS:] = slot_ref[rows_ref.shape[0] :]
    near_ref[pl.ds(centre, tiles)] = jnp.zeros((tiles, 8, TILE), jnp.float32)
    for t in range(tiles):
        for c in range(3):
            near_ref[centre + t, c : c + 1, :] = pos_ref[c, t : t + 1, :]
        near_ref[centre + t, 3:4, :] = charge_ref[t : t + 1, :]

    def inside(u, v):
        b, s = brick + u, sub + v
        return (b >= 0) & (b < bricks) & (s >= 0) & (s < subs)

    barrier = pltpu.get_barrier_semaphore()
    for u, v in AROUND:

        @pl.when(inside(u, v))
        def _(u=u, v=v):
            pl.semaphore_signal(
                barrier, inc=1, device_id=(brick + u, sub + v), device_id_type=mesh_id
            )

    beside = [
        jnp.where(at > 0, 1, 0) + jnp.where(at < size - 1, 1, 0)
        for at, size in ((brick, bricks), (sub, subs))
    ]
    pl.semaphore_wait(barrier, beside[0] + beside[1] + beside[0] * beside[1])

    def atom_copy(u, v):
        k = block_of(-u, -v)
        return pltpu.make_async_remote_copy(
            src_ref=near_ref.at[pl.ds(centre, tiles)],
            dst_ref=near_ref.at[pl.ds(k * tiles, tiles)],
            send_sem=atom_send.at[k],
            recv_sem=atom_recv.at[k],
            device_id=(brick + u, sub + v),
            device_id_type=mesh_id,
        )

    def ahead_copy(u, c):
        i = (u + 1) // 2
        return pltpu.make_async_remote_copy(
            src_ref=feat_ref.at[pl.ds(c * part, part)],
            dst_ref=near_feat_ref.at[block_of(-u, 0), pl.ds(c * part, part)],
            send_sem=ahead_send.at[i, c],
            recv_sem=ahead_recv.at[i, c],
            device_id=(brick + u, sub),
            device_id_type=mesh_id,
        )

    def side_copy(v):
        i = (v + 1) // 2
        return pltpu.make_async_remote_copy(
            src_ref=feat_ref,
            dst_ref=near_feat_ref.at[block_of(0, -v)],
            send_sem=side_send.at[i],
            recv_sem=side_recv.at[i],
            device_id=(brick, sub + v),
            device_id_type=mesh_id,
        )

    def corner_copy(w, v, c):
        i = (w + 1) + (v + 1) // 2
        at = pl.ds(c * part, part)
        return pltpu.make_async_remote_copy(
            src_ref=near_feat_ref.at[block_of(w, 0), at],
            dst_ref=near_feat_ref.at[block_of(w, -v), at],
            send_sem=corner_send.at[i, c],
            recv_sem=corner_recv.at[i, c],
            device_id=(brick, sub + v),
            device_id_type=mesh_id,
        )

    for u, v in AROUND:

        @pl.when(inside(u, v))
        def _(u=u, v=v):
            atom_copy(u, v).start()

    for c in range(CHUNKS):
        for u in (-1, 1):

            @pl.when(inside(u, 0))
            def _(u=u, c=c):
                ahead_copy(u, c).start()

        if c == 0:
            for v in (-1, 1):

                @pl.when(inside(0, v))
                def _(v=v):
                    side_copy(v).start()

    local = pltpu.make_async_copy(feat_ref, near_feat_ref.at[block_of(0, 0)], local_sem)
    local.start()
    for u, v in AROUND:
        k = block_of(u, v)

        @pl.when(jnp.logical_not(inside(u, v)))
        def _(k=k):
            near_ref[pl.ds(k * tiles, tiles)] = jnp.zeros((tiles, 8, TILE), jnp.float32)

    def forward(c):
        for w in (-1, 1):

            @pl.when(inside(w, 0))
            def _(w=w):
                ahead_copy(-w, c).wait_recv()
                for v in (-1, 1):

                    @pl.when(inside(0, v))
                    def _(w=w, v=v):
                        corner_copy(w, v, c).start()

    for u, v in AROUND:

        @pl.when(inside(-u, -v))
        def _(u=u, v=v):
            atom_copy(u, v).wait_recv()

    spread = (
        lax.broadcasted_iota(jnp.int32, (32, 4 * TILE), 0) % 8
        == lax.broadcasted_iota(jnp.int32, (32, 4 * TILE), 1) // TILE
    ).astype(jnp.bfloat16)
    chunk = 32

    def spread_near(cols, first):
        for k in range(4):
            near = pairs_ref[1, jnp.minimum(first + k, pairs - 1)]
            cols[k] = dot_tn(bf16(jnp.concatenate(three_parts(near_ref[near]), axis=0)), spread)

    def one_pair(p, cols, k):
        own = pairs_ref[0, p]
        near = pairs_ref[1, p]
        o = near_ref[centre + own]
        xi, yi, zi, qi = (o[c : c + 1, :] for c in range(4))
        sums = [jnp.zeros((8, TILE), jnp.float32) for _ in range(4)]
        for start in range(0, TILE, chunk):
            xj, yj, zj, qj = (
                cols[k, start : start + chunk, c * TILE : (c + 1) * TILE] for c in range(4)
            )
            dx, dy, dz = xi - xj, yi - yj, zi - zj
            square = dx * dx + dy * dy + dz * dz + CHARGE_SOFTEN
            rinv = lax.rsqrt(square)
            t = rinv * recip(rinv + ERFC_P * SCREEN_RATE)
            g = ERFC_C[-1]
            for coef in ERFC_C[-2::-1]:
                g = g * t + coef
            gauss = qj * jnp.exp2((-SCREEN_RATE * SCREEN_RATE * math.log2(math.e)) * square)
            screened = (g * t) * rinv
            w = (gauss * (screened + GAUSS)) * (rinv * rinv)
            for c, term in enumerate((w * dx, w * dy, w * dz, gauss * screened)):
                sums[c] += jnp.sum(term.reshape(chunk // 8, 8, TILE), axis=0)
        itself = jnp.where(near == own + centre, math.erfc(SCREEN_RATE), 0.0)
        for c in range(4):
            row = jnp.sum(sums[c], axis=0, keepdims=True)
            parts[c, pl.ds(p, 1), :] = qi * (row - itself * qi if c == 3 else row)

    def eight_pairs(i, carry):
        p = 8 * i
        for k in range(4):
            one_pair(p + k, cols_a, k)
        spread_near(cols_a, p + 8)
        for k in range(4):
            one_pair(p + 4 + k, cols_b, k)
        spread_near(cols_b, p + 12)
        return carry

    pairs = own_list_ref.shape[1]
    spread_near(cols_a, 0)
    spread_near(cols_b, 4)
    done = 0
    for c in range(CHUNKS):
        forward(c)
        upto = (c + 1) * STEP_PAIRS if c < CHUNKS - 1 else pairs
        lax.fori_loop(done // 8, upto // 8, eight_pairs, 0)
        done = upto

    pick = (
        (own_list_ref[0:1, :] == lax.broadcasted_iota(jnp.int32, (16, pairs), 0))
        & (lax.broadcasted_iota(jnp.int32, (16, pairs), 1) < count_ref[0, 0])
    ).astype(jnp.bfloat16)
    for k in range(4):
        whole = sum(dot(pick, bf16(x)) for x in three_parts(parts[k])[:3])[:tiles]
        if k < 3:
            pair_force_ref[k] = COULOMB_UNIT * whole
        else:
            pair_energy_ref[...] = (0.5 * COULOMB_UNIT) * whole

    for v in (-1, 1):

        @pl.when(inside(0, -v))
        def _(v=v):
            side_copy(v).wait_recv()

    for w in (-1, 1):
        for v in (-1, 1):

            @pl.when(inside(w, -v))
            def _(w=w, v=v):
                for c in range(CHUNKS):
                    corner_copy(w, v, c).wait_recv()

    local.wait()
    for u, v in AROUND:

        @pl.when(inside(u, v))
        def _(u=u, v=v):
            atom_copy(u, v).wait_send()

    for u in (-1, 1):

        @pl.when(inside(u, 0))
        def _(u=u):
            for c in range(CHUNKS):
                ahead_copy(u, c).wait_send()

    for v in (-1, 1):

        @pl.when(inside(0, v))
        def _(v=v):
            side_copy(v).wait_send()

    for w in (-1, 1):
        for v in (-1, 1):

            @pl.when(inside(w, v))
            def _(w=w, v=v):
                for c in range(CHUNKS):
                    corner_copy(w, v, c).wait_send()


def halo(positions, charges, features, pairs, count, slot_index):
    tiles = charges.shape[0]
    smem = pl.BlockSpec(memory_space=pltpu.SMEM)
    vmem = pl.BlockSpec(memory_space=pltpu.VMEM)
    hbm = pl.BlockSpec(memory_space=pl.ANY)
    dma = pltpu.SemaphoreType.DMA
    return pl.pallas_call(
        halo_body,
        out_shape=(
            jax.ShapeDtypeStruct((9 * tiles, 8, TILE), jnp.float32),
            jax.ShapeDtypeStruct((9,) + features.shape, features.dtype),
            jax.ShapeDtypeStruct((3, tiles, TILE), jnp.float32),
            jax.ShapeDtypeStruct((tiles, TILE), jnp.float32),
            jax.ShapeDtypeStruct((slot_index.shape[0] // 2, 2 * SLOTS), jnp.int32),
        ),
        in_specs=[smem, smem, vmem, vmem, vmem, vmem, hbm],
        out_specs=(vmem, hbm, vmem, vmem, vmem),
        scratch_shapes=[
            pltpu.VMEM((4, pairs.shape[1], TILE), jnp.float32),
            pltpu.VMEM((4, TILE, 4 * TILE), jnp.float32),
            pltpu.VMEM((4, TILE, 4 * TILE), jnp.float32),
            dma((9,)),
            dma((9,)),
            dma((2,)),
            dma((2,)),
            dma((2, CHUNKS)),
            dma((2, CHUNKS)),
            dma((4, CHUNKS)),
            dma((4, CHUNKS)),
            dma(()),
        ],
        compiler_params=pltpu.CompilerParams(
            collective_id=2, has_side_effects=True, vmem_limit_bytes=56 * MIB
        ),
        name="halo",
    )(pairs, count, positions, charges, pairs, slot_index, features)


def body(
    atom_features,
    positions,
    charges,
    slot_index,
    atom_count,
    cap_weight,
    tile_pairs,
    tile_count,
    w_qkv,
    w_out,
    gains,
    rates,
    w_read,
    w_energy,
):
    own_size = atom_features.shape[2]
    own_tiles = own_size // TILE
    near8, near_features, pair_force, pair_energy, slot_rows = halo(
        positions.reshape(3, own_tiles, TILE),
        charges.reshape(own_tiles, TILE),
        atom_features.reshape(own_size, -1),
        tile_pairs.reshape(2, -1),
        tile_count,
        slot_index,
    )
    row_force, frag_energy = fragment_model(
        near8,
        near_features,
        slot_rows,
        atom_count,
        cap_weight,
        (w_qkv, w_out, gains, rates, w_read, w_energy),
    )
    forces, energy = bring_home(row_force, pair_force, frag_energy, pair_energy)
    return forces.reshape(3, 1, 1, own_size), energy.reshape(())


def solution(mesh):
    in_specs = (
        P("brick", "sub", None, None),
        P(None, "brick", "sub", None),
        P("brick", "sub", None),
        P(("brick", "sub"), None),
        P(("brick", "sub")),
        P(("brick", "sub"), None),
        P(None, "brick", "sub", None),
        P("brick", "sub"),
        P(),
        P(),
        P(),
        P(),
        P(),
        P(),
    )
    out_specs = (P(None, "brick", "sub", None), P())
    return jax.shard_map(body, mesh=mesh, in_specs=in_specs, out_specs=out_specs, check_vma=False)
```

```python
import math

import jax
import jax.numpy as jnp
from jax import lax
from jax.experimental import pallas as pl
from jax.experimental.pallas import tpu as pltpu
from jax.sharding import PartitionSpec as P

F = 256
HEADS = 8
LAYERS = 2
SLOTS = 64
TILE = 128
GROUP = 8
ROWS = GROUP * SLOTS
QUAD = 128

NORM_EPS = 1e-05
PAIR_SOFTEN = 0.01
SCREEN_RATE = 0.1
COULOMB_UNIT = 14.4
CHARGE_SOFTEN = 1.0
FAR = 1e30
GAUSS = 2.0 * SCREEN_RATE / math.sqrt(math.pi)
ERFC_P = 0.6
ERFC_C = (
    0.33858295223558404,
    0.33681896467541816,
    0.2948193558779553,
    0.06093701313639673,
    0.3109940554359323,
    -0.6781244471753995,
    0.4339317702022656,
    -0.0979638654555287,
)
MIB = 1024 * 1024


def dot(a, b):
    return lax.dot_general(a, b, (((1,), (0,)), ((), ())), preferred_element_type=jnp.float32)


def dot_nt(a, b):
    return lax.dot_general(a, b, (((1,), (1,)), ((), ())), preferred_element_type=jnp.float32)


def dot_tn(a, b):
    return lax.dot_general(a, b, (((0,), (0,)), ((), ())), preferred_element_type=jnp.float32)


def recip(x):
    return pl.reciprocal(x, approx=True)


def norm_parts(hidden):
    centre = jnp.mean(hidden, axis=-1, keepdims=True)
    shifted = hidden - centre
    spread = jnp.mean(shifted * shifted, axis=-1, keepdims=True)
    scale = lax.rsqrt(spread + NORM_EPS)
    return shifted * scale, scale


def norm_back(grad, gain, unit, scale):
    g = grad * gain
    mean_g = jnp.mean(g, axis=-1, keepdims=True)
    mean_gu = jnp.mean(g * unit, axis=-1, keepdims=True)
    return scale * (g - mean_g - unit * mean_gu)


def bf16(x):
    return x.astype(jnp.bfloat16)


def fragment_body(
    count_ref,
    slot_ref,
    rate_ref,
    near_ref,
    feat_ref,
    cap_ref,
    wqkv_ref,
    wout_ref,
    gains_ref,
    wread_ref,
    wen_ref,
    force_ref,
    energy_ref,
    table,
    forces,
    slots,
    slot_force,
    caps,
    span_ref,
    span_cols_ref,
    order_ref,
    tally,
    bins,
    landed,
    landed_sem,
):
    tiles = near_ref.shape[0]
    frags = cap_ref.shape[0]

    def eighth_of(f):
        return (f % (frags // 2)) * (2 * SLOTS // 8) + f // (frags // 2) * (SLOTS // 8)


    def feature_copy(i):
        return pltpu.make_async_copy(feat_ref.at[i], landed.at[i], landed_sem.at[i])

    for i in range(tiles // 8):
        feature_copy(i).start()

    def widen(i, carry):
        feature_copy(i).wait()
        for k in range(8):
            at = pl.multiple_of(i * 8 * TILE + k * TILE, TILE)
            both = landed[i, k * TILE : (k + 1) * TILE, :].astype(jnp.float32)
            n = jnp.transpose(near_ref[i * 8 + k])
            atoms = jnp.concatenate([n, jnp.zeros((TILE, TILE - 8), jnp.float32)], axis=1)
            for c, part in enumerate((both[:, :QUAD], both[:, QUAD:], atoms)):
                table[pl.ds(at * 4 + c, TILE, stride=4), :] = part
            forces[pl.ds(at, TILE), :] = jnp.zeros((TILE, TILE), jnp.float32)
        return carry

    slot_force[...] = jnp.zeros_like(slot_force)
    head = lax.broadcasted_iota(jnp.int32, (1, HEADS * SLOTS), 1) // SLOTS
    head_col = lax.broadcasted_iota(jnp.int32, (1, F), 1) // (F // HEADS)
    for layer in range(LAYERS):
        wide = jnp.ones((1, HEADS * SLOTS), jnp.float32)
        cols = jnp.ones((1, F), jnp.float32)
        for h in range(HEADS):
            wide = jnp.where(head == h, rate_ref[layer, h], wide)
            cols = jnp.where(head_col == h, rate_ref[layer, h], cols)
        span_ref[layer : layer + 1, :] = 1.0 / wide
        span_cols_ref[layer : layer + 1, :] = 1.0 / cols
    slots[:TILE, :] = jnp.zeros((TILE, TILE), jnp.float32)
    slots[:frags, :SLOTS] = cap_ref[...]
    cols = jnp.transpose(slots[:TILE, :])
    for f in range(frags):
        wide = jnp.broadcast_to(cols[:SLOTS, f : f + 1], (SLOTS, TILE))
        for k in range(SLOTS // 8):
            caps[eighth_of(f) + k] = wide[k * 8 : (k + 1) * 8]
    energy_ref[...] = jnp.zeros_like(energy_ref)

    for size in range(16):
        tally[size] = 0
    for k in range(frags):
        size = (count_ref[k] + 7) >> 3
        tally[size] = tally[size] + 1
    ends = {9: 0}
    for size in range(8, 1, -1):
        ends[size] = ends[size + 1] + tally[size]
        tally[size] = ends[size + 1]
    for k in range(frags):
        live = count_ref[k]
        size = (live + 7) >> 3
        at = tally[size]
        order_ref[at] = live * 512 + eighth_of(k)
        tally[size] = at + 1
    n6, n5, n3, n2 = (ends[k] - ends[k + 1] for k in (6, 5, 3, 2))
    with6 = jnp.minimum(n6, n2)
    with5 = jnp.minimum(n5, n2 - with6 + n3)
    runs = [ends[7], ends[7] + with6, ends[6], ends[6] + with5, ends[5]]
    high = frags - 1
    made = 0
    for k in range(frags):
        fits = (
            ((k >= runs[0]) & (k < runs[1]))
            | ((k >= runs[2]) & (k < runs[3]))
            | (k >= runs[4])
        )
        both = fits & (k < high)
        big = order_ref[k]
        small = order_ref[jnp.maximum(high, 0)]
        bins[0, k] = big & 511
        bins[1, k] = small & 511
        bins[2, k] = big >> 9
        bins[3, k] = jnp.where(both, ((big >> 9) + 7) & -8, SLOTS)
        bins[4, k] = jnp.where(both, small >> 9, 0)
        made = jnp.where(k <= high, k + 1, made)
        high = high - jnp.where(both, 1, 0)
    for k in range(2 * GROUP - 1):
        bins[0, made + k] = 0
        bins[1, made + k] = 0
        bins[2, made + k] = 0
        bins[3, made + k] = SLOTS
        bins[4, made + k] = 0

    lane = lax.broadcasted_iota(jnp.int32, (1, QUAD), 1)
    head_mask = [(lane // 32 == h).astype(jnp.bfloat16) for h in range(4)]
    head_pick = [lane // 32 == h for h in range(4)]
    slot_row = lax.broadcasted_iota(jnp.int32, (SLOTS, QUAD), 0)
    slot_lane = lax.broadcasted_iota(jnp.int32, (SLOTS, QUAD), 1) % SLOTS

    def spread_heads(x):
        return jnp.concatenate([x * head_mask[h] for h in range(4)], axis=0)

    def fold_heads(x):
        out = jnp.where(head_pick[0], x[0:SLOTS], 0.0)
        for h in range(1, 4):
            out = jnp.where(head_pick[h], x[h * SLOTS : (h + 1) * SLOTS], out)
        return out

    half = 0.5 / math.sqrt(32.0)
    units = [(f, quad) for f in range(GROUP) for quad in range(2)]

    def rows_of(f):
        return slice(f * SLOTS, (f + 1) * SLOTS)

    def eighths(which):
        big, small, start = (bins[c, which] for c in (0, 1, 3))
        start = start >> 3
        for k in range(SLOTS // 8):
            yield k, jnp.where(k < start, big, small - start) + k

    def gather(b):
        for f in range(GROUP):
            for k, part in eighths(b * GROUP + f):
                rs = [slot_ref[part * 8 + j] for j in range(8)]
                at = f * SLOTS + k * 8
                for j in range(8):
                    row = pl.multiple_of(rs[j] * 4, 4)
                    slots[4 * (at + j) : 4 * (at + j) + 4, :] = table[pl.ds(row, 4), :]

    def scatter(b):
        for f in range(GROUP):
            for k, part in eighths(b * GROUP + f):
                rs = [slot_ref[part * 8 + j] for j in range(8)]
                old = [forces[pl.ds(r, 1), :] for r in rs]
                for j in range(8):
                    at = f * SLOTS + k * 8 + j
                    forces[pl.ds(rs[j], 1), :] = old[j] + slot_force[at : at + 1, :]
        return forces[pl.ds(rs[7], 1), :]

    def one_block(b, carry):
        info = [tuple(bins[c, b * GROUP + f] for c in (2, 3, 4)) for f in range(GROUP)]
        h0 = jnp.concatenate([slots[pl.ds(c, ROWS, stride=4), :] for c in range(2)], axis=1)
        atoms = slots[pl.ds(2, ROWS, stride=4), :]
        gather(b + 1)
        last = scatter(jnp.maximum(b - 1, 0))

        atom_rows = jnp.transpose(atoms)
        dists, inverses, offsets, weights = [], [], [], []
        for f in range(GROUP):
            first, start, second = info[f]
            col = atoms[rows_of(f), :]
            row = atom_rows[0:8, rows_of(f)]
            row = jnp.concatenate([row, row], axis=1)
            off = [col[:, c : c + 1] - row[c : c + 1, :] for c in range(3)]
            square = off[0] * off[0] + off[1] * off[1] + off[2] * off[2] + PAIR_SOFTEN
            inverse = lax.rsqrt(square)

            def owner(i, dead):
                late = jnp.logical_and(i >= start, i < start + second)
                return jnp.where(i < first, 1, jnp.where(late, 2, dead))

            mine = owner(slot_row, 0)
            dists.append(jnp.where(mine == owner(slot_lane, -1), square * inverse, FAR))
            inverses.append(inverse)
            offsets.append(off)
            cap = jnp.concatenate([caps[part] for _, part in eighths(b * GROUP + f)], axis=0)
            weights.append(jnp.where(mine > 0, cap, 0.0))
        dist2 = [jnp.concatenate([d, d], axis=1) for d in dists]
        weight = jnp.concatenate(weights, axis=0)

        def attention(layer, project):
            def part(f, quad, which):
                at = which * F + quad * QUAD
                return project[rows_of(f), at : at + QUAD]

            qs = [part(f, quad, 0) for f, quad in units]
            kbs = [spread_heads(part(f, quad, 1)) for f, quad in units]
            vbs = [spread_heads(part(f, quad, 2)) for f, quad in units]
            scores = [dot_nt(q, kb) for q, kb in zip(qs, kbs)]
            atts, by_dist, by_score = [], [], []
            for (f, quad), score in zip(units, scores):
                u = score * half
                th = jnp.tanh(u)
                silu = u + u * th
                span = span_ref[layer : layer + 1, quad * 256 : (quad + 1) * 256]
                damp = recip(dist2[f] + span)
                att = silu * damp
                atts.append(bf16(att))
                by_dist.append(att * damp)
                if layer == 1:
                    by_score.append(damp * ((1.0 + th) + (silu - silu * th)))
            span_cols = span_cols_ref[layer : layer + 1, :]
            message = [dot(att, vb) for att, vb in zip(atts, vbs)]
            message = jnp.concatenate(
                [jnp.concatenate(message[2 * f : 2 * f + 2], axis=1) for f in range(GROUP)], axis=0
            )
            return bf16(message * span_cols), (qs, kbs, vbs, atts, by_dist, by_score)

        gain = [gains_ref[i : i + 1, :] for i in range(LAYERS + 1)]
        unit0, _ = norm_parts(h0)
        project0 = bf16(dot(bf16(unit0 * gain[0]), wqkv_ref[0]))
        message0, kept0 = attention(0, project0)
        h1 = h0 + dot(message0, wout_ref[0])
        unit1, scale1 = norm_parts(h1)
        project1 = bf16(dot(bf16(unit1 * gain[1]), wqkv_ref[1]))
        message1, kept1 = attention(1, project1)
        h2 = h1 + dot(message1, wout_ref[1])
        unit2, scale2 = norm_parts(h2)
        u = 0.5 * dot(bf16(unit2 * gain[2]), wread_ref[...])
        th = jnp.tanh(u)
        silu = u + u * th
        weighted = weight * (wen_ref[...] + 0.0 * last)
        energy_ref[...] += jnp.sum((weighted * silu).reshape(ROWS // 8, 8, QUAD), axis=0)

        dread = bf16((0.5 * weighted) * ((1.0 + th) + (silu - silu * th)))
        dh2 = norm_back(dot_nt(dread, wread_ref[...]), gain[2], unit2, scale2)
        dmsg1 = bf16(dot_nt(bf16(dh2), wout_ref[1]) * span_cols_ref[1:2, :])
        qs, kbs, vbs, atts, by_dist, by_score = kept1
        dms = [dmsg1[rows_of(f), quad * QUAD : (quad + 1) * QUAD] for f, quad in units]
        datts = [dot_nt(dm, vb) for dm, vb in zip(dms, vbs)]
        dvs = [bf16(fold_heads(dot_tn(att, dm))) for att, dm in zip(atts, dms)]
        dss = [bf16(datt * slope) for datt, slope in zip(datts, by_score)]
        dqs = [bf16(dot(ds, kb) * half) for ds, kb in zip(dss, kbs)]
        dks = [bf16(fold_heads(dot_tn(ds, q)) * half) for ds, q in zip(dss, qs)]
        pulls = [datt * slope for datt, slope in zip(datts, by_dist)]
        dproject = jnp.concatenate(
            [
                jnp.concatenate(
                    [x[2 * f + quad] for x in (dqs, dks, dvs) for quad in range(2)], axis=1
                )
                for f in range(GROUP)
            ],
            axis=0,
        )
        dh1 = dh2 + norm_back(dot_nt(dproject, wqkv_ref[1]), gain[1], unit1, scale1)
        dmsg0 = bf16(dot_nt(bf16(dh1), wout_ref[0]) * span_cols_ref[0:1, :])
        datts = [
            dot_nt(dmsg0[rows_of(f), quad * QUAD : (quad + 1) * QUAD], vb)
            for (f, quad), vb in zip(units, kept0[2])
        ]
        pulls = [old + datt * slope for old, datt, slope in zip(pulls, datts, kept0[4])]
        force_rows = []
        for f in range(GROUP):
            pull = pulls[2 * f] + pulls[2 * f + 1]
            pull = (pull[:, :QUAD] + pull[:, QUAD:]) * inverses[f]
            pull = pull[:, :SLOTS] + pull[:, SLOTS:]
            pull = pull + jnp.transpose(pull)
            for c in range(3):
                force_rows.append(
                    -jnp.sum(pull * offsets[f][c][:, :SLOTS], axis=0, keepdims=True)
                )
        packed = jnp.concatenate(
            [
                jnp.concatenate([force_rows[3 * f + c] for f in range(GROUP)], axis=1)
                for c in range(3)
            ]
            + [jnp.zeros((5, ROWS), jnp.float32)],
            axis=0,
        )
        slot_force[:, 0:8] = jnp.transpose(packed)
        return carry

    lax.fori_loop(0, tiles // 8, widen, 0)
    gather(0)
    groups = (made + GROUP - 1) // GROUP
    lax.fori_loop(0, groups, one_block, 0)
    scatter(groups - 1)

    pick = (
        lax.broadcasted_iota(jnp.int32, (16, TILE), 0)
        == lax.broadcasted_iota(jnp.int32, (16, TILE), 1)
    ).astype(jnp.bfloat16)
    for i in range(tiles // 8):
        rows = dot_nt(pick, bf16(forces[i * 1024 : (i + 1) * 1024, :]))
        for c in range(3):
            for k in range(8):
                force_ref[i, c, k : k + 1, :] = rows[c : c + 1, k * TILE : (k + 1) * TILE]


def fragment_model(near8, near_features, slot_rows, atom_count, cap_weight, weights):
    w_qkv, w_out, gains, rates, w_read, w_energy = weights
    tiles = near8.shape[0]
    frags = atom_count.shape[0]
    smem = pl.BlockSpec(memory_space=pltpu.SMEM)
    vmem = pl.BlockSpec(memory_space=pltpu.VMEM)
    force, energy = pl.pallas_call(
        fragment_body,
        out_shape=(
            jax.ShapeDtypeStruct((tiles // 8, 3, 8, TILE), jnp.float32),
            jax.ShapeDtypeStruct((8, TILE), jnp.float32),
        ),
        in_specs=[smem, smem, smem, vmem, pl.BlockSpec(memory_space=pl.ANY)] + [vmem] * 6,
        out_specs=(vmem, vmem),
        scratch_shapes=[
            pltpu.VMEM((4 * tiles * TILE, TILE), jnp.float32),
            pltpu.VMEM((tiles * TILE, TILE), jnp.float32),
            pltpu.VMEM((4 * ROWS, TILE), jnp.float32),
            pltpu.VMEM((ROWS, TILE), jnp.float32),
            pltpu.VMEM((SLOTS // 8 * frags, 8, TILE), jnp.float32),
            pltpu.VMEM((LAYERS, HEADS * SLOTS), jnp.float32),
            pltpu.VMEM((LAYERS, F), jnp.float32),
            pltpu.SMEM((frags,), jnp.int32),
            pltpu.SMEM((16,), jnp.int32),
            pltpu.SMEM((5, frags + 2 * GROUP), jnp.int32),
            pltpu.VMEM(near_features.shape, near_features.dtype),
            pltpu.SemaphoreType.DMA((tiles // 8,)),
        ],
        compiler_params=pltpu.CompilerParams(vmem_limit_bytes=56 * MIB),
        name="fragments",
    )(
        atom_count,
        slot_rows.reshape(-1),
        rates,
        near8,
        near_features,
        cap_weight,
        w_qkv,
        w_out,
        gains,
        w_read,
        w_energy.reshape(1, -1),
    )
    return force, energy


def home_body(
    force_ref,
    pair_ref,
    frag_energy_ref,
    pair_energy_ref,
    out_ref,
    energy_ref,
    landing,
    by_sub,
    by_brick,
    force_send,
    force_recv,
    sub_send,
    sub_recv,
    brick_send,
    brick_recv,
):
    bricks, subs = by_brick.shape[0], by_sub.shape[0]
    brick, sub = lax.axis_index("brick"), lax.axis_index("sub")
    mesh_id = pl.DeviceIdType.MESH
    around = [(u, v) for u in (-1, 0, 1) for v in (-1, 0, 1) if (u, v) != (0, 0)]

    def inside(u, v):
        b, s = brick + u, sub + v
        return (b >= 0) & (b < bricks) & (s >= 0) & (s < subs)

    sub_peers = [(brick, lax.rem(sub + d, subs)) for d in range(1, subs)]
    brick_peers = [(lax.rem(brick + d, bricks), sub) for d in range(1, bricks)]

    barrier = pltpu.get_barrier_semaphore()
    for peer in sub_peers + brick_peers:
        pl.semaphore_signal(barrier, inc=1, device_id=peer, device_id_type=mesh_id)
    corners = [(u, v) for u, v in around if u != 0 and v != 0]
    for u, v in corners:

        @pl.when(inside(u, v))
        def _(u=u, v=v):
            pl.semaphore_signal(
                barrier, inc=1, device_id=(brick + u, sub + v), device_id_type=mesh_id
            )

    beside = [
        jnp.where(at > 0, 1, 0) + jnp.where(at < size - 1, 1, 0)
        for at, size in ((brick, bricks), (sub, subs))
    ]
    pl.semaphore_wait(barrier, subs + bricks - 2 + beside[0] * beside[1])

    def energy_copy(store, send, recv, k, slot, peer):
        return pltpu.make_async_remote_copy(
            src_ref=store.at[slot],
            dst_ref=store.at[slot],
            send_sem=send.at[k],
            recv_sem=recv.at[slot],
            device_id=peer,
            device_id_type=mesh_id,
        )

    by_sub[sub] = frag_energy_ref[...] + pair_energy_ref[...]
    for k, peer in enumerate(sub_peers):
        energy_copy(by_sub, sub_send, sub_recv, k, sub, peer).start()

    def force_copy(u, v):
        k = (u + 1) * 3 + v + 1
        return pltpu.make_async_remote_copy(
            src_ref=force_ref.at[k],
            dst_ref=landing.at[k],
            send_sem=force_send.at[k],
            recv_sem=force_recv.at[k],
            device_id=(brick + u, sub + v),
            device_id_type=mesh_id,
        )

    for u, v in around:

        @pl.when(inside(u, v))
        def _(u=u, v=v):
            force_copy(u, v).start()

    for k, peer in enumerate(sub_peers):
        energy_copy(by_sub, sub_send, sub_recv, k, peer[1], peer).wait_recv()
    by_brick[brick] = jnp.sum(by_sub[...], axis=0)
    for k, peer in enumerate(brick_peers):
        energy_copy(by_brick, brick_send, brick_recv, k, brick, peer).start()

    out_ref[...] = force_ref[4] + pair_ref[...]
    for u, v in around:
        @pl.when(inside(-u, -v))
        def _(u=u, v=v):
            force_copy(u, v).wait_recv()
            out_ref[...] += landing[(u + 1) * 3 + v + 1]

    for k, peer in enumerate(brick_peers):
        energy_copy(by_brick, brick_send, brick_recv, k, peer[0], peer).wait_recv()
    energy_ref[0, 0] = jnp.sum(jnp.sum(by_brick[...], axis=0))

    for u, v in around:

        @pl.when(inside(u, v))
        def _(u=u, v=v):
            force_copy(u, v).wait_send()

    for k, peer in enumerate(sub_peers):
        energy_copy(by_sub, sub_send, sub_recv, k, sub, peer).wait_send()
    for k, peer in enumerate(brick_peers):
        energy_copy(by_brick, brick_send, brick_recv, k, brick, peer).wait_send()


def bring_home(row_force, pair_force, frag_energy, pair_energy):
    bricks, subs = lax.axis_size("brick"), lax.axis_size("sub")
    vmem = pl.BlockSpec(memory_space=pltpu.VMEM)
    block = row_force.shape[1:]
    dma = pltpu.SemaphoreType.DMA
    return pl.pallas_call(
        home_body,
        out_shape=(
            jax.ShapeDtypeStruct(block, jnp.float32),
            jax.ShapeDtypeStruct((1, 1), jnp.float32),
        ),
        in_specs=[vmem] * 4,
        out_specs=(vmem, pl.BlockSpec(memory_space=pltpu.SMEM)),
        scratch_shapes=[
            pltpu.VMEM((9,) + block, jnp.float32),
            pltpu.VMEM((subs, 8, TILE), jnp.float32),
            pltpu.VMEM((bricks, 8, TILE), jnp.float32),
            dma((9,)),
            dma((9,)),
            dma((subs,)),
            dma((subs,)),
            dma((bricks,)),
            dma((bricks,)),
        ],
        compiler_params=pltpu.CompilerParams(
            collective_id=1, has_side_effects=True, vmem_limit_bytes=56 * MIB
        ),
        name="bring_home",
    )(row_force, pair_force, frag_energy, pair_energy)


AROUND = [(u, v) for u in (-1, 0, 1) for v in (-1, 0, 1) if (u, v) != (0, 0)]
CHUNKS = 4


STEP_PAIRS = 16


def three_parts(x):
    a = bf16(x).astype(jnp.float32)
    b = bf16(x - a).astype(jnp.float32)
    return [a, b, x - a - b, jnp.zeros_like(x)]


def block_of(u, v):
    return (u + 1) * 3 + v + 1


def halo_body(
    pairs_ref,
    count_ref,
    pos_ref,
    charge_ref,
    own_list_ref,
    slot_ref,
    feat_ref,
    near_ref,
    near_feat_ref,
    pair_force_ref,
    pair_energy_ref,
    rows_ref,
    parts,
    cols_a,
    cols_b,
    atom_send,
    atom_recv,
    side_send,
    side_recv,
    ahead_send,
    ahead_recv,
    corner_send,
    corner_recv,
    local_sem,
):
    bricks, subs = lax.axis_size("brick"), lax.axis_size("sub")
    brick, sub = lax.axis_index("brick"), lax.axis_index("sub")
    mesh_id = pl.DeviceIdType.MESH
    rows = feat_ref.shape[0]
    tiles = charge_ref.shape[0]
    part = rows // CHUNKS
    centre = block_of(0, 0) * tiles

    rows_ref[:, :SLOTS] = slot_ref[: rows_ref.shape[0]]
    rows_ref[:, SLOTS:] = slot_ref[rows_ref.shape[0] :]
    near_ref[pl.ds(centre, tiles)] = jnp.zeros((tiles, 8, TILE), jnp.float32)
    for t in range(tiles):
        for c in range(3):
            near_ref[centre + t, c : c + 1, :] = pos_ref[c, t : t + 1, :]
        near_ref[centre + t, 3:4, :] = charge_ref[t : t + 1, :]

    def inside(u, v):
        b, s = brick + u, sub + v
        return (b >= 0) & (b < bricks) & (s >= 0) & (s < subs)

    barrier = pltpu.get_barrier_semaphore()
    for u, v in AROUND:

        @pl.when(inside(u, v))
        def _(u=u, v=v):
            pl.semaphore_signal(
                barrier, inc=1, device_id=(brick + u, sub + v), device_id_type=mesh_id
            )

    beside = [
        jnp.where(at > 0, 1, 0) + jnp.where(at < size - 1, 1, 0)
        for at, size in ((brick, bricks), (sub, subs))
    ]
    pl.semaphore_wait(barrier, beside[0] + beside[1] + beside[0] * beside[1])

    def atom_copy(u, v):
        k = block_of(-u, -v)
        return pltpu.make_async_remote_copy(
            src_ref=near_ref.at[pl.ds(centre, tiles)],
            dst_ref=near_ref.at[pl.ds(k * tiles, tiles)],
            send_sem=atom_send.at[k],
            recv_sem=atom_recv.at[k],
            device_id=(brick + u, sub + v),
            device_id_type=mesh_id,
        )

    def ahead_copy(u, c):
        i = (u + 1) // 2
        return pltpu.make_async_remote_copy(
            src_ref=feat_ref.at[pl.ds(c * part, part)],
            dst_ref=near_feat_ref.at[block_of(-u, 0), pl.ds(c * part, part)],
            send_sem=ahead_send.at[i, c],
            recv_sem=ahead_recv.at[i, c],
            device_id=(brick + u, sub),
            device_id_type=mesh_id,
        )

    def side_copy(v):
        i = (v + 1) // 2
        return pltpu.make_async_remote_copy(
            src_ref=feat_ref,
            dst_ref=near_feat_ref.at[block_of(0, -v)],
            send_sem=side_send.at[i],
            recv_sem=side_recv.at[i],
            device_id=(brick, sub + v),
            device_id_type=mesh_id,
        )

    def corner_copy(w, v, c):
        i = (w + 1) + (v + 1) // 2
        at = pl.ds(c * part, part)
        return pltpu.make_async_remote_copy(
            src_ref=near_feat_ref.at[block_of(w, 0), at],
            dst_ref=near_feat_ref.at[block_of(w, -v), at],
            send_sem=corner_send.at[i, c],
            recv_sem=corner_recv.at[i, c],
            device_id=(brick, sub + v),
            device_id_type=mesh_id,
        )

    for u, v in AROUND:

        @pl.when(inside(u, v))
        def _(u=u, v=v):
            atom_copy(u, v).start()

    for c in range(CHUNKS):
        for u in (-1, 1):

            @pl.when(inside(u, 0))
            def _(u=u, c=c):
                ahead_copy(u, c).start()

        if c == 0:
            for v in (-1, 1):

                @pl.when(inside(0, v))
                def _(v=v):
                    side_copy(v).start()

    local = pltpu.make_async_copy(feat_ref, near_feat_ref.at[block_of(0, 0)], local_sem)
    local.start()
    for u, v in AROUND:
        k = block_of(u, v)

        @pl.when(jnp.logical_not(inside(u, v)))
        def _(k=k):
            near_ref[pl.ds(k * tiles, tiles)] = jnp.zeros((tiles, 8, TILE), jnp.float32)

    def forward(c):
        for w in (-1, 1):

            @pl.when(inside(w, 0))
            def _(w=w):
                ahead_copy(-w, c).wait_recv()
                for v in (-1, 1):

                    @pl.when(inside(0, v))
                    def _(w=w, v=v):
                        corner_copy(w, v, c).start()

    for u, v in AROUND:

        @pl.when(inside(-u, -v))
        def _(u=u, v=v):
            atom_copy(u, v).wait_recv()

    spread = (
        lax.broadcasted_iota(jnp.int32, (32, 4 * TILE), 0) % 8
        == lax.broadcasted_iota(jnp.int32, (32, 4 * TILE), 1) // TILE
    ).astype(jnp.bfloat16)
    chunk = 32

    def spread_near(cols, first):
        for k in range(4):
            near = pairs_ref[1, jnp.minimum(first + k, pairs - 1)]
            cols[k] = dot_tn(bf16(jnp.concatenate(three_parts(near_ref[near]), axis=0)), spread)

    def one_pair(p, cols, k):
        own = pairs_ref[0, p]
        near = pairs_ref[1, p]
        o = near_ref[centre + own]
        xi, yi, zi, qi = (o[c : c + 1, :] for c in range(4))
        sums = [jnp.zeros((8, TILE), jnp.float32) for _ in range(4)]
        for start in range(0, TILE, chunk):
            xj, yj, zj, qj = (
                cols[k, start : start + chunk, c * TILE : (c + 1) * TILE] for c in range(4)
            )
            dx, dy, dz = xi - xj, yi - yj, zi - zj
            square = dx * dx + dy * dy + dz * dz + CHARGE_SOFTEN
            rinv = lax.rsqrt(square)
            t = rinv * recip(rinv + ERFC_P * SCREEN_RATE)
            g = ERFC_C[-1]
            for coef in ERFC_C[-2::-1]:
                g = g * t + coef
            gauss = qj * jnp.exp2((-SCREEN_RATE * SCREEN_RATE * math.log2(math.e)) * square)
            screened = (g * t) * rinv
            w = (gauss * (screened + GAUSS)) * (rinv * rinv)
            for c, term in enumerate((w * dx, w * dy, w * dz, gauss * screened)):
                sums[c] += jnp.sum(term.reshape(chunk // 8, 8, TILE), axis=0)
        itself = jnp.where(near == own + centre, math.erfc(SCREEN_RATE), 0.0)
        for c in range(4):
            row = jnp.sum(sums[c], axis=0, keepdims=True)
            parts[c, pl.ds(p, 1), :] = qi * (row - itself * qi if c == 3 else row)

    def eight_pairs(i, carry):
        p = 8 * i
        for k in range(4):
            one_pair(p + k, cols_a, k)
        spread_near(cols_a, p + 8)
        for k in range(4):
            one_pair(p + 4 + k, cols_b, k)
        spread_near(cols_b, p + 12)
        return carry

    pairs = own_list_ref.shape[1]
    spread_near(cols_a, 0)
    spread_near(cols_b, 4)
    done = 0
    for c in range(CHUNKS + 1):
        upto = (c + 1) * STEP_PAIRS if c < CHUNKS else pairs
        lax.fori_loop(done // 8, upto // 8, eight_pairs, 0)
        done = upto
        if c < CHUNKS:
            forward(c)

    pick = (
        (own_list_ref[0:1, :] == lax.broadcasted_iota(jnp.int32, (16, pairs), 0))
        & (lax.broadcasted_iota(jnp.int32, (16, pairs), 1) < count_ref[0, 0])
    ).astype(jnp.bfloat16)
    for k in range(4):
        whole = sum(dot(pick, bf16(x)) for x in three_parts(parts[k])[:3])[:tiles]
        if k < 3:
            pair_force_ref[k] = COULOMB_UNIT * whole
        else:
            pair_energy_ref[...] = (0.5 * COULOMB_UNIT) * whole

    for v in (-1, 1):

        @pl.when(inside(0, -v))
        def _(v=v):
            side_copy(v).wait_recv()

    for w in (-1, 1):
        for v in (-1, 1):

            @pl.when(inside(w, -v))
            def _(w=w, v=v):
                for c in range(CHUNKS):
                    corner_copy(w, v, c).wait_recv()

    local.wait()
    for u, v in AROUND:

        @pl.when(inside(u, v))
        def _(u=u, v=v):
            atom_copy(u, v).wait_send()

    for u in (-1, 1):

        @pl.when(inside(u, 0))
        def _(u=u):
            for c in range(CHUNKS):
                ahead_copy(u, c).wait_send()

    for v in (-1, 1):

        @pl.when(inside(0, v))
        def _(v=v):
            side_copy(v).wait_send()

    for w in (-1, 1):
        for v in (-1, 1):

            @pl.when(inside(w, v))
            def _(w=w, v=v):
                for c in range(CHUNKS):
                    corner_copy(w, v, c).wait_send()


def halo(positions, charges, features, pairs, count, slot_index):
    tiles = charges.shape[0]
    smem = pl.BlockSpec(memory_space=pltpu.SMEM)
    vmem = pl.BlockSpec(memory_space=pltpu.VMEM)
    hbm = pl.BlockSpec(memory_space=pl.ANY)
    dma = pltpu.SemaphoreType.DMA
    return pl.pallas_call(
        halo_body,
        out_shape=(
            jax.ShapeDtypeStruct((9 * tiles, 8, TILE), jnp.float32),
            jax.ShapeDtypeStruct((9,) + features.shape, features.dtype),
            jax.ShapeDtypeStruct((3, tiles, TILE), jnp.float32),
            jax.ShapeDtypeStruct((tiles, TILE), jnp.float32),
            jax.ShapeDtypeStruct((slot_index.shape[0] // 2, 2 * SLOTS), jnp.int32),
        ),
        in_specs=[smem, smem, vmem, vmem, vmem, vmem, hbm],
        out_specs=(vmem, hbm, vmem, vmem, vmem),
        scratch_shapes=[
            pltpu.VMEM((4, pairs.shape[1], TILE), jnp.float32),
            pltpu.VMEM((4, TILE, 4 * TILE), jnp.float32),
            pltpu.VMEM((4, TILE, 4 * TILE), jnp.float32),
            dma((9,)),
            dma((9,)),
            dma((2,)),
            dma((2,)),
            dma((2, CHUNKS)),
            dma((2, CHUNKS)),
            dma((4, CHUNKS)),
            dma((4, CHUNKS)),
            dma(()),
        ],
        compiler_params=pltpu.CompilerParams(
            collective_id=2, has_side_effects=True, vmem_limit_bytes=56 * MIB
        ),
        name="halo",
    )(pairs, count, positions, charges, pairs, slot_index, features)


def body(
    atom_features,
    positions,
    charges,
    slot_index,
    atom_count,
    cap_weight,
    tile_pairs,
    tile_count,
    w_qkv,
    w_out,
    gains,
    rates,
    w_read,
    w_energy,
):
    own_size = atom_features.shape[2]
    own_tiles = own_size // TILE
    near8, near_features, pair_force, pair_energy, slot_rows = halo(
        positions.reshape(3, own_tiles, TILE),
        charges.reshape(own_tiles, TILE),
        atom_features.reshape(own_size, -1),
        tile_pairs.reshape(2, -1),
        tile_count,
        slot_index,
    )
    row_force, frag_energy = fragment_model(
        near8,
        near_features,
        slot_rows,
        atom_count,
        cap_weight,
        (w_qkv, w_out, gains, rates, w_read, w_energy),
    )
    forces, energy = bring_home(row_force, pair_force, frag_energy, pair_energy)
    return forces.reshape(3, 1, 1, own_size), energy.reshape(())


def solution(mesh):
    in_specs = (
        P("brick", "sub", None, None),
        P(None, "brick", "sub", None),
        P("brick", "sub", None),
        P(("brick", "sub"), None),
        P(("brick", "sub")),
        P(("brick", "sub"), None),
        P(None, "brick", "sub", None),
        P("brick", "sub"),
        P(),
        P(),
        P(),
        P(),
        P(),
        P(),
    )
    out_specs = (P(None, "brick", "sub", None), P())
    return jax.shard_map(body, mesh=mesh, in_specs=in_specs, out_specs=out_specs, check_vma=False)
```

```python
import math

import jax
import jax.numpy as jnp
from jax import lax
from jax.experimental import pallas as pl
from jax.experimental.pallas import tpu as pltpu
from jax.sharding import PartitionSpec as P

F = 256
HEADS = 8
LAYERS = 2
SLOTS = 64
TILE = 128
GROUP = 8
ROWS = GROUP * SLOTS
QUAD = 128

NORM_EPS = 1e-05
PAIR_SOFTEN = 0.01
SCREEN_RATE = 0.1
COULOMB_UNIT = 14.4
CHARGE_SOFTEN = 1.0
FAR = 1e30
GAUSS = 2.0 * SCREEN_RATE / math.sqrt(math.pi)
ERFC_P = 0.6
ERFC_C = (
    0.33858295223558404,
    0.33681896467541816,
    0.2948193558779553,
    0.06093701313639673,
    0.3109940554359323,
    -0.6781244471753995,
    0.4339317702022656,
    -0.0979638654555287,
)
MIB = 1024 * 1024


def dot(a, b):
    return lax.dot_general(a, b, (((1,), (0,)), ((), ())), preferred_element_type=jnp.float32)


def dot_nt(a, b):
    return lax.dot_general(a, b, (((1,), (1,)), ((), ())), preferred_element_type=jnp.float32)


def dot_tn(a, b):
    return lax.dot_general(a, b, (((0,), (0,)), ((), ())), preferred_element_type=jnp.float32)


def recip(x):
    return pl.reciprocal(x, approx=True)


def norm_parts(hidden):
    centre = jnp.mean(hidden, axis=-1, keepdims=True)
    shifted = hidden - centre
    spread = jnp.mean(shifted * shifted, axis=-1, keepdims=True)
    scale = lax.rsqrt(spread + NORM_EPS)
    return shifted * scale, scale


def norm_back(grad, gain, unit, scale):
    g = grad * gain
    mean_g = jnp.mean(g, axis=-1, keepdims=True)
    mean_gu = jnp.mean(g * unit, axis=-1, keepdims=True)
    return scale * (g - mean_g - unit * mean_gu)


def bf16(x):
    return x.astype(jnp.bfloat16)


def fragment_body(
    count_ref,
    slot_ref,
    rate_ref,
    near_ref,
    feat_ref,
    cap_ref,
    wqkv_ref,
    wout_ref,
    gains_ref,
    wread_ref,
    wen_ref,
    force_ref,
    energy_ref,
    table,
    forces,
    slots,
    slot_force,
    caps,
    span_ref,
    span_cols_ref,
    order_ref,
    tally,
    bins,
    landed,
    landed_sem,
):
    tiles = near_ref.shape[0]
    frags = cap_ref.shape[0]

    def eighth_of(f):
        return (f % (frags // 2)) * (2 * SLOTS // 8) + f // (frags // 2) * (SLOTS // 8)


    def feature_copy(i):
        return pltpu.make_async_copy(feat_ref.at[i], landed.at[i], landed_sem.at[i])

    for i in range(tiles // 8):
        feature_copy(i).start()

    def widen(i, carry):
        feature_copy(i).wait()
        for k in range(8):
            at = pl.multiple_of(i * 8 * TILE + k * TILE, TILE)
            both = landed[i, k * TILE : (k + 1) * TILE, :].astype(jnp.float32)
            n = jnp.transpose(near_ref[i * 8 + k])
            atoms = jnp.concatenate([n, jnp.zeros((TILE, TILE - 8), jnp.float32)], axis=1)
            for c, part in enumerate((both[:, :QUAD], both[:, QUAD:], atoms)):
                table[pl.ds(at * 4 + c, TILE, stride=4), :] = part
            forces[pl.ds(at, TILE), :] = jnp.zeros((TILE, TILE), jnp.float32)
        return carry

    slot_force[...] = jnp.zeros_like(slot_force)
    head = lax.broadcasted_iota(jnp.int32, (1, HEADS * SLOTS), 1) // SLOTS
    head_col = lax.broadcasted_iota(jnp.int32, (1, F), 1) // (F // HEADS)
    for layer in range(LAYERS):
        wide = jnp.ones((1, HEADS * SLOTS), jnp.float32)
        cols = jnp.ones((1, F), jnp.float32)
        for h in range(HEADS):
            wide = jnp.where(head == h, rate_ref[layer, h], wide)
            cols = jnp.where(head_col == h, rate_ref[layer, h], cols)
        span_ref[layer : layer + 1, :] = 1.0 / wide
        span_cols_ref[layer : layer + 1, :] = 1.0 / cols
    slots[:TILE, :] = jnp.zeros((TILE, TILE), jnp.float32)
    slots[:frags, :SLOTS] = cap_ref[...]
    cols = jnp.transpose(slots[:TILE, :])
    for f in range(frags):
        wide = jnp.broadcast_to(cols[:SLOTS, f : f + 1], (SLOTS, TILE))
        for k in range(SLOTS // 8):
            caps[eighth_of(f) + k] = wide[k * 8 : (k + 1) * 8]
    energy_ref[...] = jnp.zeros_like(energy_ref)

    for size in range(16):
        tally[size] = 0
    for k in range(frags):
        size = (count_ref[k] + 7) >> 3
        tally[size] = tally[size] + 1
    ends = {9: 0}
    for size in range(8, 1, -1):
        ends[size] = ends[size + 1] + tally[size]
        tally[size] = ends[size + 1]
    for k in range(frags):
        live = count_ref[k]
        size = (live + 7) >> 3
        at = tally[size]
        order_ref[at] = live * 512 + eighth_of(k)
        tally[size] = at + 1
    n6, n5, n3, n2 = (ends[k] - ends[k + 1] for k in (6, 5, 3, 2))
    with6 = jnp.minimum(n6, n2)
    with5 = jnp.minimum(n5, n2 - with6 + n3)
    runs = [ends[7], ends[7] + with6, ends[6], ends[6] + with5, ends[5]]
    high = frags - 1
    made = 0
    for k in range(frags):
        fits = (
            ((k >= runs[0]) & (k < runs[1]))
            | ((k >= runs[2]) & (k < runs[3]))
            | (k >= runs[4])
        )
        both = fits & (k < high)
        big = order_ref[k]
        small = order_ref[jnp.maximum(high, 0)]
        bins[0, k] = big & 511
        bins[1, k] = small & 511
        bins[2, k] = big >> 9
        bins[3, k] = jnp.where(both, ((big >> 9) + 7) & -8, SLOTS)
        bins[4, k] = jnp.where(both, small >> 9, 0)
        made = jnp.where(k <= high, k + 1, made)
        high = high - jnp.where(both, 1, 0)
    for k in range(2 * GROUP - 1):
        bins[0, made + k] = 0
        bins[1, made + k] = 0
        bins[2, made + k] = 0
        bins[3, made + k] = SLOTS
        bins[4, made + k] = 0

    lane = lax.broadcasted_iota(jnp.int32, (1, QUAD), 1)
    head_mask = [(lane // 32 == h).astype(jnp.bfloat16) for h in range(4)]
    head_pick = [lane // 32 == h for h in range(4)]
    slot_row = lax.broadcasted_iota(jnp.int32, (SLOTS, QUAD), 0)
    slot_lane = lax.broadcasted_iota(jnp.int32, (SLOTS, QUAD), 1) % SLOTS

    def spread_heads(x):
        return jnp.concatenate([x * head_mask[h] for h in range(4)], axis=0)

    def fold_heads(x):
        out = jnp.where(head_pick[0], x[0:SLOTS], 0.0)
        for h in range(1, 4):
            out = jnp.where(head_pick[h], x[h * SLOTS : (h + 1) * SLOTS], out)
        return out

    half = 0.5 / math.sqrt(32.0)
    units = [(f, quad) for f in range(GROUP) for quad in range(2)]

    def rows_of(f):
        return slice(f * SLOTS, (f + 1) * SLOTS)

    def eighths(which):
        big, small, start = (bins[c, which] for c in (0, 1, 3))
        start = start >> 3
        for k in range(SLOTS // 8):
            yield k, jnp.where(k < start, big, small - start) + k

    def gather(b):
        for f in range(GROUP):
            for k, part in eighths(b * GROUP + f):
                rs = [slot_ref[part * 8 + j] for j in range(8)]
                at = f * SLOTS + k * 8
                for j in range(8):
                    row = pl.multiple_of(rs[j] * 4, 4)
                    slots[4 * (at + j) : 4 * (at + j) + 4, :] = table[pl.ds(row, 4), :]

    def scatter(b):
        for f in range(GROUP):
            for k, part in eighths(b * GROUP + f):
                rs = [slot_ref[part * 8 + j] for j in range(8)]
                old = [forces[pl.ds(r, 1), :] for r in rs]
                for j in range(8):
                    at = f * SLOTS + k * 8 + j
                    forces[pl.ds(rs[j], 1), :] = old[j] + slot_force[at : at + 1, :]
        return forces[pl.ds(rs[7], 1), :]

    def one_block(b, carry):
        info = [tuple(bins[c, b * GROUP + f] for c in (2, 3, 4)) for f in range(GROUP)]
        h0 = jnp.concatenate([slots[pl.ds(c, ROWS, stride=4), :] for c in range(2)], axis=1)
        atoms = slots[pl.ds(2, ROWS, stride=4), :]
        gather(b + 1)
        last = scatter(jnp.maximum(b - 1, 0))

        atom_rows = jnp.transpose(atoms)
        dists, inverses, offsets, weights = [], [], [], []
        for f in range(GROUP):
            first, start, second = info[f]
            col = atoms[rows_of(f), :]
            row = atom_rows[0:8, rows_of(f)]
            row = jnp.concatenate([row, row], axis=1)
            off = [col[:, c : c + 1] - row[c : c + 1, :] for c in range(3)]
            square = off[0] * off[0] + off[1] * off[1] + off[2] * off[2] + PAIR_SOFTEN
            inverse = lax.rsqrt(square)

            def owner(i, dead):
                late = jnp.logical_and(i >= start, i < start + second)
                return jnp.where(i < first, 1, jnp.where(late, 2, dead))

            mine = owner(slot_row, 0)
            dists.append(jnp.where(mine == owner(slot_lane, -1), square * inverse, FAR))
            inverses.append(inverse)
            offsets.append(off)
            cap = jnp.concatenate([caps[part] for _, part in eighths(b * GROUP + f)], axis=0)
            weights.append(jnp.where(mine > 0, cap, 0.0))
        dist2 = [jnp.concatenate([d, d], axis=1) for d in dists]
        weight = jnp.concatenate(weights, axis=0)

        def attention(layer, project):
            def part(f, quad, which):
                at = which * F + quad * QUAD
                return project[rows_of(f), at : at + QUAD]

            qs = [part(f, quad, 0) for f, quad in units]
            kbs = [spread_heads(part(f, quad, 1)) for f, quad in units]
            vbs = [spread_heads(part(f, quad, 2)) for f, quad in units]
            scores = [dot_nt(q, kb) for q, kb in zip(qs, kbs)]
            atts, by_dist, by_score = [], [], []
            for (f, quad), score in zip(units, scores):
                u = score * half
                th = jnp.tanh(u)
                silu = u + u * th
                span = span_ref[layer : layer + 1, quad * 256 : (quad + 1) * 256]
                damp = recip(dist2[f] + span)
                att = silu * damp
                atts.append(bf16(att))
                by_dist.append(att * damp)
                if layer == 1:
                    by_score.append(damp * ((1.0 + th) + (silu - silu * th)))
            span_cols = span_cols_ref[layer : layer + 1, :]
            message = [dot(att, vb) for att, vb in zip(atts, vbs)]
            message = jnp.concatenate(
                [jnp.concatenate(message[2 * f : 2 * f + 2], axis=1) for f in range(GROUP)], axis=0
            )
            return bf16(message * span_cols), (qs, kbs, vbs, atts, by_dist, by_score)

        gain = [gains_ref[i : i + 1, :] for i in range(LAYERS + 1)]
        unit0, _ = norm_parts(h0)
        project0 = bf16(dot(bf16(unit0 * gain[0]), wqkv_ref[0]))
        message0, kept0 = attention(0, project0)
        h1 = h0 + dot(message0, wout_ref[0])
        unit1, scale1 = norm_parts(h1)
        project1 = bf16(dot(bf16(unit1 * gain[1]), wqkv_ref[1]))
        message1, kept1 = attention(1, project1)
        h2 = h1 + dot(message1, wout_ref[1])
        unit2, scale2 = norm_parts(h2)
        u = 0.5 * dot(bf16(unit2 * gain[2]), wread_ref[...])
        th = jnp.tanh(u)
        silu = u + u * th
        weighted = weight * (wen_ref[...] + 0.0 * last)
        energy_ref[...] += jnp.sum((weighted * silu).reshape(ROWS // 8, 8, QUAD), axis=0)

        dread = bf16((0.5 * weighted) * ((1.0 + th) + (silu - silu * th)))
        dh2 = norm_back(dot_nt(dread, wread_ref[...]), gain[2], unit2, scale2)
        dmsg1 = bf16(dot_nt(bf16(dh2), wout_ref[1]) * span_cols_ref[1:2, :])
        qs, kbs, vbs, atts, by_dist, by_score = kept1
        dms = [dmsg1[rows_of(f), quad * QUAD : (quad + 1) * QUAD] for f, quad in units]
        datts = [dot_nt(dm, vb) for dm, vb in zip(dms, vbs)]
        dvs = [bf16(fold_heads(dot_tn(att, dm))) for att, dm in zip(atts, dms)]
        dss = [bf16(datt * slope) for datt, slope in zip(datts, by_score)]
        dqs = [bf16(dot(ds, kb) * half) for ds, kb in zip(dss, kbs)]
        dks = [bf16(fold_heads(dot_tn(ds, q)) * half) for ds, q in zip(dss, qs)]
        pulls = [datt * slope for datt, slope in zip(datts, by_dist)]
        dproject = jnp.concatenate(
            [
                jnp.concatenate(
                    [x[2 * f + quad] for x in (dqs, dks, dvs) for quad in range(2)], axis=1
                )
                for f in range(GROUP)
            ],
            axis=0,
        )
        dh1 = dh2 + norm_back(dot_nt(dproject, wqkv_ref[1]), gain[1], unit1, scale1)
        dmsg0 = bf16(dot_nt(bf16(dh1), wout_ref[0]) * span_cols_ref[0:1, :])
        datts = [
            dot_nt(dmsg0[rows_of(f), quad * QUAD : (quad + 1) * QUAD], vb)
            for (f, quad), vb in zip(units, kept0[2])
        ]
        pulls = [old + datt * slope for old, datt, slope in zip(pulls, datts, kept0[4])]
        force_rows = []
        for f in range(GROUP):
            pull = pulls[2 * f] + pulls[2 * f + 1]
            pull = (pull[:, :QUAD] + pull[:, QUAD:]) * inverses[f]
            pull = pull[:, :SLOTS] + pull[:, SLOTS:]
            pull = pull + jnp.transpose(pull)
            for c in range(3):
                force_rows.append(
                    -jnp.sum(pull * offsets[f][c][:, :SLOTS], axis=0, keepdims=True)
                )
        packed = jnp.concatenate(
            [
                jnp.concatenate([force_rows[3 * f + c] for f in range(GROUP)], axis=1)
                for c in range(3)
            ]
            + [jnp.zeros((5, ROWS), jnp.float32)],
            axis=0,
        )
        slot_force[:, 0:8] = jnp.transpose(packed)
        return carry

    lax.fori_loop(0, tiles // 8, widen, 0)
    gather(0)
    groups = (made + GROUP - 1) // GROUP
    lax.fori_loop(0, groups, one_block, 0)
    scatter(groups - 1)

    pick = (
        lax.broadcasted_iota(jnp.int32, (16, TILE), 0)
        == lax.broadcasted_iota(jnp.int32, (16, TILE), 1)
    ).astype(jnp.bfloat16)
    for i in range(tiles // 8):
        rows = dot_nt(pick, bf16(forces[i * 1024 : (i + 1) * 1024, :]))
        for c in range(3):
            for k in range(8):
                force_ref[i, c, k : k + 1, :] = rows[c : c + 1, k * TILE : (k + 1) * TILE]


def fragment_model(near8, near_features, slot_rows, atom_count, cap_weight, weights):
    w_qkv, w_out, gains, rates, w_read, w_energy = weights
    tiles = near8.shape[0]
    frags = atom_count.shape[0]
    smem = pl.BlockSpec(memory_space=pltpu.SMEM)
    vmem = pl.BlockSpec(memory_space=pltpu.VMEM)
    force, energy = pl.pallas_call(
        fragment_body,
        out_shape=(
            jax.ShapeDtypeStruct((tiles // 8, 3, 8, TILE), jnp.float32),
            jax.ShapeDtypeStruct((8, TILE), jnp.float32),
        ),
        in_specs=[smem, smem, smem, vmem, pl.BlockSpec(memory_space=pl.ANY)] + [vmem] * 6,
        out_specs=(vmem, vmem),
        scratch_shapes=[
            pltpu.VMEM((4 * tiles * TILE, TILE), jnp.float32),
            pltpu.VMEM((tiles * TILE, TILE), jnp.float32),
            pltpu.VMEM((4 * ROWS, TILE), jnp.float32),
            pltpu.VMEM((ROWS, TILE), jnp.float32),
            pltpu.VMEM((SLOTS // 8 * frags, 8, TILE), jnp.float32),
            pltpu.VMEM((LAYERS, HEADS * SLOTS), jnp.float32),
            pltpu.VMEM((LAYERS, F), jnp.float32),
            pltpu.SMEM((frags,), jnp.int32),
            pltpu.SMEM((16,), jnp.int32),
            pltpu.SMEM((5, frags + 2 * GROUP), jnp.int32),
            pltpu.VMEM(near_features.shape, near_features.dtype),
            pltpu.SemaphoreType.DMA((tiles // 8,)),
        ],
        compiler_params=pltpu.CompilerParams(vmem_limit_bytes=56 * MIB),
        name="fragments",
    )(
        atom_count,
        slot_rows.reshape(-1),
        rates,
        near8,
        near_features,
        cap_weight,
        w_qkv,
        w_out,
        gains,
        w_read,
        w_energy.reshape(1, -1),
    )
    return force, energy


def home_body(
    force_ref,
    pair_ref,
    frag_energy_ref,
    pair_energy_ref,
    out_ref,
    energy_ref,
    landing,
    by_sub,
    by_brick,
    force_send,
    force_recv,
    sub_send,
    sub_recv,
    brick_send,
    brick_recv,
):
    bricks, subs = by_brick.shape[0], by_sub.shape[0]
    brick, sub = lax.axis_index("brick"), lax.axis_index("sub")
    mesh_id = pl.DeviceIdType.MESH
    around = [(u, v) for u in (-1, 0, 1) for v in (-1, 0, 1) if (u, v) != (0, 0)]

    def inside(u, v):
        b, s = brick + u, sub + v
        return (b >= 0) & (b < bricks) & (s >= 0) & (s < subs)

    sub_peers = [(brick, lax.rem(sub + d, subs)) for d in range(1, subs)]
    brick_peers = [(lax.rem(brick + d, bricks), sub) for d in range(1, bricks)]

    barrier = pltpu.get_barrier_semaphore()
    for peer in sub_peers + brick_peers:
        pl.semaphore_signal(barrier, inc=1, device_id=peer, device_id_type=mesh_id)
    corners = [(u, v) for u, v in around if u != 0 and v != 0]
    for u, v in corners:

        @pl.when(inside(u, v))
        def _(u=u, v=v):
            pl.semaphore_signal(
                barrier, inc=1, device_id=(brick + u, sub + v), device_id_type=mesh_id
            )

    beside = [
        jnp.where(at > 0, 1, 0) + jnp.where(at < size - 1, 1, 0)
        for at, size in ((brick, bricks), (sub, subs))
    ]
    pl.semaphore_wait(barrier, subs + bricks - 2 + beside[0] * beside[1])

    def energy_copy(store, send, recv, k, slot, peer):
        return pltpu.make_async_remote_copy(
            src_ref=store.at[slot],
            dst_ref=store.at[slot],
            send_sem=send.at[k],
            recv_sem=recv.at[slot],
            device_id=peer,
            device_id_type=mesh_id,
        )

    by_sub[sub] = frag_energy_ref[...] + pair_energy_ref[...]
    for k, peer in enumerate(sub_peers):
        energy_copy(by_sub, sub_send, sub_recv, k, sub, peer).start()

    def force_copy(u, v):
        k = (u + 1) * 3 + v + 1
        return pltpu.make_async_remote_copy(
            src_ref=force_ref.at[k],
            dst_ref=landing.at[k],
            send_sem=force_send.at[k],
            recv_sem=force_recv.at[k],
            device_id=(brick + u, sub + v),
            device_id_type=mesh_id,
        )

    for u, v in around:

        @pl.when(inside(u, v))
        def _(u=u, v=v):
            force_copy(u, v).start()

    for k, peer in enumerate(sub_peers):
        energy_copy(by_sub, sub_send, sub_recv, k, peer[1], peer).wait_recv()
    by_brick[brick] = jnp.sum(by_sub[...], axis=0)
    for k, peer in enumerate(brick_peers):
        energy_copy(by_brick, brick_send, brick_recv, k, brick, peer).start()

    out_ref[...] = force_ref[4] + pair_ref[...]
    for u, v in around:
        @pl.when(inside(-u, -v))
        def _(u=u, v=v):
            force_copy(u, v).wait_recv()
            out_ref[...] += landing[(u + 1) * 3 + v + 1]

    for k, peer in enumerate(brick_peers):
        energy_copy(by_brick, brick_send, brick_recv, k, peer[0], peer).wait_recv()
    energy_ref[0, 0] = jnp.sum(jnp.sum(by_brick[...], axis=0))

    for u, v in around:

        @pl.when(inside(u, v))
        def _(u=u, v=v):
            force_copy(u, v).wait_send()

    for k, peer in enumerate(sub_peers):
        energy_copy(by_sub, sub_send, sub_recv, k, sub, peer).wait_send()
    for k, peer in enumerate(brick_peers):
        energy_copy(by_brick, brick_send, brick_recv, k, brick, peer).wait_send()


def bring_home(row_force, pair_force, frag_energy, pair_energy):
    bricks, subs = lax.axis_size("brick"), lax.axis_size("sub")
    vmem = pl.BlockSpec(memory_space=pltpu.VMEM)
    block = row_force.shape[1:]
    dma = pltpu.SemaphoreType.DMA
    return pl.pallas_call(
        home_body,
        out_shape=(
            jax.ShapeDtypeStruct(block, jnp.float32),
            jax.ShapeDtypeStruct((1, 1), jnp.float32),
        ),
        in_specs=[vmem] * 4,
        out_specs=(vmem, pl.BlockSpec(memory_space=pltpu.SMEM)),
        scratch_shapes=[
            pltpu.VMEM((9,) + block, jnp.float32),
            pltpu.VMEM((subs, 8, TILE), jnp.float32),
            pltpu.VMEM((bricks, 8, TILE), jnp.float32),
            dma((9,)),
            dma((9,)),
            dma((subs,)),
            dma((subs,)),
            dma((bricks,)),
            dma((bricks,)),
        ],
        compiler_params=pltpu.CompilerParams(
            collective_id=1, has_side_effects=True, vmem_limit_bytes=56 * MIB
        ),
        name="bring_home",
    )(row_force, pair_force, frag_energy, pair_energy)


AROUND = [(u, v) for u in (-1, 0, 1) for v in (-1, 0, 1) if (u, v) != (0, 0)]
CHUNKS = 2


STEP_PAIRS = 16


def three_parts(x):
    a = bf16(x).astype(jnp.float32)
    b = bf16(x - a).astype(jnp.float32)
    return [a, b, x - a - b, jnp.zeros_like(x)]


def block_of(u, v):
    return (u + 1) * 3 + v + 1


def halo_body(
    pairs_ref,
    count_ref,
    pos_ref,
    charge_ref,
    own_list_ref,
    slot_ref,
    feat_ref,
    near_ref,
    near_feat_ref,
    pair_force_ref,
    pair_energy_ref,
    rows_ref,
    parts,
    cols_a,
    cols_b,
    atom_send,
    atom_recv,
    side_send,
    side_recv,
    ahead_send,
    ahead_recv,
    corner_send,
    corner_recv,
    local_sem,
):
    bricks, subs = lax.axis_size("brick"), lax.axis_size("sub")
    brick, sub = lax.axis_index("brick"), lax.axis_index("sub")
    mesh_id = pl.DeviceIdType.MESH
    rows = feat_ref.shape[0]
    tiles = charge_ref.shape[0]
    part = rows // CHUNKS
    centre = block_of(0, 0) * tiles

    rows_ref[:, :SLOTS] = slot_ref[: rows_ref.shape[0]]
    rows_ref[:, SLOTS:] = slot_ref[rows_ref.shape[0] :]
    near_ref[pl.ds(centre, tiles)] = jnp.zeros((tiles, 8, TILE), jnp.float32)
    for t in range(tiles):
        for c in range(3):
            near_ref[centre + t, c : c + 1, :] = pos_ref[c, t : t + 1, :]
        near_ref[centre + t, 3:4, :] = charge_ref[t : t + 1, :]

    def inside(u, v):
        b, s = brick + u, sub + v
        return (b >= 0) & (b < bricks) & (s >= 0) & (s < subs)

    barrier = pltpu.get_barrier_semaphore()
    for u, v in AROUND:

        @pl.when(inside(u, v))
        def _(u=u, v=v):
            pl.semaphore_signal(
                barrier, inc=1, device_id=(brick + u, sub + v), device_id_type=mesh_id
            )

    beside = [
        jnp.where(at > 0, 1, 0) + jnp.where(at < size - 1, 1, 0)
        for at, size in ((brick, bricks), (sub, subs))
    ]
    pl.semaphore_wait(barrier, beside[0] + beside[1] + beside[0] * beside[1])

    def atom_copy(u, v):
        k = block_of(-u, -v)
        return pltpu.make_async_remote_copy(
            src_ref=near_ref.at[pl.ds(centre, tiles)],
            dst_ref=near_ref.at[pl.ds(k * tiles, tiles)],
            send_sem=atom_send.at[k],
            recv_sem=atom_recv.at[k],
            device_id=(brick + u, sub + v),
            device_id_type=mesh_id,
        )

    def ahead_copy(u, c):
        i = (u + 1) // 2
        return pltpu.make_async_remote_copy(
            src_ref=feat_ref.at[pl.ds(c * part, part)],
            dst_ref=near_feat_ref.at[block_of(-u, 0), pl.ds(c * part, part)],
            send_sem=ahead_send.at[i, c],
            recv_sem=ahead_recv.at[i, c],
            device_id=(brick + u, sub),
            device_id_type=mesh_id,
        )

    def side_copy(v):
        i = (v + 1) // 2
        return pltpu.make_async_remote_copy(
            src_ref=feat_ref,
            dst_ref=near_feat_ref.at[block_of(0, -v)],
            send_sem=side_send.at[i],
            recv_sem=side_recv.at[i],
            device_id=(brick, sub + v),
            device_id_type=mesh_id,
        )

    def corner_copy(w, v, c):
        i = (w + 1) + (v + 1) // 2
        at = pl.ds(c * part, part)
        return pltpu.make_async_remote_copy(
            src_ref=near_feat_ref.at[block_of(w, 0), at],
            dst_ref=near_feat_ref.at[block_of(w, -v), at],
            send_sem=corner_send.at[i, c],
            recv_sem=corner_recv.at[i, c],
            device_id=(brick, sub + v),
            device_id_type=mesh_id,
        )

    for u, v in AROUND:

        @pl.when(inside(u, v))
        def _(u=u, v=v):
            atom_copy(u, v).start()

    for c in range(CHUNKS):
        for u in (-1, 1):

            @pl.when(inside(u, 0))
            def _(u=u, c=c):
                ahead_copy(u, c).start()

        if c == 0:
            for v in (-1, 1):

                @pl.when(inside(0, v))
                def _(v=v):
                    side_copy(v).start()

    local = pltpu.make_async_copy(feat_ref, near_feat_ref.at[block_of(0, 0)], local_sem)
    local.start()
    for u, v in AROUND:
        k = block_of(u, v)

        @pl.when(jnp.logical_not(inside(u, v)))
        def _(k=k):
            near_ref[pl.ds(k * tiles, tiles)] = jnp.zeros((tiles, 8, TILE), jnp.float32)

    def forward(c):
        for w in (-1, 1):

            @pl.when(inside(w, 0))
            def _(w=w):
                ahead_copy(-w, c).wait_recv()
                for v in (-1, 1):

                    @pl.when(inside(0, v))
                    def _(w=w, v=v):
                        corner_copy(w, v, c).start()

    for u, v in AROUND:

        @pl.when(inside(-u, -v))
        def _(u=u, v=v):
            atom_copy(u, v).wait_recv()

    spread = (
        lax.broadcasted_iota(jnp.int32, (32, 4 * TILE), 0) % 8
        == lax.broadcasted_iota(jnp.int32, (32, 4 * TILE), 1) // TILE
    ).astype(jnp.bfloat16)
    chunk = 32

    def spread_near(cols, first):
        for k in range(8):
            near = pairs_ref[1, jnp.minimum(first + k, pairs - 1)]
            cols[k] = dot_tn(bf16(jnp.concatenate(three_parts(near_ref[near]), axis=0)), spread)

    def one_pair(p, cols, k):
        own = pairs_ref[0, p]
        near = pairs_ref[1, p]
        o = near_ref[centre + own]
        xi, yi, zi, qi = (o[c : c + 1, :] for c in range(4))
        sums = [jnp.zeros((8, TILE), jnp.float32) for _ in range(4)]
        for start in range(0, TILE, chunk):
            xj, yj, zj, qj = (
                cols[k, start : start + chunk, c * TILE : (c + 1) * TILE] for c in range(4)
            )
            dx, dy, dz = xi - xj, yi - yj, zi - zj
            square = dx * dx + dy * dy + dz * dz + CHARGE_SOFTEN
            rinv = lax.rsqrt(square)
            t = rinv * recip(rinv + ERFC_P * SCREEN_RATE)
            g = ERFC_C[-1]
            for coef in ERFC_C[-2::-1]:
                g = g * t + coef
            gauss = qj * jnp.exp2((-SCREEN_RATE * SCREEN_RATE * math.log2(math.e)) * square)
            screened = (g * t) * rinv
            w = (gauss * (screened + GAUSS)) * (rinv * rinv)
            for c, term in enumerate((w * dx, w * dy, w * dz, gauss * screened)):
                sums[c] += jnp.sum(term.reshape(chunk // 8, 8, TILE), axis=0)
        itself = jnp.where(near == own + centre, math.erfc(SCREEN_RATE), 0.0)
        for c in range(4):
            row = jnp.sum(sums[c], axis=0, keepdims=True)
            parts[c, pl.ds(p, 1), :] = qi * (row - itself * qi if c == 3 else row)

    def sixteen_pairs(i, carry):
        p = 16 * i
        for k in range(8):
            one_pair(p + k, cols_a, k)
        spread_near(cols_a, p + 16)
        for k in range(8):
            one_pair(p + 8 + k, cols_b, k)
        spread_near(cols_b, p + 24)
        return carry

    pairs = own_list_ref.shape[1]
    spread_near(cols_a, 0)
    spread_near(cols_b, 8)
    done = 0
    for c in range(CHUNKS + 1):
        upto = (c + 1) * STEP_PAIRS if c < CHUNKS else pairs
        lax.fori_loop(done // 16, upto // 16, sixteen_pairs, 0)
        done = upto
        if c < CHUNKS:
            forward(c)

    pick = (
        (own_list_ref[0:1, :] == lax.broadcasted_iota(jnp.int32, (16, pairs), 0))
        & (lax.broadcasted_iota(jnp.int32, (16, pairs), 1) < count_ref[0, 0])
    ).astype(jnp.bfloat16)
    for k in range(4):
        whole = sum(dot(pick, bf16(x)) for x in three_parts(parts[k])[:3])[:tiles]
        if k < 3:
            pair_force_ref[k] = COULOMB_UNIT * whole
        else:
            pair_energy_ref[...] = (0.5 * COULOMB_UNIT) * whole

    for v in (-1, 1):

        @pl.when(inside(0, -v))
        def _(v=v):
            side_copy(v).wait_recv()

    for w in (-1, 1):
        for v in (-1, 1):

            @pl.when(inside(w, -v))
            def _(w=w, v=v):
                for c in range(CHUNKS):
                    corner_copy(w, v, c).wait_recv()

    local.wait()
    for u, v in AROUND:

        @pl.when(inside(u, v))
        def _(u=u, v=v):
            atom_copy(u, v).wait_send()

    for u in (-1, 1):

        @pl.when(inside(u, 0))
        def _(u=u):
            for c in range(CHUNKS):
                ahead_copy(u, c).wait_send()

    for v in (-1, 1):

        @pl.when(inside(0, v))
        def _(v=v):
            side_copy(v).wait_send()

    for w in (-1, 1):
        for v in (-1, 1):

            @pl.when(inside(w, v))
            def _(w=w, v=v):
                for c in range(CHUNKS):
                    corner_copy(w, v, c).wait_send()


def halo(positions, charges, features, pairs, count, slot_index):
    tiles = charges.shape[0]
    smem = pl.BlockSpec(memory_space=pltpu.SMEM)
    vmem = pl.BlockSpec(memory_space=pltpu.VMEM)
    hbm = pl.BlockSpec(memory_space=pl.ANY)
    dma = pltpu.SemaphoreType.DMA
    return pl.pallas_call(
        halo_body,
        out_shape=(
            jax.ShapeDtypeStruct((9 * tiles, 8, TILE), jnp.float32),
            jax.ShapeDtypeStruct((9,) + features.shape, features.dtype),
            jax.ShapeDtypeStruct((3, tiles, TILE), jnp.float32),
            jax.ShapeDtypeStruct((tiles, TILE), jnp.float32),
            jax.ShapeDtypeStruct((slot_index.shape[0] // 2, 2 * SLOTS), jnp.int32),
        ),
        in_specs=[smem, smem, vmem, vmem, vmem, vmem, hbm],
        out_specs=(vmem, hbm, vmem, vmem, vmem),
        scratch_shapes=[
            pltpu.VMEM((4, pairs.shape[1], TILE), jnp.float32),
            pltpu.VMEM((8, TILE, 4 * TILE), jnp.float32),
            pltpu.VMEM((8, TILE, 4 * TILE), jnp.float32),
            dma((9,)),
            dma((9,)),
            dma((2,)),
            dma((2,)),
            dma((2, CHUNKS)),
            dma((2, CHUNKS)),
            dma((4, CHUNKS)),
            dma((4, CHUNKS)),
            dma(()),
        ],
        compiler_params=pltpu.CompilerParams(
            collective_id=2, has_side_effects=True, vmem_limit_bytes=56 * MIB
        ),
        name="halo",
    )(pairs, count, positions, charges, pairs, slot_index, features)


def body(
    atom_features,
    positions,
    charges,
    slot_index,
    atom_count,
    cap_weight,
    tile_pairs,
    tile_count,
    w_qkv,
    w_out,
    gains,
    rates,
    w_read,
    w_energy,
):
    own_size = atom_features.shape[2]
    own_tiles = own_size // TILE
    near8, near_features, pair_force, pair_energy, slot_rows = halo(
        positions.reshape(3, own_tiles, TILE),
        charges.reshape(own_tiles, TILE),
        atom_features.reshape(own_size, -1),
        tile_pairs.reshape(2, -1),
        tile_count,
        slot_index,
    )
    row_force, frag_energy = fragment_model(
        near8,
        near_features,
        slot_rows,
        atom_count,
        cap_weight,
        (w_qkv, w_out, gains, rates, w_read, w_energy),
    )
    forces, energy = bring_home(row_force, pair_force, frag_energy, pair_energy)
    return forces.reshape(3, 1, 1, own_size), energy.reshape(())


def solution(mesh):
    in_specs = (
        P("brick", "sub", None, None),
        P(None, "brick", "sub", None),
        P("brick", "sub", None),
        P(("brick", "sub"), None),
        P(("brick", "sub")),
        P(("brick", "sub"), None),
        P(None, "brick", "sub", None),
        P("brick", "sub"),
        P(),
        P(),
        P(),
        P(),
        P(),
        P(),
    )
    out_specs = (P(None, "brick", "sub", None), P())
    return jax.shard_map(body, mesh=mesh, in_specs=in_specs, out_specs=out_specs, check_vma=False)
```
